256 devices in a mesh: chain: 16 (over y, x), heads: 16 (over z, core).
Axes of the slice: x: 4, y: 4, z: 8, core: 2. Of those that a mesh axis runs over, the one named last changes fastest.
Arguments:
- query_input: bfloat16 [8192, 4096], P('chain', 'heads'), may hold values from -8 to 8
- key_input: bfloat16 [8192, 4096], P('chain', 'heads'), may hold values from -8 to 8
- value_input: bfloat16 [8192, 4096], P('chain', 'heads'), may hold values from -6 to 6
- grad_output: bfloat16 [8192, 4096], P('chain', 'heads'), may hold values from -6 to 6
- selection: int32 [16, 32, 3], P(None, 'heads'), may hold values from 0 to 14, as said below
Outputs:
- grad_queries: bfloat16 [8192, 4096], P(('chain', 'heads'))
- grad_keys: bfloat16 [8192, 4096], P(('chain', 'heads'))
- grad_values: bfloat16 [8192, 4096], P(('chain', 'heads'))
The draws below stay inside these ranges and needn't reach their ends.
Inputs may be any that keep to these rules, and one draw needn't show every extreme that they name: `selection`: for query block b and every head: slot 0 names block b - 1 (b itself when b is 0), the other slots name distinct blocks below b - 1; where no such block is left a slot names b itself and is empty.
All inputs are finite; a program needn't handle non-finite values.
Results may differ from the reference program's by a relative error of at most 0.035.
Values may be sent and summed in bfloat16 or wider, within the bound.
No kernel may reach another device: no remote copies, remote signals or barrier semaphores. Data moves between devices by JAX's collectives and lax.ppermute only.
A program may use at most 128 MiB of HBM per device.

```python
import jax
import jax.numpy as jnp
from jax import lax

BLOCK = 512
HEAD_DIM = 128
TOPK = 3
HEADS = 32
BLOCKS = 16
TOKENS = 8192


def draw_query_input(key, part):
    own_key = jax.random.fold_in(key, 1)
    base = jnp.clip(jax.random.normal(own_key, (TOKENS, HEADS * HEAD_DIM), jnp.float32), -8.0, 8.0)
    return base.astype(jnp.bfloat16)


def draw_key_input(key, part):
    own_key = jax.random.fold_in(key, 2)
    base = jnp.clip(jax.random.normal(own_key, (TOKENS, HEADS * HEAD_DIM), jnp.float32), -8.0, 8.0)
    return base.astype(jnp.bfloat16)


def draw_selection(key, part):
    key = jax.random.fold_in(key, 5)
    raw = jax.random.randint(key, (BLOCKS, HEADS, BLOCKS), 0, BLOCKS)
    candidate = jnp.arange(BLOCKS, dtype=jnp.int32)[None, None, :]
    block_id = jnp.arange(BLOCKS, dtype=jnp.int32)[:, None, None]
    ceiling = 4 * BLOCKS * BLOCKS
    ranked = (raw + candidate) * BLOCKS + candidate
    ranked = jnp.where(candidate < block_id - 1, ranked, ceiling + candidate)
    lowest, picked = lax.top_k(-ranked, TOPK - 1)
    usable = -lowest < ceiling
    picked = jnp.where(usable, picked.astype(jnp.int32), block_id)
    first = jnp.broadcast_to(jnp.maximum(block_id - 1, 0), (BLOCKS, HEADS, 1))
    return jnp.concatenate([first, picked], axis=2).astype(jnp.int32)


def steps_of(key, shape, split, least, largest):
    gain = 1.0
    for dim, blocks in split:
        steps = jax.random.uniform(jax.random.fold_in(jax.random.fold_in(key, 6), dim), (blocks,), jnp.float32, least / len(split), largest / len(split))
        gain = gain * jnp.repeat(jnp.exp(steps), shape[dim] // blocks).reshape((-1,) + (1,) * (len(shape) - 1 - dim))
    return gain


def gaussian(stream_key, dims, scale, most, pieces=(), held_as=jnp.bfloat16):
    result = jax.random.normal(stream_key, dims, jnp.float32) * scale
    if len(pieces) > 0:
        result = steps_of(stream_key, dims, pieces, -0.22, 0.18) * result
    return jnp.clip(result, min=-most, max=most).astype(held_as)


def setup_inputs(seed: int = 0) -> dict:
    streams_of = jax.random.split(jax.random.key(seed), 6)
    return {
        "query_input": draw_query_input(jax.random.fold_in(streams_of[5], 71), 0),
        "key_input": draw_key_input(jax.random.fold_in(streams_of[5], 71), 0),
        "value_input": gaussian(streams_of[2], (TOKENS, HEADS * HEAD_DIM), 1.0, 6.0, ((0, 16), (1, 16))),
        "grad_output": gaussian(streams_of[3], (TOKENS, HEADS * HEAD_DIM), 1.0, 6.0, ((0, 16), (1, 16))),
        "selection": draw_selection(jax.random.fold_in(streams_of[5], 71), 0),
    }


MASKED = -1.0e30


def block_backward(query_block, key_slots, value_slots, grad_block, allowed, scaling):
    query_float = query_block.astype(jnp.float32)
    key_float = key_slots.astype(jnp.float32)
    value_float = value_slots.astype(jnp.float32)
    grad_float = grad_block.astype(jnp.float32)
    scores = scaling * jnp.einsum("hqd,hjkd->hqjk", query_float, key_float)
    scores = jnp.where(allowed, scores, MASKED)
    row_max = jnp.max(scores, axis=(2, 3), keepdims=True)
    raised = jnp.exp(scores - row_max)
    row_total = jnp.sum(raised, axis=(2, 3), keepdims=True)
    probability = raised / row_total
    probability_low = probability.astype(jnp.bfloat16)
    output = jnp.einsum("hqjk,hjkd->hqd", probability_low.astype(jnp.float32), value_float)
    delta_row = jnp.sum(grad_float * output, axis=2)
    grad_probs = jnp.einsum("hqd,hjkd->hqjk", grad_float, value_float)
    grad_scores = (probability * (grad_probs - delta_row[:, :, None, None])).astype(jnp.bfloat16)
    grad_scores_float = grad_scores.astype(jnp.float32)
    grad_query = (scaling * jnp.einsum("hqjk,hjkd->hqd", grad_scores_float, key_float)).astype(jnp.bfloat16)
    grad_key = scaling * jnp.einsum("hqjk,hqd->hjkd", grad_scores_float, query_float)
    grad_value = jnp.einsum("hqjk,hqd->hjkd", probability_low.astype(jnp.float32), grad_float)
    return grad_query, grad_key, grad_value


def reference(query_input, key_input, value_input, grad_output, selection):
    scaling = HEAD_DIM ** -0.5
    shape_four = (BLOCKS, BLOCK, HEADS, HEAD_DIM)
    query_four = query_input.reshape(shape_four)
    key_four = key_input.reshape(shape_four)
    value_four = value_input.reshape(shape_four)
    grad_four = grad_output.reshape(shape_four)
    head_range = jnp.arange(HEADS, dtype=jnp.int32)[:, None]
    position = jnp.arange(BLOCK)
    causal = position[:, None] >= position[None, :]

    def accumulate(block_index, running):
        query_grads, key_sums, value_sums = running
        block_id = jnp.asarray(block_index).astype(jnp.int32)
        chosen = lax.dynamic_index_in_dim(selection, block_id, 0, keepdims=False).astype(jnp.int32)
        own_slot = jnp.full((HEADS, 1), block_id, jnp.int32)
        slot_index = jnp.concatenate([chosen, own_slot], axis=1)
        key_slots = key_four[slot_index, :, head_range, :]
        value_slots = value_four[slot_index, :, head_range, :]
        query_block = lax.dynamic_index_in_dim(query_four, block_id, 0, keepdims=False).transpose(1, 0, 2)
        grad_block = lax.dynamic_index_in_dim(grad_four, block_id, 0, keepdims=False).transpose(1, 0, 2)
        earlier = chosen < block_id
        allowed = jnp.concatenate([
            jnp.broadcast_to(earlier[:, None, :, None], (HEADS, BLOCK, TOPK, BLOCK)),
            jnp.broadcast_to(causal[None, :, None, :], (HEADS, BLOCK, 1, BLOCK))], axis=2)
        grad_query, grad_key, grad_value = block_backward(query_block, key_slots, value_slots, grad_block, allowed, scaling)
        query_grads = lax.dynamic_update_index_in_dim(query_grads, grad_query.transpose(1, 0, 2), block_id, 0)
        key_sums = key_sums.at[slot_index, :, head_range, :].add(grad_key)
        value_sums = value_sums.at[slot_index, :, head_range, :].add(grad_value)
        return query_grads, key_sums, value_sums

    start_state = (jnp.zeros(shape_four, jnp.bfloat16), jnp.zeros(shape_four, jnp.float32), jnp.zeros(shape_four, jnp.float32))
    query_grads, key_sums, value_sums = lax.fori_loop(0, BLOCKS, accumulate, start_state)
    flat = (TOKENS, HEADS * HEAD_DIM)
    return (query_grads.reshape(flat), key_sums.astype(jnp.bfloat16).reshape(flat), value_sums.astype(jnp.bfloat16).reshape(flat))
```

```python
import math

import jax
import jax.numpy as jnp
from jax import lax
from jax.experimental import pallas as pl
from jax.experimental.pallas import tpu as pltpu
from jax.sharding import PartitionSpec as P

HEAD_DIM = 128
TOPK = 3
MASKED = -1e30
SCALING = HEAD_DIM ** (-0.5)
TILE = 256
MIB = 1 << 20


def columns(head):
    return slice(head * HEAD_DIM, (head + 1) * HEAD_DIM)


def pick_kernel(selection_ref, held_ref, out_ref):
    blocks, _, _, width = held_ref.shape
    heads = width // HEAD_DIM

    def fill(block, carry):
        for head in range(heads):
            for slot in range(TOPK):
                source = selection_ref[(block * heads + head) * TOPK + slot]
                out_ref[block, :, slot, :, columns(head)] = held_ref[source, :, :, columns(head)]
        return carry

    lax.fori_loop(0, blocks, fill, 0)


def reduce_kernel(selection_ref, terms_ref, out_ref, total_ref):
    blocks, _, _, width = out_ref.shape
    heads = width // HEAD_DIM
    total_ref[...] = jnp.zeros_like(total_ref)

    def add(block, carry):
        for head in range(heads):
            for slot in range(TOPK):
                target = selection_ref[(block * heads + head) * TOPK + slot]
                total_ref[target, :, :, columns(head)] += terms_ref[
                    block, :, slot, :, columns(head)
                ].astype(jnp.float32)
        return carry

    lax.fori_loop(0, blocks, add, 0)
    out_ref[...] = total_ref[...].astype(out_ref.dtype)


def dot(left, right, left_dim, right_dim):
    return lax.dot_general(
        left, right, (((left_dim,), (right_dim,)), ((), ())), preferred_element_type=jnp.float32
    )


def attend_kernel(
    selection_ref,
    position_ref,
    query_ref,
    key_ref,
    value_ref,
    grad_ref,
    listed_ref,
    grad_query_ref,
    terms_ref,
    own_ref,
    prob_ref,
    grad_prob_ref,
    prob_low_ref,
    grad_score_ref,
):
    head, heads = pl.program_id(0), pl.num_programs(0)
    block = position_ref[0]
    rows = query_ref.shape[0]
    chunks, _, _, chunk, _ = listed_ref.shape
    live = [
        selection_ref[(block * heads + head) * TOPK + slot] < block for slot in range(TOPK)
    ]

    def slot_rows(which, slot):
        if slot == TOPK:
            return (key_ref, value_ref)[which][...]
        return listed_ref[:, which, slot].reshape(rows, HEAD_DIM)

    def query_tile(index, carry):
        first = pl.multiple_of(index * TILE, TILE)
        tile = pl.ds(first, TILE)
        query, grad = query_ref[tile, :], grad_ref[tile, :]
        top = None
        for slot in range(TOPK + 1):
            scores = dot(slot_rows(0, slot), query, 1, 1)
            if slot == TOPK:
                key_at = lax.broadcasted_iota(jnp.int32, scores.shape, 0)
                query_at = lax.broadcasted_iota(jnp.int32, scores.shape, 1) + first
                scores = jnp.where(key_at <= query_at, scores, MASKED)
            prob_ref[slot] = scores
            highest = jnp.max(scores, axis=0, keepdims=True)
            if slot < TOPK:
                highest = jnp.where(live[slot], highest, MASKED)
            top = highest if top is None else jnp.maximum(top, highest)
        total = jnp.zeros_like(top)
        for slot in range(TOPK + 1):
            shift = jnp.where(live[slot], top, -MASKED) if slot < TOPK else top
            raised = jnp.exp2((prob_ref[slot] - shift) * (SCALING * math.log2(math.e)))
            prob_ref[slot] = raised
            total += jnp.sum(raised, axis=0, keepdims=True)
        inverse = 1.0 / total
        delta = jnp.zeros_like(top)
        for slot in range(TOPK + 1):
            probability = prob_ref[slot] * inverse
            prob_ref[slot] = probability
            low = probability.astype(jnp.bfloat16)
            prob_low_ref[slot, :, tile] = low
            grad_probs = dot(slot_rows(1, slot), grad, 1, 1)
            grad_prob_ref[slot] = grad_probs
            delta += jnp.sum(low.astype(jnp.float32) * grad_probs, axis=0, keepdims=True)
        for slot in range(TOPK + 1):
            grad_score_ref[slot, :, tile] = (
                prob_ref[slot] * (grad_prob_ref[slot] - delta)
            ).astype(jnp.bfloat16)
        return carry

    lax.fori_loop(0, rows // TILE, query_tile, 0)
    query, grad = query_ref[...], grad_ref[...]
    grad_query = None
    for slot in range(TOPK + 1):
        grad_scores = grad_score_ref[slot]
        grad_value = dot(prob_low_ref[slot], grad, 1, 0).reshape(chunks, chunk, HEAD_DIM)
        grad_key = (dot(grad_scores, query, 1, 0) * SCALING).reshape(chunks, chunk, HEAD_DIM)
        if slot < TOPK:
            terms_ref[:, 0, slot] = grad_key.astype(jnp.bfloat16)
            terms_ref[:, 1, slot] = grad_value.astype(jnp.bfloat16)
        else:
            own_ref[:, 0] = grad_key
            own_ref[:, 1] = grad_value
        part = dot(slot_rows(0, slot).T, grad_scores, 1, 0)
        grad_query = part if grad_query is None else grad_query + part
    grad_query_ref[...] = (grad_query * SCALING).T.astype(jnp.bfloat16)


def on_device(query_input, key_input, value_input, grad_output, selection):
    rows, width = query_input.shape
    heads = width // HEAD_DIM
    chain, spread = lax.axis_size("chain"), lax.axis_size("heads")
    chunk = rows // chain
    listed = selection.reshape(-1)
    position = lax.axis_index("chain").astype(jnp.int32).reshape(1)
    smem = pl.BlockSpec(memory_space=pltpu.SMEM)
    vmem = pl.BlockSpec(memory_space=pltpu.VMEM)

    def swap(array, axis):
        return lax.all_to_all(array, axis, split_axis=0, concat_axis=0, tiled=True)

    pair = jnp.stack(
        [part.reshape(chain, chunk, width) for part in (key_input, value_input)], axis=1
    )
    held = swap(pair, "chain")
    picked = pl.pallas_call(
        pick_kernel,
        out_shape=jax.ShapeDtypeStruct((chain, 2, TOPK, chunk, width), jnp.bfloat16),
        in_specs=[smem, vmem],
        out_specs=vmem,
        compiler_params=pltpu.CompilerParams(vmem_limit_bytes=8 * MIB),
        name="pick",
    )(listed, held)
    slots = swap(picked, "chain")

    def head_block(*lead):
        block = lead + (HEAD_DIM,)
        return pl.BlockSpec(block, lambda head, *_: (0,) * len(lead) + (head,))

    grad_query, terms, own = pl.pallas_call(
        attend_kernel,
        out_shape=(
            jax.ShapeDtypeStruct((rows, width), jnp.bfloat16),
            jax.ShapeDtypeStruct((chain, 2, TOPK, chunk, width), jnp.bfloat16),
            jax.ShapeDtypeStruct((chain, 2, chunk, width), jnp.float32),
        ),
        grid_spec=pltpu.PrefetchScalarGridSpec(
            num_scalar_prefetch=2,
            grid=(heads,),
            in_specs=[head_block(rows)] * 4 + [head_block(chain, 2, TOPK, chunk)],
            out_specs=(
                head_block(rows),
                head_block(chain, 2, TOPK, chunk),
                head_block(chain, 2, chunk),
            ),
            scratch_shapes=[
                pltpu.VMEM((TOPK + 1, rows, TILE), jnp.float32),
                pltpu.VMEM((TOPK + 1, rows, TILE), jnp.float32),
                pltpu.VMEM((TOPK + 1, rows, rows), jnp.bfloat16),
                pltpu.VMEM((TOPK + 1, rows, rows), jnp.bfloat16),
            ],
        ),
        compiler_params=pltpu.CompilerParams(vmem_limit_bytes=32 * MIB),
        name="attend",
    )(listed, position, query_input, key_input, value_input, grad_output, slots)

    returned = swap(terms, "chain")
    summed = pl.pallas_call(
        reduce_kernel,
        out_shape=jax.ShapeDtypeStruct((chain, 2, chunk, width), jnp.bfloat16),
        in_specs=[smem, vmem],
        out_specs=vmem,
        scratch_shapes=[pltpu.VMEM((chain, 2, chunk, width), jnp.float32)],
        compiler_params=pltpu.CompilerParams(vmem_limit_bytes=8 * MIB),
        name="reduce",
    )(listed, returned)
    others = swap(summed, "chain")
    whole = (others.astype(jnp.float32) + own).astype(jnp.bfloat16)

    share = rows // spread
    whole = whole.reshape(spread, chain // spread, 2, chunk, width).swapaxes(1, 2)
    whole = swap(whole.reshape(spread, 2, share, width), "heads")
    grad_query = swap(grad_query.reshape(spread, share, width), "heads")

    def lay(array):
        return array.swapaxes(0, 1).reshape(share, spread * width)

    return (lay(grad_query), lay(whole[:, 0]), lay(whole[:, 1]))


def solution(mesh):
    in_specs = (
        P("chain", "heads"),
        P("chain", "heads"),
        P("chain", "heads"),
        P("chain", "heads"),
        P(None, "heads", None),
    )
    out_specs = (
        P(("chain", "heads"), None),
        P(("chain", "heads"), None),
        P(("chain", "heads"), None),
    )
    return jax.shard_map(
        on_device, mesh=mesh, in_specs=in_specs, out_specs=out_specs, check_vma=False
    )
```

```python
import math

import jax
import jax.numpy as jnp
from jax import lax
from jax.experimental import pallas as pl
from jax.experimental.pallas import tpu as pltpu
from jax.sharding import PartitionSpec as P

HEAD_DIM = 128
TOPK = 3
MASKED = -1e30
SCALING = HEAD_DIM ** (-0.5)
EXPONENT = SCALING * math.log2(math.e)
TILE = 256
STATS = 8
MIB = 1 << 20


def head_columns(head, offset=0):
    start = head * HEAD_DIM + offset
    if isinstance(head, int):
        return pl.ds(start, HEAD_DIM)
    return pl.ds(pl.multiple_of(start, HEAD_DIM), HEAD_DIM)


def dot(left, right, left_dim, right_dim):
    return lax.dot_general(
        left, right, (((left_dim,), (right_dim,)), ((), ())), preferred_element_type=jnp.float32
    )


def stack_kernel(key_ref, value_ref, out_ref, held_ref, in_sem, out_sem):
    pieces = in_sem.shape[1]
    length = key_ref.shape[0] // pieces
    arrive, leave = [], []
    for index, part in enumerate((key_ref, value_ref)):
        for piece in range(pieces):
            span = pl.ds(piece * length, length)
            held = held_ref.at[index, span]
            arrive.append(pltpu.make_async_copy(part.at[span], held, in_sem.at[index, piece]))
            leave.append(
                pltpu.make_async_copy(held, out_ref.at[span, index], out_sem.at[index, piece])
            )
    for copy in arrive:
        copy.start()
    for first, second in zip(arrive, leave):
        first.wait()
        second.start()
    for copy in leave:
        copy.wait()


def pick_kernel(selection_ref, held_ref, out_ref, filled_ref, sem):
    blocks, _, _, width = held_ref.shape
    heads = width // HEAD_DIM
    copies = []
    for block in range(blocks):
        for head in range(heads):
            for slot in range(TOPK):
                source = selection_ref[(block * heads + head) * TOPK + slot]
                filled_ref[block, :, slot, :, head_columns(head)] = held_ref[
                    source, :, :, head_columns(head)
                ]
        copies.append(
            pltpu.make_async_copy(filled_ref.at[block], out_ref.at[block], sem.at[block])
        )
        copies[-1].start()
    for copy in copies:
        copy.wait()


def reduce_kernel(selection_ref, terms_ref, out_ref, total_ref, low_ref, sem):
    blocks, _, _, width = out_ref.shape
    heads = width // HEAD_DIM
    total_ref[...] = jnp.zeros_like(total_ref)

    def add(block, carry):
        for head in range(heads):
            for slot in range(TOPK):
                target = selection_ref[(block * heads + head) * TOPK + slot]
                total_ref[target, :, :, head_columns(head)] += terms_ref[
                    block, :, slot, :, head_columns(head)
                ].astype(jnp.float32)
        return carry

    lax.fori_loop(0, blocks, add, 0)
    pieces = sem.shape[0]
    copies = []
    for piece in range(pieces):
        span = pl.ds(piece * (blocks // pieces), blocks // pieces)
        low_ref[span] = total_ref[span].astype(low_ref.dtype)
        copies.append(pltpu.make_async_copy(low_ref.at[span], out_ref.at[span], sem.at[piece]))
        copies[-1].start()
    for copy in copies:
        copy.wait()


def causal(scores, first):
    key_at = lax.broadcasted_iota(jnp.int32, scores.shape, 0)
    query_at = lax.broadcasted_iota(jnp.int32, scores.shape, 1) + first
    return jnp.where(key_at <= query_at, scores, MASKED)


def own_forward_kernel(query_ref, key_ref, value_ref, grad_ref, rows_ref, stats_ref):
    heads, _, rows = stats_ref.shape
    width = heads * HEAD_DIM
    rows_ref[:, :width] = query_ref[...]
    rows_ref[:, width:] = grad_ref[...]

    def one_head(head, carry):
        columns = head_columns(head)
        key, value = key_ref[:, columns], value_ref[:, columns]
        for first in range(0, rows, TILE):
            tile = pl.ds(first, TILE)
            scores = causal(dot(key, query_ref[tile, columns], 1, 1), first)
            top = jnp.max(scores, axis=0, keepdims=True)
            raised = jnp.exp2((scores - top) * EXPONENT)
            product = raised * dot(value, grad_ref[tile, columns], 1, 1)
            stats_ref[head, 0:1, tile] = top
            stats_ref[head, 1:2, tile] = jnp.sum(raised, axis=0, keepdims=True)
            stats_ref[head, 2:3, tile] = jnp.sum(product, axis=0, keepdims=True)
        return carry

    lax.fori_loop(0, heads, one_head, 0)


def far_kernel(
    selection_ref,
    position_ref,
    rows_ref,
    listed_ref,
    own_stats_ref,
    terms_ref,
    grad_scores_ref,
    stats_ref,
    score_ref,
    grad_prob_ref,
    prob_ref,
    grad_score_ref,
    term_ref,
    terms_sem,
    grad_scores_sem,
):
    heads, _, rows = own_stats_ref.shape
    chunks, _, _, chunk, width = listed_ref.shape
    block = position_ref[0]
    copies = []

    def send(source, target, sem):
        copies.append(pltpu.make_async_copy(source, target, sem))
        copies[-1].start()

    for head in range(heads):
        columns, grad_columns = head_columns(head), head_columns(head, width)
        live = [
            selection_ref[(block * heads + head) * TOPK + slot] < block for slot in range(TOPK)
        ]
        keys = [listed_ref[:, 0, slot, :, columns].reshape(rows, HEAD_DIM) for slot in range(TOPK)]
        values = [
            listed_ref[:, 1, slot, :, columns].reshape(rows, HEAD_DIM) for slot in range(TOPK)
        ]
        for first in range(0, rows, TILE):
            tile = pl.ds(first, TILE)
            query, grad = rows_ref[tile, columns], rows_ref[tile, grad_columns]
            top = jnp.full((1, TILE), MASKED, jnp.float32)
            for slot in range(TOPK):
                scores = dot(keys[slot], query, 1, 1)
                score_ref[head, slot, :, tile] = scores
                highest = jnp.max(scores, axis=0, keepdims=True)
                top = jnp.maximum(top, jnp.where(live[slot], highest, MASKED))
            total = jnp.zeros_like(top)
            product = jnp.zeros_like(top)
            for slot in range(TOPK):
                shift = jnp.where(live[slot], top, -MASKED)
                raised = jnp.exp2((score_ref[head, slot, :, tile] - shift) * EXPONENT)
                score_ref[head, slot, :, tile] = raised
                grad_probs = dot(values[slot], grad, 1, 1)
                grad_prob_ref[head, slot, :, tile] = grad_probs
                total += jnp.sum(raised, axis=0, keepdims=True)
                product += jnp.sum(raised * grad_probs, axis=0, keepdims=True)
            own_top = own_stats_ref[head, 0:1, tile]
            highest = jnp.maximum(own_top, top)
            own_factor = jnp.exp2((own_top - highest) * EXPONENT)
            factor = jnp.exp2((top - highest) * EXPONENT)
            inverse = 1.0 / (own_factor * own_stats_ref[head, 1:2, tile] + factor * total)
            own_weight, weight = own_factor * inverse, factor * inverse
            delta = own_weight * own_stats_ref[head, 2:3, tile] + weight * product
            stats_ref[head, 0:1, tile] = own_weight
            stats_ref[head, 1:2, tile] = delta
            for slot in range(TOPK):
                probability = score_ref[head, slot, :, tile] * weight
                prob_ref[head, slot, :, tile] = probability.astype(jnp.bfloat16)
                grad_score_ref[head, slot, :, tile] = (
                    probability * (grad_prob_ref[head, slot, :, tile] - delta)
                ).astype(jnp.bfloat16)
        query, grad = rows_ref[:, columns], rows_ref[:, grad_columns]
        shape = (chunks, chunk, HEAD_DIM)
        for slot in range(TOPK):
            grad_scores = grad_score_ref[head, slot]
            send(
                grad_score_ref.at[head, slot],
                grad_scores_ref.at[head, slot],
                grad_scores_sem.at[head, slot],
            )
            grad_key = dot(grad_scores, query, 1, 0) * SCALING
            grad_value = dot(prob_ref[head, slot], grad, 1, 0)
            for which, term in enumerate((grad_key, grad_value)):
                term_ref[:, which, slot, :, columns] = term.astype(jnp.bfloat16).reshape(shape)
                send(
                    term_ref.at[:, which, slot, :, columns],
                    terms_ref.at[:, which, slot, :, columns],
                    terms_sem.at[head, slot, which],
                )
    for copy in copies:
        copy.wait()


def own_backward_kernel(
    query_ref,
    key_ref,
    value_ref,
    grad_ref,
    listed_ref,
    grad_scores_ref,
    own_stats_ref,
    stats_ref,
    own_ref,
):
    heads, _, rows = stats_ref.shape
    chunks, _, chunk, _ = own_ref.shape

    def one_head(head, carry):
        columns = head_columns(head)
        query, key = query_ref[:, columns], key_ref[:, columns]
        value, grad = value_ref[:, columns], grad_ref[:, columns]
        shape = (chunks, chunk, HEAD_DIM)
        scores = causal(dot(key, query, 1, 1), 0)
        raised = jnp.exp2((scores - own_stats_ref[head, 0:1, :]) * EXPONENT)
        probability = raised * stats_ref[head, 0:1, :]
        grad_probs = dot(value, grad, 1, 1)
        grad_scores = (probability * (grad_probs - stats_ref[head, 1:2, :])).astype(jnp.bfloat16)
        grad_key = dot(grad_scores, query, 1, 0) * SCALING
        own_ref[:, 1, :, columns] = grad_key.reshape(shape)
        grad_value = dot(probability.astype(jnp.bfloat16), grad, 1, 0)
        own_ref[:, 2, :, columns] = grad_value.reshape(shape)
        part = dot(key.T, grad_scores, 1, 0)
        for slot in range(TOPK):
            listed = listed_ref[:, 0, slot, :, columns].reshape(rows, HEAD_DIM)
            part += dot(listed.T, grad_scores_ref[head, slot], 1, 0)
        own_ref[:, 0, :, columns] = (part * SCALING).T.reshape(shape)
        return carry

    lax.fori_loop(0, heads, one_head, 0)


def finish_kernel(own_ref, others_ref, out_ref):
    out_ref[:, 0] = own_ref[:, 0].astype(jnp.bfloat16)
    out_ref[:, 1:] = (others_ref[...].astype(jnp.float32) + own_ref[:, 1:]).astype(jnp.bfloat16)


def lay_kernel(parts_ref, *refs):
    outs, sem = refs[:-1], refs[-1]
    senders, _, _, width = parts_ref.shape
    copies = [
        pltpu.make_async_copy(
            parts_ref.at[sender, index],
            out.at[:, pl.ds(sender * width, width)],
            sem.at[index, sender],
        )
        for index, out in enumerate(outs)
        for sender in range(senders)
    ]
    for copy in copies:
        copy.start()
    for copy in copies:
        copy.wait()


def on_device(query_input, key_input, value_input, grad_output, selection):
    rows, width = query_input.shape
    heads = width // HEAD_DIM
    chain, spread = lax.axis_size("chain"), lax.axis_size("heads")
    chunk = rows // chain
    share = rows // spread
    listed = selection.reshape(-1)
    position = lax.axis_index("chain").astype(jnp.int32).reshape(1)
    smem = pl.BlockSpec(memory_space=pltpu.SMEM)
    vmem = pl.BlockSpec(memory_space=pltpu.VMEM)
    anywhere = pl.BlockSpec(memory_space=pl.ANY)
    low, full = jnp.bfloat16, jnp.float32

    def swap(array, axis):
        return lax.all_to_all(array, axis, split_axis=0, concat_axis=0, tiled=True)

    def call(kernel, name, in_specs, out_specs, out_shape, scratch=(), limit=4, slots=0):
        flops = 2 * heads * slots * rows * rows * HEAD_DIM
        return pl.pallas_call(
            kernel,
            out_shape=out_shape,
            in_specs=in_specs,
            out_specs=out_specs,
            scratch_shapes=list(scratch),
            cost_estimate=pl.CostEstimate(
                flops=flops, bytes_accessed=4 * MIB, transcendentals=heads * rows * rows
            ),
            compiler_params=pltpu.CompilerParams(vmem_limit_bytes=limit * MIB),
            name=name,
        )

    pair = call(
        stack_kernel,
        "stack",
        [anywhere] * 2,
        anywhere,
        jax.ShapeDtypeStruct((chain, 2, chunk, width), low),
        [
            pltpu.VMEM((2, chain, chunk, width), low),
            pltpu.SemaphoreType.DMA((2, 2)),
            pltpu.SemaphoreType.DMA((2, 2)),
        ],
        limit=59,
    )(key_input.reshape(chain, chunk, width), value_input.reshape(chain, chunk, width))
    held = swap(pair, "chain")
    picked = call(
        pick_kernel,
        "pick",
        [smem, vmem],
        anywhere,
        jax.ShapeDtypeStruct((chain, 2, TOPK, chunk, width), low),
        [
            pltpu.VMEM((chain, 2, TOPK, chunk, width), low),
            pltpu.SemaphoreType.DMA((chain,)),
        ],
    )(listed, held)
    slots = swap(picked, "chain")
    own_rows, own_stats = call(
        own_forward_kernel,
        "own_forward",
        [vmem] * 4,
        (vmem, vmem),
        (
            jax.ShapeDtypeStruct((rows, 2 * width), low),
            jax.ShapeDtypeStruct((heads, STATS, rows), full),
        ),
        limit=12,
        slots=2,
    )(query_input, key_input, value_input, grad_output)
    terms, grad_scores, stats = call(
        far_kernel,
        "far",
        [smem, smem] + [vmem] * 3,
        (anywhere, anywhere, vmem),
        (
            jax.ShapeDtypeStruct((chain, 2, TOPK, chunk, width), low),
            jax.ShapeDtypeStruct((heads, TOPK, rows, rows), low),
            jax.ShapeDtypeStruct((heads, STATS, rows), full),
        ),
        [
            pltpu.VMEM((heads, TOPK, rows, rows), full),
            pltpu.VMEM((heads, TOPK, rows, rows), full),
            pltpu.VMEM((heads, TOPK, rows, rows), low),
            pltpu.VMEM((heads, TOPK, rows, rows), low),
            pltpu.VMEM((chain, 2, TOPK, chunk, width), low),
            pltpu.SemaphoreType.DMA((heads, TOPK, 2)),
            pltpu.SemaphoreType.DMA((heads, TOPK)),
        ],
        limit=32,
        slots=4 * TOPK,
    )(listed, position, own_rows, slots, own_stats)
    returned = swap(terms, "chain")
    own = call(
        own_backward_kernel,
        "own_backward",
        [vmem] * 8,
        vmem,
        jax.ShapeDtypeStruct((chain, 3, chunk, width), full),
        limit=12,
        slots=5 + TOPK,
    )(
        query_input, key_input, value_input, grad_output, slots, grad_scores, own_stats, stats
    )
    summed = call(
        reduce_kernel,
        "reduce",
        [smem, vmem],
        anywhere,
        jax.ShapeDtypeStruct((chain, 2, chunk, width), low),
        [
            pltpu.VMEM((chain, 2, chunk, width), full),
            pltpu.VMEM((chain, 2, chunk, width), low),
            pltpu.SemaphoreType.DMA((4,)),
        ],
    )(listed, returned)
    others = swap(summed, "chain")

    def by_share(array):
        lead = array.shape[1:-2]
        array = array.reshape((spread, chain // spread) + lead + (chunk, width))
        return jnp.moveaxis(array, 1, -3).reshape((spread,) + lead + (share, width))

    whole = call(
        finish_kernel,
        "finish",
        [vmem] * 2,
        vmem,
        jax.ShapeDtypeStruct((spread, 3, share, width), low),
    )(by_share(own), by_share(others))
    whole = swap(whole, "heads")
    return call(
        lay_kernel,
        "lay",
        [vmem],
        (anywhere,) * 3,
        (jax.ShapeDtypeStruct((share, spread * width), low),) * 3,
        [pltpu.SemaphoreType.DMA((3, spread))],
    )(whole)


def solution(mesh):
    in_specs = (
        P("chain", "heads"),
        P("chain", "heads"),
        P("chain", "heads"),
        P("chain", "heads"),
        P(None, "heads", None),
    )
    out_specs = (
        P(("chain", "heads"), None),
        P(("chain", "heads"), None),
        P(("chain", "heads"), None),
    )
    return jax.shard_map(
        on_device, mesh=mesh, in_specs=in_specs, out_specs=out_specs, check_vma=False
    )
```

```python
import math

import jax
import jax.numpy as jnp
from jax import lax
from jax.experimental import pallas as pl
from jax.experimental.pallas import tpu as pltpu
from jax.sharding import PartitionSpec as P

HEAD_DIM = 128
TOPK = 3
MASKED = -1e30
SCALING = HEAD_DIM ** (-0.5)
EXPONENT = SCALING * math.log2(math.e)
TILE = 256
STATS = 8
MIB = 1 << 20


def head_columns(head, offset=0):
    start = head * HEAD_DIM + offset
    if isinstance(head, int):
        return pl.ds(start, HEAD_DIM)
    return pl.ds(pl.multiple_of(start, HEAD_DIM), HEAD_DIM)


def dot(left, right, left_dim, right_dim):
    return lax.dot_general(
        left, right, (((left_dim,), (right_dim,)), ((), ())), preferred_element_type=jnp.float32
    )


def stack_kernel(key_ref, value_ref, out_ref, held_ref, in_sem, out_sem):
    pieces = in_sem.shape[1]
    length = key_ref.shape[0] // pieces
    arrive, leave = [], []
    for index, part in enumerate((key_ref, value_ref)):
        for piece in range(pieces):
            span = pl.ds(piece * length, length)
            held = held_ref.at[index, span]
            arrive.append(pltpu.make_async_copy(part.at[span], held, in_sem.at[index, piece]))
            leave.append(
                pltpu.make_async_copy(held, out_ref.at[span, index], out_sem.at[index, piece])
            )
    for copy in arrive:
        copy.start()
    for first, second in zip(arrive, leave):
        first.wait()
        second.start()
    for copy in leave:
        copy.wait()


def pick_kernel(selection_ref, held_ref, after_ref, out_ref):
    blocks, _, _, width = held_ref.shape
    heads = width // HEAD_DIM
    for block in range(blocks):
        for head in range(heads):
            for slot in range(TOPK):
                source = selection_ref[(block * heads + head) * TOPK + slot]
                out_ref[block, :, slot, :, head_columns(head)] = held_ref[
                    source, :, :, head_columns(head)
                ]


def reduce_kernel(selection_ref, terms_ref, out_ref, *total_refs):
    blocks, _, _, width = out_ref.shape
    heads = width // HEAD_DIM
    for total_ref in total_refs:
        total_ref[...] = jnp.zeros_like(total_ref)

    def add(block, carry):
        for slot in range(TOPK):
            for head, total_ref in enumerate(total_refs):
                target = selection_ref[(block * heads + head) * TOPK + slot]
                total_ref[target] += terms_ref[block, :, slot, :, head_columns(head)].astype(
                    jnp.float32
                )
        return carry

    lax.fori_loop(0, blocks, add, 0, unroll=4)
    for head, total_ref in enumerate(total_refs):
        out_ref[:, :, :, head_columns(head)] = total_ref[...].astype(out_ref.dtype)


def causal(scores, first):
    key_at = lax.broadcasted_iota(jnp.int32, scores.shape, 0)
    query_at = lax.broadcasted_iota(jnp.int32, scores.shape, 1) + first
    return jnp.where(key_at <= query_at, scores, MASKED)


def own_forward_kernel(
    query_ref, key_ref, value_ref, grad_ref, rows_ref, stats_ref, held_ref, sem
):
    heads, _, rows = stats_ref.shape
    targets = (rows_ref, held_ref.at[0], held_ref.at[1], held_ref.at[2])
    copies = [
        pltpu.make_async_copy(source, target, sem.at[index])
        for index, (source, target) in enumerate(
            zip((query_ref, key_ref, value_ref, grad_ref), targets)
        )
    ]
    for copy in copies:
        copy.start()
    for copy in copies:
        copy.wait()

    def one_head(head, carry):
        columns = head_columns(head)
        key, value = held_ref[0, :, columns], held_ref[1, :, columns]
        for first in range(0, rows, TILE):
            tile = pl.ds(first, TILE)
            scores = causal(dot(key, rows_ref[tile, columns], 1, 1), first)
            top = jnp.max(scores, axis=0, keepdims=True)
            raised = jnp.exp2((scores - top) * EXPONENT)
            product = raised * dot(value, held_ref[2, tile, columns], 1, 1)
            stats_ref[head, 0:1, tile] = top
            stats_ref[head, 1:2, tile] = jnp.sum(raised, axis=0, keepdims=True)
            stats_ref[head, 2:3, tile] = jnp.sum(product, axis=0, keepdims=True)
        return carry

    lax.fori_loop(0, heads, one_head, 0)


def far_kernel(
    selection_ref,
    position_ref,
    rows_ref,
    grad_ref,
    listed_ref,
    own_stats_ref,
    terms_ref,
    part_ref,
    stats_ref,
    grad_rows_ref,
    sem,
    *scratch,
):
    heads, _, rows = own_stats_ref.shape
    chunks, _, _, chunk, _ = listed_ref.shape
    block = position_ref[0]
    fetch = pltpu.make_async_copy(grad_ref, grad_rows_ref, sem)
    fetch.start()

    def listed(which, slot, head):
        return listed_ref[:, which, slot, :, head_columns(head)].reshape(rows, HEAD_DIM)

    def softmax(head):
        score_ref, grad_prob_ref, prob_ref, grad_score_ref = scratch[4 * head : 4 * head + 4]
        columns = head_columns(head)
        live = [
            selection_ref[(block * heads + head) * TOPK + slot] < block for slot in range(TOPK)
        ]
        for first in range(0, rows, TILE):
            tile = pl.ds(first, TILE)
            top = jnp.full((1, TILE), MASKED, jnp.float32)
            for slot in range(TOPK):
                scores = dot(listed(0, slot, head), rows_ref[tile, columns], 1, 1)
                score_ref[slot, :, tile] = scores
                highest = jnp.max(scores, axis=0, keepdims=True)
                top = jnp.maximum(top, jnp.where(live[slot], highest, MASKED))
            if head == 0 and first == 0:
                fetch.wait()
            total = jnp.zeros_like(top)
            product = jnp.zeros_like(top)
            for slot in range(TOPK):
                shift = jnp.where(live[slot], top, -MASKED)
                raised = jnp.exp2((score_ref[slot, :, tile] - shift) * EXPONENT)
                score_ref[slot, :, tile] = raised
                grad_probs = dot(listed(1, slot, head), grad_rows_ref[tile, columns], 1, 1)
                grad_prob_ref[slot, :, tile] = grad_probs
                total += jnp.sum(raised, axis=0, keepdims=True)
                product += jnp.sum(raised * grad_probs, axis=0, keepdims=True)
            own_top = own_stats_ref[head, 0:1, tile]
            highest = jnp.maximum(own_top, top)
            own_factor = jnp.exp2((own_top - highest) * EXPONENT)
            factor = jnp.exp2((top - highest) * EXPONENT)
            inverse = 1.0 / (own_factor * own_stats_ref[head, 1:2, tile] + factor * total)
            own_weight, weight = own_factor * inverse, factor * inverse
            delta = own_weight * own_stats_ref[head, 2:3, tile] + weight * product
            stats_ref[head, 0:1, tile] = own_weight
            stats_ref[head, 1:2, tile] = delta
            for slot in range(TOPK):
                probability = score_ref[slot, :, tile] * weight
                prob_ref[slot, :, tile] = probability.astype(jnp.bfloat16)
                grad_score_ref[slot, :, tile] = (
                    probability * (grad_prob_ref[slot, :, tile] - delta)
                ).astype(jnp.bfloat16)

    def gradients(head):
        _, _, prob_ref, grad_score_ref = scratch[4 * head : 4 * head + 4]
        columns = head_columns(head)
        query, grad = rows_ref[:, columns], grad_rows_ref[:, columns]
        shape = (chunks, chunk, HEAD_DIM)
        part = None
        for slot in range(TOPK):
            grad_scores = grad_score_ref[slot]
            grad_key = dot(grad_scores, query, 1, 0) * SCALING
            terms_ref[:, 0, slot, :, columns] = grad_key.astype(jnp.bfloat16).reshape(shape)
            grad_value = dot(prob_ref[slot], grad, 1, 0)
            terms_ref[:, 1, slot, :, columns] = grad_value.astype(jnp.bfloat16).reshape(shape)
            product = dot(listed(0, slot, head).T, grad_scores, 1, 0)
            part = product if part is None else part + product
        part_ref[head] = part

    for head in range(heads):
        softmax(head)
        gradients(head)


def own_backward_kernel(
    query_ref,
    key_ref,
    value_ref,
    grad_ref,
    part_ref,
    own_stats_ref,
    stats_ref,
    own_ref,
):
    heads, _, rows = stats_ref.shape
    chunks, _, chunk, _ = own_ref.shape

    def one_head(head, carry):
        columns = head_columns(head)
        query, key = query_ref[:, columns], key_ref[:, columns]
        value, grad = value_ref[:, columns], grad_ref[:, columns]
        scores = causal(dot(key, query, 1, 1), 0)
        raised = jnp.exp2((scores - own_stats_ref[head, 0:1, :]) * EXPONENT)
        probability = raised * stats_ref[head, 0:1, :]
        grad_probs = dot(value, grad, 1, 1)
        grad_scores = (probability * (grad_probs - stats_ref[head, 1:2, :])).astype(jnp.bfloat16)
        results = (
            ((part_ref[head] + dot(key.T, grad_scores, 1, 0)) * SCALING).T,
            dot(grad_scores, query, 1, 0) * SCALING,
            dot(probability.astype(jnp.bfloat16), grad, 1, 0),
        )
        for index, result in enumerate(results):
            own_ref[:, index, :, columns] = result.astype(jnp.bfloat16).reshape(
                chunks, chunk, HEAD_DIM
            )
        return carry

    lax.fori_loop(0, heads, one_head, 0)


def finish_kernel(own_ref, others_ref, out_ref):
    out_ref[:, 0] = own_ref[:, 0]
    out_ref[:, 1:] = (
        others_ref[...].astype(jnp.float32) + own_ref[:, 1:].astype(jnp.float32)
    ).astype(jnp.bfloat16)


def lay_kernel(parts_ref, *refs):
    outs, sem = refs[:-1], refs[-1]
    senders, _, _, width = parts_ref.shape
    copies = [
        pltpu.make_async_copy(
            parts_ref.at[sender, index],
            out.at[:, pl.ds(sender * width, width)],
            sem.at[index, sender],
        )
        for index, out in enumerate(outs)
        for sender in range(senders)
    ]
    for copy in copies:
        copy.start()
    for copy in copies:
        copy.wait()


def on_device(query_input, key_input, value_input, grad_output, selection):
    rows, width = query_input.shape
    heads = width // HEAD_DIM
    chain, spread = lax.axis_size("chain"), lax.axis_size("heads")
    chunk = rows // chain
    share = rows // spread
    listed = selection.reshape(-1)
    position = lax.axis_index("chain").astype(jnp.int32).reshape(1)
    smem = pl.BlockSpec(memory_space=pltpu.SMEM)
    vmem = pl.BlockSpec(memory_space=pltpu.VMEM)
    anywhere = pl.BlockSpec(memory_space=pl.ANY)
    low, full = jnp.bfloat16, jnp.float32

    def swap(array, axis):
        return lax.all_to_all(array, axis, split_axis=0, concat_axis=0, tiled=True)

    def call(kernel, name, in_specs, out_specs, out_shape, scratch=(), limit=4, slots=0):
        flops = 2 * heads * slots * rows * rows * HEAD_DIM
        return pl.pallas_call(
            kernel,
            out_shape=out_shape,
            in_specs=in_specs,
            out_specs=out_specs,
            scratch_shapes=list(scratch),
            cost_estimate=pl.CostEstimate(
                flops=flops, bytes_accessed=4 * MIB, transcendentals=heads * rows * rows
            ),
            compiler_params=pltpu.CompilerParams(vmem_limit_bytes=limit * MIB),
            name=name,
        )

    pair = call(
        stack_kernel,
        "stack",
        [anywhere] * 2,
        anywhere,
        jax.ShapeDtypeStruct((chain, 2, chunk, width), low),
        [
            pltpu.VMEM((2, chain, chunk, width), low),
            pltpu.SemaphoreType.DMA((2, 2)),
            pltpu.SemaphoreType.DMA((2, 2)),
        ],
        limit=59,
    )(key_input.reshape(chain, chunk, width), value_input.reshape(chain, chunk, width))
    held = swap(pair, "chain")
    own_rows, own_stats = call(
        own_forward_kernel,
        "own_forward",
        [anywhere] * 4,
        (vmem, vmem),
        (
            jax.ShapeDtypeStruct((rows, width), low),
            jax.ShapeDtypeStruct((heads, STATS, rows), full),
        ),
        [pltpu.VMEM((3, rows, width), low), pltpu.SemaphoreType.DMA((4,))],
        limit=58,
        slots=2,
    )(query_input, key_input, value_input, grad_output)
    picked = call(
        pick_kernel,
        "pick",
        [smem, vmem, anywhere],
        vmem,
        jax.ShapeDtypeStruct((chain, 2, TOPK, chunk, width), low),
    )(listed, held, own_stats)
    slots = swap(picked, "chain")
    terms, part, stats = call(
        far_kernel,
        "far",
        [smem, smem, vmem, anywhere, vmem, vmem],
        (vmem, vmem, vmem),
        (
            jax.ShapeDtypeStruct((chain, 2, TOPK, chunk, width), low),
            jax.ShapeDtypeStruct((heads, HEAD_DIM, rows), full),
            jax.ShapeDtypeStruct((heads, STATS, rows), full),
        ),
        [pltpu.VMEM((rows, width), low), pltpu.SemaphoreType.DMA(())]
        + [
            pltpu.VMEM((TOPK, rows, rows), full),
            pltpu.VMEM((TOPK, rows, rows), full),
            pltpu.VMEM((TOPK, rows, rows), low),
            pltpu.VMEM((TOPK, rows, rows), low),
        ]
        * heads,
        limit=32,
        slots=5 * TOPK,
    )(listed, position, own_rows, grad_output, slots, own_stats)
    returned = swap(terms, "chain")
    own = call(
        own_backward_kernel,
        "own_backward",
        [vmem] * 7,
        vmem,
        jax.ShapeDtypeStruct((chain, 3, chunk, width), low),
        limit=12,
        slots=5,
    )(query_input, key_input, value_input, grad_output, part, own_stats, stats)
    summed = call(
        reduce_kernel,
        "reduce",
        [smem, vmem],
        vmem,
        jax.ShapeDtypeStruct((chain, 2, chunk, width), low),
        [pltpu.VMEM((chain, 2, chunk, HEAD_DIM), full)] * heads,
    )(listed, returned)
    others = swap(summed, "chain")

    def by_share(array):
        lead = array.shape[1:-2]
        array = array.reshape((spread, chain // spread) + lead + (chunk, width))
        return jnp.moveaxis(array, 1, -3).reshape((spread,) + lead + (share, width))

    whole = call(
        finish_kernel,
        "finish",
        [vmem] * 2,
        vmem,
        jax.ShapeDtypeStruct((spread, 3, share, width), low),
    )(by_share(own), by_share(others))
    whole = swap(whole, "heads")
    return call(
        lay_kernel,
        "lay",
        [vmem],
        (anywhere,) * 3,
        (jax.ShapeDtypeStruct((share, spread * width), low),) * 3,
        [pltpu.SemaphoreType.DMA((3, spread))],
    )(whole)


def solution(mesh):
    in_specs = (
        P("chain", "heads"),
        P("chain", "heads"),
        P("chain", "heads"),
        P("chain", "heads"),
        P(None, "heads", None),
    )
    out_specs = (
        P(("chain", "heads"), None),
        P(("chain", "heads"), None),
        P(("chain", "heads"), None),
    )
    return jax.shard_map(
        on_device, mesh=mesh, in_specs=in_specs, out_specs=out_specs, check_vma=False
    )
```

```python
import math

import jax
import jax.numpy as jnp
from jax import lax
from jax.experimental import pallas as pl
from jax.experimental.pallas import tpu as pltpu
from jax.sharding import PartitionSpec as P

HEAD_DIM = 128
TOPK = 3
MASKED = -1e30
SCALING = HEAD_DIM ** (-0.5)
EXPONENT = SCALING * math.log2(math.e)
TILE = 256
STATS = 8
MIB = 1 << 20


def head_columns(head, offset=0):
    start = head * HEAD_DIM + offset
    if isinstance(head, int):
        return pl.ds(start, HEAD_DIM)
    return pl.ds(pl.multiple_of(start, HEAD_DIM), HEAD_DIM)


def dot(left, right, left_dim, right_dim):
    return lax.dot_general(
        left, right, (((left_dim,), (right_dim,)), ((), ())), preferred_element_type=jnp.float32
    )


def stack_kernel(key_ref, value_ref, out_ref, held_ref, in_sem, out_sem):
    pieces = in_sem.shape[1]
    length = key_ref.shape[0] // pieces
    arrive, leave = [], []
    for index, part in enumerate((key_ref, value_ref)):
        for piece in range(pieces):
            span = pl.ds(piece * length, length)
            held = held_ref.at[index, span]
            arrive.append(pltpu.make_async_copy(part.at[span], held, in_sem.at[index, piece]))
            leave.append(
                pltpu.make_async_copy(held, out_ref.at[span, index], out_sem.at[index, piece])
            )
    for copy in arrive:
        copy.start()
    for first, second in zip(arrive, leave):
        first.wait()
        second.start()
    for copy in leave:
        copy.wait()


def pick_kernel(selection_ref, held_ref, out_ref, filled_ref, sem):
    blocks, _, _, width = held_ref.shape
    heads = width // HEAD_DIM
    copies = []
    for block in range(blocks):
        filled_ref[block, :, 0] = held_ref[max(block - 1, 0)]
        for head in range(heads):
            columns = head_columns(head)
            for slot in range(1, TOPK):
                source = selection_ref[(block * heads + head) * TOPK + slot]
                filled_ref[block, :, slot, :, columns] = held_ref[source, :, :, columns]
        copies.append(
            pltpu.make_async_copy(filled_ref.at[block], out_ref.at[block], sem.at[block])
        )
        copies[-1].start()
    for copy in copies:
        copy.wait()


def reduce_kernel(selection_ref, terms_ref, out_ref, *total_refs):
    blocks, _, _, width = out_ref.shape
    heads = width // HEAD_DIM
    for head, total_ref in enumerate(total_refs):
        total_ref[: blocks - 1] = terms_ref[1:, :, 0, :, head_columns(head)].astype(jnp.float32)
        total_ref[blocks - 1] = jnp.zeros_like(total_ref[blocks - 1])
    for block in range(blocks):
        for slot in range(1, TOPK):
            for head, total_ref in enumerate(total_refs):
                target = selection_ref[(block * heads + head) * TOPK + slot]
                total_ref[target] += terms_ref[block, :, slot, :, head_columns(head)].astype(
                    jnp.float32
                )
    for head, total_ref in enumerate(total_refs):
        out_ref[:, :, :, head_columns(head)] = total_ref[...].astype(out_ref.dtype)


def causal(scores, first):
    key_at = lax.broadcasted_iota(jnp.int32, scores.shape, 0)
    query_at = lax.broadcasted_iota(jnp.int32, scores.shape, 1) + first
    return jnp.where(key_at <= query_at, scores, MASKED)


def own_forward_kernel(
    query_ref, key_ref, value_ref, grad_ref, rows_ref, stats_ref, held_ref, sem
):
    heads, _, rows = stats_ref.shape
    targets = (rows_ref, held_ref.at[0], held_ref.at[1], held_ref.at[2])
    copies = [
        pltpu.make_async_copy(source, target, sem.at[index])
        for index, (source, target) in enumerate(
            zip((query_ref, key_ref, value_ref, grad_ref), targets)
        )
    ]
    for copy in copies:
        copy.start()
    for copy in copies:
        copy.wait()

    def one_head(head, carry):
        columns = head_columns(head)
        key, value = held_ref[0, :, columns], held_ref[1, :, columns]
        for first in range(0, rows, TILE):
            tile = pl.ds(first, TILE)
            scores = causal(dot(key, rows_ref[tile, columns], 1, 1), first)
            top = jnp.max(scores, axis=0, keepdims=True)
            raised = jnp.exp2((scores - top) * EXPONENT)
            product = raised * dot(value, held_ref[2, tile, columns], 1, 1)
            stats_ref[head, 0:1, tile] = top
            stats_ref[head, 1:2, tile] = jnp.sum(raised, axis=0, keepdims=True)
            stats_ref[head, 2:3, tile] = jnp.sum(product, axis=0, keepdims=True)
        return carry

    lax.fori_loop(0, heads, one_head, 0)


def far_kernel(
    selection_ref,
    position_ref,
    rows_ref,
    grad_ref,
    listed_ref,
    own_stats_ref,
    terms_ref,
    part_ref,
    stats_ref,
    grad_rows_ref,
    sem,
    score_ref,
    grad_prob_ref,
    prob_ref,
    grad_score_ref,
):
    heads, _, rows = own_stats_ref.shape
    chunks, _, _, chunk, _ = listed_ref.shape
    block = position_ref[0]
    fetch = pltpu.make_async_copy(grad_ref, grad_rows_ref, sem)
    fetch.start()

    def one_head(head, carry):
        columns = head_columns(head)
        live = [
            selection_ref[(block * heads + head) * TOPK + slot] < block for slot in range(TOPK)
        ]

        def listed(which, slot):
            return listed_ref[:, which, slot, :, columns].reshape(rows, HEAD_DIM)

        def scores_of(tile):
            top = jnp.full((1, TILE), MASKED, jnp.float32)
            for slot in range(TOPK):
                scores = dot(listed(0, slot), rows_ref[tile, columns], 1, 1)
                score_ref[slot, :, tile] = scores
                highest = jnp.max(scores, axis=0, keepdims=True)
                top = jnp.maximum(top, jnp.where(live[slot], highest, MASKED))
            return top

        tiles = [pl.ds(first, TILE) for first in range(0, rows, TILE)]
        tops = [scores_of(tile) for tile in tiles]
        pl.when(head == 0)(fetch.wait)
        for tile, top in zip(tiles, tops):
            total = jnp.zeros_like(top)
            product = jnp.zeros_like(top)
            for slot in range(TOPK):
                shift = jnp.where(live[slot], top, -MASKED)
                raised = jnp.exp2((score_ref[slot, :, tile] - shift) * EXPONENT)
                score_ref[slot, :, tile] = raised
                grad_probs = dot(listed(1, slot), grad_rows_ref[tile, columns], 1, 1)
                grad_prob_ref[slot, :, tile] = grad_probs
                total += jnp.sum(raised, axis=0, keepdims=True)
                product += jnp.sum(raised * grad_probs, axis=0, keepdims=True)
            own_top = own_stats_ref[head, 0:1, tile]
            highest = jnp.maximum(own_top, top)
            own_factor = jnp.exp2((own_top - highest) * EXPONENT)
            factor = jnp.exp2((top - highest) * EXPONENT)
            inverse = 1.0 / (own_factor * own_stats_ref[head, 1:2, tile] + factor * total)
            own_weight, weight = own_factor * inverse, factor * inverse
            delta = own_weight * own_stats_ref[head, 2:3, tile] + weight * product
            stats_ref[head, 0:1, tile] = own_weight
            stats_ref[head, 1:2, tile] = delta
            for slot in range(TOPK):
                probability = score_ref[slot, :, tile] * weight
                prob_ref[slot, :, tile] = probability.astype(jnp.bfloat16)
                grad_score_ref[slot, :, tile] = (
                    probability * (grad_prob_ref[slot, :, tile] - delta)
                ).astype(jnp.bfloat16)
        query, grad = rows_ref[:, columns], grad_rows_ref[:, columns]
        shape = (chunks, chunk, HEAD_DIM)
        part = None
        for slot in range(TOPK):
            grad_scores = grad_score_ref[slot]
            grad_key = dot(grad_scores, query, 1, 0) * SCALING
            terms_ref[:, 0, slot, :, columns] = grad_key.astype(jnp.bfloat16).reshape(shape)
            grad_value = dot(prob_ref[slot], grad, 1, 0)
            terms_ref[:, 1, slot, :, columns] = grad_value.astype(jnp.bfloat16).reshape(shape)
            product = dot(listed(0, slot).T, grad_scores, 1, 0)
            part = product if part is None else part + product
        part_ref[head] = part
        return carry

    lax.fori_loop(0, heads, one_head, 0)


def own_backward_kernel(
    query_ref,
    key_ref,
    value_ref,
    grad_ref,
    part_ref,
    own_stats_ref,
    stats_ref,
    own_ref,
):
    heads, _, rows = stats_ref.shape
    chunks, _, chunk, _ = own_ref.shape

    def one_head(head, carry):
        columns = head_columns(head)
        query, key = query_ref[:, columns], key_ref[:, columns]
        value, grad = value_ref[:, columns], grad_ref[:, columns]
        scores = causal(dot(key, query, 1, 1), 0)
        raised = jnp.exp2((scores - own_stats_ref[head, 0:1, :]) * EXPONENT)
        probability = raised * stats_ref[head, 0:1, :]
        grad_probs = dot(value, grad, 1, 1)
        grad_scores = (probability * (grad_probs - stats_ref[head, 1:2, :])).astype(jnp.bfloat16)
        results = (
            ((part_ref[head] + dot(key.T, grad_scores, 1, 0)) * SCALING).T,
            dot(grad_scores, query, 1, 0) * SCALING,
            dot(probability.astype(jnp.bfloat16), grad, 1, 0),
        )
        for index, result in enumerate(results):
            own_ref[:, index, :, columns] = result.astype(jnp.bfloat16).reshape(
                chunks, chunk, HEAD_DIM
            )
        return carry

    lax.fori_loop(0, heads, one_head, 0)


def finish_kernel(own_ref, others_ref, out_ref):
    out_ref[:, 0] = own_ref[:, 0]
    out_ref[:, 1:] = (
        others_ref[...].astype(jnp.float32) + own_ref[:, 1:].astype(jnp.float32)
    ).astype(jnp.bfloat16)


def lay_kernel(parts_ref, *refs):
    outs, sem = refs[:-1], refs[-1]
    senders, _, _, width = parts_ref.shape
    copies = [
        pltpu.make_async_copy(
            parts_ref.at[sender, index],
            out.at[:, pl.ds(sender * width, width)],
            sem.at[index, sender],
        )
        for index, out in enumerate(outs)
        for sender in range(senders)
    ]
    for copy in copies:
        copy.start()
    for copy in copies:
        copy.wait()


def on_device(query_input, key_input, value_input, grad_output, selection):
    rows, width = query_input.shape
    heads = width // HEAD_DIM
    chain, spread = lax.axis_size("chain"), lax.axis_size("heads")
    chunk = rows // chain
    share = rows // spread
    listed = selection.reshape(-1)
    position = lax.axis_index("chain").astype(jnp.int32).reshape(1)
    smem = pl.BlockSpec(memory_space=pltpu.SMEM)
    vmem = pl.BlockSpec(memory_space=pltpu.VMEM)
    anywhere = pl.BlockSpec(memory_space=pl.ANY)
    low, full = jnp.bfloat16, jnp.float32

    def swap(array, axis):
        return lax.all_to_all(array, axis, split_axis=0, concat_axis=0, tiled=True)

    def call(kernel, name, in_specs, out_specs, out_shape, scratch=(), limit=4, slots=0):
        flops = 2 * heads * slots * rows * rows * HEAD_DIM
        return pl.pallas_call(
            kernel,
            out_shape=out_shape,
            in_specs=in_specs,
            out_specs=out_specs,
            scratch_shapes=list(scratch),
            cost_estimate=pl.CostEstimate(
                flops=flops, bytes_accessed=4 * MIB, transcendentals=heads * rows * rows
            ),
            compiler_params=pltpu.CompilerParams(vmem_limit_bytes=limit * MIB),
            name=name,
        )

    pair = call(
        stack_kernel,
        "stack",
        [anywhere] * 2,
        anywhere,
        jax.ShapeDtypeStruct((chain, 2, chunk, width), low),
        [
            pltpu.VMEM((2, chain, chunk, width), low),
            pltpu.SemaphoreType.DMA((2, 2)),
            pltpu.SemaphoreType.DMA((2, 2)),
        ],
        limit=59,
    )(key_input.reshape(chain, chunk, width), value_input.reshape(chain, chunk, width))
    held = swap(pair, "chain")
    own_rows, own_stats = call(
        own_forward_kernel,
        "own_forward",
        [anywhere] * 4,
        (vmem, vmem),
        (
            jax.ShapeDtypeStruct((rows, width), low),
            jax.ShapeDtypeStruct((heads, STATS, rows), full),
        ),
        [pltpu.VMEM((3, rows, width), low), pltpu.SemaphoreType.DMA((4,))],
        limit=58,
        slots=2,
    )(query_input, key_input, value_input, grad_output)
    picked = call(
        pick_kernel,
        "pick",
        [smem, vmem],
        anywhere,
        jax.ShapeDtypeStruct((chain, 2, TOPK, chunk, width), low),
        [
            pltpu.VMEM((chain, 2, TOPK, chunk, width), low),
            pltpu.SemaphoreType.DMA((chain,)),
        ],
    )(listed, held)
    slots = swap(picked, "chain")
    terms, part, stats = call(
        far_kernel,
        "far",
        [smem, smem, vmem, anywhere, vmem, vmem],
        (vmem, vmem, vmem),
        (
            jax.ShapeDtypeStruct((chain, 2, TOPK, chunk, width), low),
            jax.ShapeDtypeStruct((heads, HEAD_DIM, rows), full),
            jax.ShapeDtypeStruct((heads, STATS, rows), full),
        ),
        [
            pltpu.VMEM((rows, width), low),
            pltpu.SemaphoreType.DMA(()),
            pltpu.VMEM((TOPK, rows, rows), full),
            pltpu.VMEM((TOPK, rows, rows), full),
            pltpu.VMEM((TOPK, rows, rows), low),
            pltpu.VMEM((TOPK, rows, rows), low),
        ],
        limit=24,
        slots=5 * TOPK,
    )(listed, position, own_rows, grad_output, slots, own_stats)
    returned = swap(terms, "chain")
    own = call(
        own_backward_kernel,
        "own_backward",
        [vmem] * 7,
        vmem,
        jax.ShapeDtypeStruct((chain, 3, chunk, width), low),
        limit=12,
        slots=5,
    )(query_input, key_input, value_input, grad_output, part, own_stats, stats)
    summed = call(
        reduce_kernel,
        "reduce",
        [smem, vmem],
        vmem,
        jax.ShapeDtypeStruct((chain, 2, chunk, width), low),
        [pltpu.VMEM((chain, 2, chunk, HEAD_DIM), full)] * heads,
    )(listed, returned)
    others = swap(summed, "chain")

    def by_share(array):
        lead = array.shape[1:-2]
        array = array.reshape((spread, chain // spread) + lead + (chunk, width))
        return jnp.moveaxis(array, 1, -3).reshape((spread,) + lead + (share, width))

    whole = call(
        finish_kernel,
        "finish",
        [vmem] * 2,
        vmem,
        jax.ShapeDtypeStruct((spread, 3, share, width), low),
    )(by_share(own), by_share(others))
    whole = swap(whole, "heads")
    return call(
        lay_kernel,
        "lay",
        [vmem],
        (anywhere,) * 3,
        (jax.ShapeDtypeStruct((share, spread * width), low),) * 3,
        [pltpu.SemaphoreType.DMA((3, spread))],
    )(whole)


def solution(mesh):
    in_specs = (
        P("chain", "heads"),
        P("chain", "heads"),
        P("chain", "heads"),
        P("chain", "heads"),
        P(None, "heads", None),
    )
    out_specs = (
        P(("chain", "heads"), None),
        P(("chain", "heads"), None),
        P(("chain", "heads"), None),
    )
    return jax.shard_map(
        on_device, mesh=mesh, in_specs=in_specs, out_specs=out_specs, check_vma=False
    )
```

```python
import math

import jax
import jax.numpy as jnp
from jax import lax
from jax.experimental import pallas as pl
from jax.experimental.pallas import tpu as pltpu
from jax.sharding import PartitionSpec as P

HEAD_DIM = 128
TOPK = 3
MASKED = -1e30
SCALING = HEAD_DIM ** (-0.5)
EXPONENT = SCALING * math.log2(math.e)
TILE = 256
STATS = 8
MIB = 1 << 20


def head_columns(head, offset=0):
    start = head * HEAD_DIM + offset
    if isinstance(head, int):
        return pl.ds(start, HEAD_DIM)
    return pl.ds(pl.multiple_of(start, HEAD_DIM), HEAD_DIM)


def dot(left, right, left_dim, right_dim):
    return lax.dot_general(
        left, right, (((left_dim,), (right_dim,)), ((), ())), preferred_element_type=jnp.float32
    )


def stack_kernel(key_ref, value_ref, out_ref, held_ref, in_sem, out_sem):
    pieces = in_sem.shape[1]
    length = key_ref.shape[0] // pieces
    arrive, leave = [], []
    for index, part in enumerate((key_ref, value_ref)):
        for piece in range(pieces):
            span = pl.ds(piece * length, length)
            held = held_ref.at[index, span]
            arrive.append(pltpu.make_async_copy(part.at[span], held, in_sem.at[index, piece]))
            leave.append(
                pltpu.make_async_copy(held, out_ref.at[span, index], out_sem.at[index, piece])
            )
    for copy in arrive:
        copy.start()
    for first, second in zip(arrive, leave):
        first.wait()
        second.start()
    for copy in leave:
        copy.wait()


def pick_kernel(selection_ref, held_ref, out_ref, filled_ref, sem):
    blocks, _, _, width = held_ref.shape
    heads = width // HEAD_DIM
    copies = []
    for block in range(blocks):
        filled_ref[block, :, 0] = held_ref[max(block - 1, 0)]
        for head in range(heads):
            columns = head_columns(head)
            for slot in range(1, TOPK):
                source = selection_ref[(block * heads + head) * TOPK + slot]
                filled_ref[block, :, slot, :, columns] = held_ref[source, :, :, columns]
        copies.append(
            pltpu.make_async_copy(filled_ref.at[block], out_ref.at[block], sem.at[block])
        )
        copies[-1].start()
    for copy in copies:
        copy.wait()


def reduce_kernel(selection_ref, terms_ref, out_ref, *total_refs):
    blocks, _, _, width = out_ref.shape
    heads = width // HEAD_DIM
    for head, total_ref in enumerate(total_refs):
        total_ref[: blocks - 1] = terms_ref[1:, :, 0, :, head_columns(head)].astype(jnp.float32)
        total_ref[blocks - 1] = jnp.zeros_like(total_ref[blocks - 1])
    for block in range(blocks):
        for slot in range(1, TOPK):
            for head, total_ref in enumerate(total_refs):
                target = selection_ref[(block * heads + head) * TOPK + slot]
                total_ref[target] += terms_ref[block, :, slot, :, head_columns(head)].astype(
                    jnp.float32
                )
    for head, total_ref in enumerate(total_refs):
        out_ref[:, :, :, head_columns(head)] = total_ref[...].astype(out_ref.dtype)


def causal(scores, first):
    key_at = lax.broadcasted_iota(jnp.int32, scores.shape, 0)
    query_at = lax.broadcasted_iota(jnp.int32, scores.shape, 1) + first
    return jnp.where(key_at <= query_at, scores, MASKED)


def own_forward_kernel(
    selection_ref,
    query_ref,
    key_ref,
    value_ref,
    grad_ref,
    listed_ref,
    turned_ref,
    stats_ref,
    held_ref,
    sem,
):
    heads, _, rows = stats_ref.shape
    copies = [
        pltpu.make_async_copy(source, held_ref.at[index], sem.at[index])
        for index, source in enumerate((query_ref, grad_ref, key_ref, value_ref))
    ]
    for copy in copies:
        copy.start()

    def hand_on(index, carry):
        listed_ref[index] = selection_ref[index]
        return carry

    lax.fori_loop(0, selection_ref.shape[0], hand_on, 0)
    for copy in copies:
        copy.wait()

    def one_head(head, carry):
        columns = head_columns(head)
        key, value = held_ref[2, :, columns], held_ref[3, :, columns]
        for index in range(2):
            turned_ref[index, head] = held_ref[index, :, columns].T
        for first in range(0, rows, TILE):
            tile = pl.ds(first, TILE)
            scores = causal(dot(key, turned_ref[0, head, :, tile], 1, 0), first)
            top = jnp.max(scores, axis=0, keepdims=True)
            raised = jnp.exp2((scores - top) * EXPONENT)
            product = raised * dot(value, turned_ref[1, head, :, tile], 1, 0)
            stats_ref[head, 0:1, tile] = top
            stats_ref[head, 1:2, tile] = jnp.sum(raised, axis=0, keepdims=True)
            stats_ref[head, 2:3, tile] = jnp.sum(product, axis=0, keepdims=True)
        return carry

    lax.fori_loop(0, heads, one_head, 0)


def far_kernel(
    selection_ref,
    position_ref,
    turned_ref,
    query_ref,
    grad_ref,
    listed_ref,
    own_stats_ref,
    terms_ref,
    part_ref,
    stats_ref,
    rows_ref,
    sem,
    *scratch,
):
    heads, _, rows = own_stats_ref.shape
    chunks, _, _, chunk, _ = listed_ref.shape
    block = position_ref[0]
    copies = [
        pltpu.make_async_copy(source, rows_ref.at[index], sem.at[index])
        for index, source in enumerate((query_ref, grad_ref))
    ]
    for copy in copies:
        copy.start()

    def listed(which, slot, head):
        return listed_ref[:, which, slot, :, head_columns(head)].reshape(rows, HEAD_DIM)

    def softmax(head):
        score_ref, grad_prob_ref, prob_ref, grad_score_ref = scratch[4 * head : 4 * head + 4]
        live = [
            selection_ref[(block * heads + head) * TOPK + slot] < block for slot in range(TOPK)
        ]
        for first in range(0, rows, TILE):
            tile = pl.ds(first, TILE)
            top = jnp.full((1, TILE), MASKED, jnp.float32)
            for slot in range(TOPK):
                scores = dot(listed(0, slot, head), turned_ref[0, head, :, tile], 1, 0)
                score_ref[slot, :, tile] = scores
                highest = jnp.max(scores, axis=0, keepdims=True)
                top = jnp.maximum(top, jnp.where(live[slot], highest, MASKED))
            total = jnp.zeros_like(top)
            product = jnp.zeros_like(top)
            for slot in range(TOPK):
                shift = jnp.where(live[slot], top, -MASKED)
                raised = jnp.exp2((score_ref[slot, :, tile] - shift) * EXPONENT)
                score_ref[slot, :, tile] = raised
                grad_probs = dot(listed(1, slot, head), turned_ref[1, head, :, tile], 1, 0)
                grad_prob_ref[slot, :, tile] = grad_probs
                total += jnp.sum(raised, axis=0, keepdims=True)
                product += jnp.sum(raised * grad_probs, axis=0, keepdims=True)
            own_top = own_stats_ref[head, 0:1, tile]
            highest = jnp.maximum(own_top, top)
            own_factor = jnp.exp2((own_top - highest) * EXPONENT)
            factor = jnp.exp2((top - highest) * EXPONENT)
            inverse = 1.0 / (own_factor * own_stats_ref[head, 1:2, tile] + factor * total)
            own_weight, weight = own_factor * inverse, factor * inverse
            delta = own_weight * own_stats_ref[head, 2:3, tile] + weight * product
            stats_ref[head, 0:1, tile] = own_weight
            stats_ref[head, 1:2, tile] = delta
            for slot in range(TOPK):
                probability = score_ref[slot, :, tile] * weight
                prob_ref[slot, :, tile] = probability.astype(jnp.bfloat16)
                grad_score_ref[slot, :, tile] = (
                    probability * (grad_prob_ref[slot, :, tile] - delta)
                ).astype(jnp.bfloat16)

    def gradients(head):
        _, _, prob_ref, grad_score_ref = scratch[4 * head : 4 * head + 4]
        columns = head_columns(head)
        query, grad = rows_ref[0, :, columns], rows_ref[1, :, columns]
        shape = (chunks, chunk, HEAD_DIM)
        part = None
        for slot in range(TOPK):
            grad_scores = grad_score_ref[slot]
            grad_key = dot(grad_scores, query, 1, 0) * SCALING
            terms_ref[:, 0, slot, :, columns] = grad_key.astype(jnp.bfloat16).reshape(shape)
            grad_value = dot(prob_ref[slot], grad, 1, 0)
            terms_ref[:, 1, slot, :, columns] = grad_value.astype(jnp.bfloat16).reshape(shape)
            product = dot(listed(0, slot, head).T, grad_scores, 1, 0)
            part = product if part is None else part + product
        part_ref[head] = part

    for head in range(heads):
        softmax(head)
        if head == 0:
            for copy in copies:
                copy.wait()
        gradients(head)


def own_backward_kernel(
    query_ref,
    key_ref,
    value_ref,
    grad_ref,
    part_ref,
    own_stats_ref,
    stats_ref,
    own_ref,
):
    heads, _, rows = stats_ref.shape
    chunks, _, chunk, _ = own_ref.shape

    def one_head(head, carry):
        columns = head_columns(head)
        query, key = query_ref[:, columns], key_ref[:, columns]
        value, grad = value_ref[:, columns], grad_ref[:, columns]
        scores = causal(dot(key, query, 1, 1), 0)
        raised = jnp.exp2((scores - own_stats_ref[head, 0:1, :]) * EXPONENT)
        probability = raised * stats_ref[head, 0:1, :]
        grad_probs = dot(value, grad, 1, 1)
        grad_scores = (probability * (grad_probs - stats_ref[head, 1:2, :])).astype(jnp.bfloat16)
        results = (
            ((part_ref[head] + dot(key.T, grad_scores, 1, 0)) * SCALING).T,
            dot(grad_scores, query, 1, 0) * SCALING,
            dot(probability.astype(jnp.bfloat16), grad, 1, 0),
        )
        for index, result in enumerate(results):
            own_ref[:, index, :, columns] = result.astype(jnp.bfloat16).reshape(
                chunks, chunk, HEAD_DIM
            )
        return carry

    lax.fori_loop(0, heads, one_head, 0)


def finish_kernel(own_ref, others_ref, out_ref):
    out_ref[:, 0] = own_ref[:, 0]
    out_ref[:, 1:] = (
        others_ref[...].astype(jnp.float32) + own_ref[:, 1:].astype(jnp.float32)
    ).astype(jnp.bfloat16)


def lay_kernel(parts_ref, *refs):
    outs, sem = refs[:-1], refs[-1]
    senders, _, _, width = parts_ref.shape
    copies = [
        pltpu.make_async_copy(
            parts_ref.at[sender, index],
            out.at[:, pl.ds(sender * width, width)],
            sem.at[index, sender],
        )
        for index, out in enumerate(outs)
        for sender in range(senders)
    ]
    for copy in copies:
        copy.start()
    for copy in copies:
        copy.wait()


def on_device(query_input, key_input, value_input, grad_output, selection):
    rows, width = query_input.shape
    heads = width // HEAD_DIM
    chain, spread = lax.axis_size("chain"), lax.axis_size("heads")
    chunk = rows // chain
    share = rows // spread
    listed = selection.reshape(-1)
    position = lax.axis_index("chain").astype(jnp.int32).reshape(1)
    smem = pl.BlockSpec(memory_space=pltpu.SMEM)
    vmem = pl.BlockSpec(memory_space=pltpu.VMEM)
    anywhere = pl.BlockSpec(memory_space=pl.ANY)
    low, full = jnp.bfloat16, jnp.float32

    def swap(array, axis):
        return lax.all_to_all(array, axis, split_axis=0, concat_axis=0, tiled=True)

    def call(kernel, name, in_specs, out_specs, out_shape, scratch=(), limit=4, slots=0):
        flops = 2 * heads * slots * rows * rows * HEAD_DIM
        return pl.pallas_call(
            kernel,
            out_shape=out_shape,
            in_specs=in_specs,
            out_specs=out_specs,
            scratch_shapes=list(scratch),
            cost_estimate=pl.CostEstimate(
                flops=flops, bytes_accessed=4 * MIB, transcendentals=heads * rows * rows
            ),
            compiler_params=pltpu.CompilerParams(vmem_limit_bytes=limit * MIB),
            name=name,
        )

    pair = call(
        stack_kernel,
        "stack",
        [anywhere] * 2,
        anywhere,
        jax.ShapeDtypeStruct((chain, 2, chunk, width), low),
        [
            pltpu.VMEM((2, chain, chunk, width), low),
            pltpu.SemaphoreType.DMA((2, 2)),
            pltpu.SemaphoreType.DMA((2, 2)),
        ],
        limit=59,
    )(key_input.reshape(chain, chunk, width), value_input.reshape(chain, chunk, width))
    held = swap(pair, "chain")
    listed, turned, own_stats = call(
        own_forward_kernel,
        "own_forward",
        [smem] + [anywhere] * 4,
        (smem, vmem, vmem),
        (
            jax.ShapeDtypeStruct(listed.shape, jnp.int32),
            jax.ShapeDtypeStruct((2, heads, HEAD_DIM, rows), low),
            jax.ShapeDtypeStruct((heads, STATS, rows), full),
        ),
        [pltpu.VMEM((4, rows, width), low), pltpu.SemaphoreType.DMA((4,))],
        limit=58,
        slots=2,
    )(listed, query_input, key_input, value_input, grad_output)
    picked = call(
        pick_kernel,
        "pick",
        [smem, vmem],
        anywhere,
        jax.ShapeDtypeStruct((chain, 2, TOPK, chunk, width), low),
        [
            pltpu.VMEM((chain, 2, TOPK, chunk, width), low),
            pltpu.SemaphoreType.DMA((chain,)),
        ],
    )(listed, held)
    slots = swap(picked, "chain")
    terms, part, stats = call(
        far_kernel,
        "far",
        [smem, smem, vmem, anywhere, anywhere, vmem, vmem],
        (vmem, vmem, vmem),
        (
            jax.ShapeDtypeStruct((chain, 2, TOPK, chunk, width), low),
            jax.ShapeDtypeStruct((heads, HEAD_DIM, rows), full),
            jax.ShapeDtypeStruct((heads, STATS, rows), full),
        ),
        [pltpu.VMEM((2, rows, width), low), pltpu.SemaphoreType.DMA((2,))]
        + [
            pltpu.VMEM((TOPK, rows, rows), full),
            pltpu.VMEM((TOPK, rows, rows), full),
            pltpu.VMEM((TOPK, rows, rows), low),
            pltpu.VMEM((TOPK, rows, rows), low),
        ]
        * heads,
        limit=32,
        slots=5 * TOPK,
    )(listed, position, turned, query_input, grad_output, slots, own_stats)
    returned = swap(terms, "chain")
    own = call(
        own_backward_kernel,
        "own_backward",
        [vmem] * 7,
        vmem,
        jax.ShapeDtypeStruct((chain, 3, chunk, width), low),
        limit=12,
        slots=5,
    )(query_input, key_input, value_input, grad_output, part, own_stats, stats)
    summed = call(
        reduce_kernel,
        "reduce",
        [smem, vmem],
        vmem,
        jax.ShapeDtypeStruct((chain, 2, chunk, width), low),
        [pltpu.VMEM((chain, 2, chunk, HEAD_DIM), full)] * heads,
    )(listed, returned)
    others = swap(summed, "chain")

    def by_share(array):
        lead = array.shape[1:-2]
        array = array.reshape((spread, chain // spread) + lead + (chunk, width))
        return jnp.moveaxis(array, 1, -3).reshape((spread,) + lead + (share, width))

    whole = call(
        finish_kernel,
        "finish",
        [vmem] * 2,
        vmem,
        jax.ShapeDtypeStruct((spread, 3, share, width), low),
    )(by_share(own), by_share(others))
    whole = swap(whole, "heads")
    return call(
        lay_kernel,
        "lay",
        [vmem],
        (anywhere,) * 3,
        (jax.ShapeDtypeStruct((share, spread * width), low),) * 3,
        [pltpu.SemaphoreType.DMA((3, spread))],
    )(whole)


def solution(mesh):
    in_specs = (
        P("chain", "heads"),
        P("chain", "heads"),
        P("chain", "heads"),
        P("chain", "heads"),
        P(None, "heads", None),
    )
    out_specs = (
        P(("chain", "heads"), None),
        P(("chain", "heads"), None),
        P(("chain", "heads"), None),
    )
    return jax.shard_map(
        on_device, mesh=mesh, in_specs=in_specs, out_specs=out_specs, check_vma=False
    )
```

```python
import math

import jax
import jax.numpy as jnp
from jax import lax
from jax.experimental import pallas as pl
from jax.experimental.pallas import tpu as pltpu
from jax.sharding import PartitionSpec as P

HEAD_DIM = 128
TOPK = 3
MASKED = -1e30
SCALING = HEAD_DIM ** (-0.5)
EXPONENT = SCALING * math.log2(math.e)
TILE = 256
STATS = 8
SUBLANES = 8
MIB = 1 << 20


def head_columns(head, offset=0):
    start = head * HEAD_DIM + offset
    if isinstance(head, int):
        return pl.ds(start, HEAD_DIM)
    return pl.ds(pl.multiple_of(start, HEAD_DIM), HEAD_DIM)


def dot(left, right, left_dim, right_dim):
    return lax.dot_general(
        left, right, (((left_dim,), (right_dim,)), ((), ())), preferred_element_type=jnp.float32
    )


def stack_kernel(key_ref, value_ref, out_ref, held_ref, in_sem, out_sem):
    pieces = in_sem.shape[1]
    length = key_ref.shape[0] // pieces
    arrive, leave = [], []
    for index, part in enumerate((key_ref, value_ref)):
        for piece in range(pieces):
            span = pl.ds(piece * length, length)
            held = held_ref.at[index, span]
            arrive.append(pltpu.make_async_copy(part.at[span], held, in_sem.at[index, piece]))
            leave.append(
                pltpu.make_async_copy(held, out_ref.at[span, index], out_sem.at[index, piece])
            )
    for copy in arrive:
        copy.start()
    for first, second in zip(arrive, leave):
        first.wait()
        second.start()
    for copy in leave:
        copy.wait()


def pick_kernel(selection_ref, held_ref, out_ref, filled_ref, sem):
    blocks, _, _, width = held_ref.shape
    heads = width // HEAD_DIM
    copies = []
    for block in range(blocks):
        filled_ref[block, :, 0] = held_ref[max(block - 1, 0)]
        for head in range(heads):
            columns = head_columns(head)
            for slot in range(1, TOPK):
                source = selection_ref[(block * heads + head) * TOPK + slot]
                filled_ref[block, :, slot, :, columns] = held_ref[source, :, :, columns]
        copies.append(
            pltpu.make_async_copy(filled_ref.at[block], out_ref.at[block], sem.at[block])
        )
        copies[-1].start()
    for copy in copies:
        copy.wait()


def reduce_kernel(selection_ref, terms_ref, out_ref, *total_refs):
    blocks, _, _, width = out_ref.shape
    heads = width // HEAD_DIM
    for head, total_ref in enumerate(total_refs):
        total_ref[: blocks - 1] = terms_ref[1:, :, 0, :, head_columns(head)].astype(jnp.float32)
        total_ref[blocks - 1] = jnp.zeros_like(total_ref[blocks - 1])
    for block in range(blocks):
        for slot in range(1, TOPK):
            for head, total_ref in enumerate(total_refs):
                target = selection_ref[(block * heads + head) * TOPK + slot]
                total_ref[target] += terms_ref[block, :, slot, :, head_columns(head)].astype(
                    jnp.float32
                )
    for head, total_ref in enumerate(total_refs):
        out_ref[:, :, :, head_columns(head)] = total_ref[...].astype(out_ref.dtype)


def fold(array):
    return jnp.sum(array.reshape(-1, SUBLANES, array.shape[1]), axis=0)


def causal(scores, first):
    key_at = lax.broadcasted_iota(jnp.int32, scores.shape, 0)
    query_at = lax.broadcasted_iota(jnp.int32, scores.shape, 1) + first
    return jnp.where(key_at <= query_at, scores, MASKED)


def own_forward_kernel(
    selection_ref,
    query_ref,
    key_ref,
    value_ref,
    grad_ref,
    listed_ref,
    turned_ref,
    stats_ref,
    held_ref,
    sem,
):
    heads, _, rows = stats_ref.shape
    copies = [
        pltpu.make_async_copy(source, held_ref.at[index], sem.at[index])
        for index, source in enumerate((query_ref, grad_ref, key_ref, value_ref))
    ]
    for copy in copies:
        copy.start()

    def hand_on(index, carry):
        listed_ref[index] = selection_ref[index]
        return carry

    lax.fori_loop(0, selection_ref.shape[0], hand_on, 0)
    for copy in copies:
        copy.wait()

    def one_head(head, carry):
        columns = head_columns(head)
        key, value = held_ref[2, :, columns], held_ref[3, :, columns]
        for index in range(2):
            turned_ref[index, head] = held_ref[index, :, columns].T
        for first in range(0, rows, TILE):
            tile = pl.ds(first, TILE)
            scores = causal(dot(key, turned_ref[0, head, :, tile], 1, 0), first)
            top = jnp.max(scores, axis=0, keepdims=True)
            raised = jnp.exp2((scores - top) * EXPONENT)
            product = raised * dot(value, turned_ref[1, head, :, tile], 1, 0)
            stats_ref[head, 0:1, tile] = top
            stats_ref[head, 1:2, tile] = jnp.sum(raised, axis=0, keepdims=True)
            stats_ref[head, 2:3, tile] = jnp.sum(product, axis=0, keepdims=True)
        return carry

    lax.fori_loop(0, heads, one_head, 0)


def far_kernel(
    selection_ref,
    position_ref,
    turned_ref,
    query_ref,
    grad_ref,
    listed_ref,
    own_stats_ref,
    terms_ref,
    part_ref,
    stats_ref,
    rows_ref,
    sem,
    *scratch,
):
    heads, _, rows = own_stats_ref.shape
    chunks, _, _, chunk, _ = listed_ref.shape
    block = position_ref[0]
    copies = [
        pltpu.make_async_copy(source, rows_ref.at[index], sem.at[index])
        for index, source in enumerate((query_ref, grad_ref))
    ]
    for copy in copies:
        copy.start()

    def listed(which, head):
        return listed_ref[:, which, :, :, head_columns(head)].reshape(TOPK * rows, HEAD_DIM)

    def softmax(head):
        score_ref, grad_prob_ref, prob_ref, grad_score_ref = scratch[4 * head : 4 * head + 4]
        live = [
            selection_ref[(block * heads + head) * TOPK + slot] < block for slot in range(TOPK)
        ]
        shape = (chunks, TOPK, chunk, TILE)
        for first in range(0, rows, TILE):
            tile = pl.ds(first, TILE)
            scores = dot(listed(0, head), turned_ref[0, head, :, tile], 1, 0)
            score_ref[:, :, :, tile] = scores.reshape(shape)
            grad_probs = dot(listed(1, head), turned_ref[1, head, :, tile], 1, 0)
            grad_prob_ref[:, :, :, tile] = grad_probs.reshape(shape)
            top = jnp.full((1, TILE), MASKED, jnp.float32)
            for slot in range(TOPK):
                highest = jnp.max(
                    score_ref[:, slot, :, tile].reshape(rows, TILE), axis=0, keepdims=True
                )
                top = jnp.maximum(top, jnp.where(live[slot], highest, MASKED))
            total = jnp.zeros((SUBLANES, TILE), jnp.float32)
            product = jnp.zeros_like(total)
            for slot in range(TOPK):
                shift = jnp.where(live[slot], top, -MASKED)
                for part in range(chunks):
                    raised = jnp.exp2((score_ref[part, slot, :, tile] - shift) * EXPONENT)
                    score_ref[part, slot, :, tile] = raised
                    total += fold(raised)
                    product += fold(raised * grad_prob_ref[part, slot, :, tile])
            total = jnp.sum(total, axis=0, keepdims=True)
            product = jnp.sum(product, axis=0, keepdims=True)
            own_top = own_stats_ref[head, 0:1, tile]
            highest = jnp.maximum(own_top, top)
            own_factor = jnp.exp2((own_top - highest) * EXPONENT)
            factor = jnp.exp2((top - highest) * EXPONENT)
            inverse = 1.0 / (own_factor * own_stats_ref[head, 1:2, tile] + factor * total)
            own_weight, weight = own_factor * inverse, factor * inverse
            delta = own_weight * own_stats_ref[head, 2:3, tile] + weight * product
            stats_ref[head, 0:1, tile] = own_weight
            stats_ref[head, 1:2, tile] = delta
            for slot in range(TOPK):
                for part in range(chunks):
                    probability = score_ref[part, slot, :, tile] * weight
                    prob_ref[part, slot, :, tile] = probability.astype(jnp.bfloat16)
                    grad_score_ref[part, slot, :, tile] = (
                        probability * (grad_prob_ref[part, slot, :, tile] - delta)
                    ).astype(jnp.bfloat16)

    def gradients(head):
        _, _, prob_ref, grad_score_ref = scratch[4 * head : 4 * head + 4]
        columns = head_columns(head)
        query, grad = rows_ref[0, :, columns], rows_ref[1, :, columns]
        shape = (chunks, TOPK, chunk, HEAD_DIM)
        prob = prob_ref[...].reshape(TOPK * rows, rows)
        grad_scores = grad_score_ref[...].reshape(TOPK * rows, rows)
        grad_key = dot(grad_scores, query, 1, 0) * SCALING
        terms_ref[:, 0, :, :, columns] = grad_key.astype(jnp.bfloat16).reshape(shape)
        grad_value = dot(prob, grad, 1, 0)
        terms_ref[:, 1, :, :, columns] = grad_value.astype(jnp.bfloat16).reshape(shape)
        part_ref[head] = dot(listed(0, head).T, grad_scores, 1, 0)

    for head in range(heads):
        softmax(head)
        if head == 0:
            for copy in copies:
                copy.wait()
        gradients(head)


def own_backward_kernel(
    query_ref,
    key_ref,
    value_ref,
    grad_ref,
    part_ref,
    own_stats_ref,
    stats_ref,
    own_ref,
):
    heads, _, rows = stats_ref.shape
    chunks, _, chunk, _ = own_ref.shape

    def one_head(head, carry):
        columns = head_columns(head)
        query, key = query_ref[:, columns], key_ref[:, columns]
        value, grad = value_ref[:, columns], grad_ref[:, columns]
        scores = causal(dot(key, query, 1, 1), 0)
        raised = jnp.exp2((scores - own_stats_ref[head, 0:1, :]) * EXPONENT)
        probability = raised * stats_ref[head, 0:1, :]
        grad_probs = dot(value, grad, 1, 1)
        grad_scores = (probability * (grad_probs - stats_ref[head, 1:2, :])).astype(jnp.bfloat16)
        results = (
            ((part_ref[head] + dot(key.T, grad_scores, 1, 0)) * SCALING).T,
            dot(grad_scores, query, 1, 0) * SCALING,
            dot(probability.astype(jnp.bfloat16), grad, 1, 0),
        )
        for index, result in enumerate(results):
            own_ref[:, index, :, columns] = result.astype(jnp.bfloat16).reshape(
                chunks, chunk, HEAD_DIM
            )
        return carry

    lax.fori_loop(0, heads, one_head, 0)


def finish_kernel(own_ref, others_ref, out_ref):
    out_ref[:, 0] = own_ref[:, 0]
    out_ref[:, 1:] = (
        others_ref[...].astype(jnp.float32) + own_ref[:, 1:].astype(jnp.float32)
    ).astype(jnp.bfloat16)


def lay_kernel(parts_ref, *refs):
    outs, sem = refs[:-1], refs[-1]
    senders, _, _, width = parts_ref.shape
    copies = [
        pltpu.make_async_copy(
            parts_ref.at[sender, index],
            out.at[:, pl.ds(sender * width, width)],
            sem.at[index, sender],
        )
        for index, out in enumerate(outs)
        for sender in range(senders)
    ]
    for copy in copies:
        copy.start()
    for copy in copies:
        copy.wait()


def on_device(query_input, key_input, value_input, grad_output, selection):
    rows, width = query_input.shape
    heads = width // HEAD_DIM
    chain, spread = lax.axis_size("chain"), lax.axis_size("heads")
    chunk = rows // chain
    share = rows // spread
    listed = selection.reshape(-1)
    position = lax.axis_index("chain").astype(jnp.int32).reshape(1)
    smem = pl.BlockSpec(memory_space=pltpu.SMEM)
    vmem = pl.BlockSpec(memory_space=pltpu.VMEM)
    anywhere = pl.BlockSpec(memory_space=pl.ANY)
    low, full = jnp.bfloat16, jnp.float32

    def swap(array, axis):
        return lax.all_to_all(array, axis, split_axis=0, concat_axis=0, tiled=True)

    def call(kernel, name, in_specs, out_specs, out_shape, scratch=(), limit=4, slots=0):
        flops = 2 * heads * slots * rows * rows * HEAD_DIM
        return pl.pallas_call(
            kernel,
            out_shape=out_shape,
            in_specs=in_specs,
            out_specs=out_specs,
            scratch_shapes=list(scratch),
            cost_estimate=pl.CostEstimate(
                flops=flops, bytes_accessed=4 * MIB, transcendentals=heads * rows * rows
            ),
            compiler_params=pltpu.CompilerParams(vmem_limit_bytes=limit * MIB),
            name=name,
        )

    pair = call(
        stack_kernel,
        "stack",
        [anywhere] * 2,
        anywhere,
        jax.ShapeDtypeStruct((chain, 2, chunk, width), low),
        [
            pltpu.VMEM((2, chain, chunk, width), low),
            pltpu.SemaphoreType.DMA((2, 2)),
            pltpu.SemaphoreType.DMA((2, 2)),
        ],
        limit=59,
    )(key_input.reshape(chain, chunk, width), value_input.reshape(chain, chunk, width))
    held = swap(pair, "chain")
    listed, turned, own_stats = call(
        own_forward_kernel,
        "own_forward",
        [smem] + [anywhere] * 4,
        (smem, vmem, vmem),
        (
            jax.ShapeDtypeStruct(listed.shape, jnp.int32),
            jax.ShapeDtypeStruct((2, heads, HEAD_DIM, rows), low),
            jax.ShapeDtypeStruct((heads, STATS, rows), full),
        ),
        [pltpu.VMEM((4, rows, width), low), pltpu.SemaphoreType.DMA((4,))],
        limit=16,
        slots=2,
    )(listed, query_input, key_input, value_input, grad_output)
    picked = call(
        pick_kernel,
        "pick",
        [smem, vmem],
        anywhere,
        jax.ShapeDtypeStruct((chain, 2, TOPK, chunk, width), low),
        [
            pltpu.VMEM((chain, 2, TOPK, chunk, width), low),
            pltpu.SemaphoreType.DMA((chain,)),
        ],
    )(listed, held)
    slots = swap(picked, "chain")
    terms, part, stats = call(
        far_kernel,
        "far",
        [smem, smem, vmem, anywhere, anywhere, vmem, vmem],
        (vmem, vmem, vmem),
        (
            jax.ShapeDtypeStruct((chain, 2, TOPK, chunk, width), low),
            jax.ShapeDtypeStruct((heads, HEAD_DIM, rows), full),
            jax.ShapeDtypeStruct((heads, STATS, rows), full),
        ),
        [pltpu.VMEM((2, rows, width), low), pltpu.SemaphoreType.DMA((2,))]
        + [
            pltpu.VMEM((chain, TOPK, chunk, rows), full),
            pltpu.VMEM((chain, TOPK, chunk, rows), full),
            pltpu.VMEM((chain, TOPK, chunk, rows), low),
            pltpu.VMEM((chain, TOPK, chunk, rows), low),
        ]
        * heads,
        limit=32,
        slots=5 * TOPK,
    )(listed, position, turned, query_input, grad_output, slots, own_stats)
    returned = swap(terms, "chain")
    own = call(
        own_backward_kernel,
        "own_backward",
        [vmem] * 7,
        vmem,
        jax.ShapeDtypeStruct((chain, 3, chunk, width), low),
        limit=12,
        slots=5,
    )(query_input, key_input, value_input, grad_output, part, own_stats, stats)
    summed = call(
        reduce_kernel,
        "reduce",
        [smem, vmem],
        vmem,
        jax.ShapeDtypeStruct((chain, 2, chunk, width), low),
        [pltpu.VMEM((chain, 2, chunk, HEAD_DIM), full)] * heads,
    )(listed, returned)
    others = swap(summed, "chain")

    def by_share(array):
        lead = array.shape[1:-2]
        array = array.reshape((spread, chain // spread) + lead + (chunk, width))
        return jnp.moveaxis(array, 1, -3).reshape((spread,) + lead + (share, width))

    whole = call(
        finish_kernel,
        "finish",
        [vmem] * 2,
        vmem,
        jax.ShapeDtypeStruct((spread, 3, share, width), low),
    )(by_share(own), by_share(others))
    whole = swap(whole, "heads")
    return call(
        lay_kernel,
        "lay",
        [vmem],
        (anywhere,) * 3,
        (jax.ShapeDtypeStruct((share, spread * width), low),) * 3,
        [pltpu.SemaphoreType.DMA((3, spread))],
    )(whole)


def solution(mesh):
    in_specs = (
        P("chain", "heads"),
        P("chain", "heads"),
        P("chain", "heads"),
        P("chain", "heads"),
        P(None, "heads", None),
    )
    out_specs = (
        P(("chain", "heads"), None),
        P(("chain", "heads"), None),
        P(("chain", "heads"), None),
    )
    return jax.shard_map(
        on_device, mesh=mesh, in_specs=in_specs, out_specs=out_specs, check_vma=False
    )
```

```python
import math

import jax
import jax.numpy as jnp
from jax import lax
from jax.experimental import pallas as pl
from jax.experimental.pallas import tpu as pltpu
from jax.sharding import PartitionSpec as P

HEAD_DIM = 128
TOPK = 3
MASKED = -1e30
SCALING = HEAD_DIM ** (-0.5)
EXPONENT = SCALING * math.log2(math.e)
TILE = 256
STATS = 8
SUBLANES = 8
MIB = 1 << 20


def head_columns(head, offset=0):
    start = head * HEAD_DIM + offset
    if isinstance(head, int):
        return pl.ds(start, HEAD_DIM)
    return pl.ds(pl.multiple_of(start, HEAD_DIM), HEAD_DIM)


def dot(left, right, left_dim, right_dim):
    return lax.dot_general(
        left, right, (((left_dim,), (right_dim,)), ((), ())), preferred_element_type=jnp.float32
    )


def stack_kernel(key_ref, value_ref, out_ref, held_ref, in_sem, out_sem):
    pieces = in_sem.shape[1]
    length = key_ref.shape[0] // pieces
    arrive, leave = [], []
    for index, part in enumerate((key_ref, value_ref)):
        for piece in range(pieces):
            span = pl.ds(piece * length, length)
            held = held_ref.at[index, span]
            arrive.append(pltpu.make_async_copy(part.at[span], held, in_sem.at[index, piece]))
            leave.append(
                pltpu.make_async_copy(held, out_ref.at[span, index], out_sem.at[index, piece])
            )
    for copy in arrive:
        copy.start()
    for first, second in zip(arrive, leave):
        first.wait()
        second.start()
    for copy in leave:
        copy.wait()


def pick_kernel(selection_ref, held_ref, out_ref, filled_ref, sem):
    blocks, _, _, width = held_ref.shape
    heads = width // HEAD_DIM
    copies = []
    for block in range(blocks):
        filled_ref[block, :, 0] = held_ref[max(block - 1, 0)]
        for head in range(heads):
            columns = head_columns(head)
            for slot in range(1, TOPK):
                source = selection_ref[(block * heads + head) * TOPK + slot]
                filled_ref[block, :, slot, :, columns] = held_ref[source, :, :, columns]
        copies.append(
            pltpu.make_async_copy(filled_ref.at[block], out_ref.at[block], sem.at[block])
        )
        copies[-1].start()
    for copy in copies:
        copy.wait()


def reduce_kernel(selection_ref, terms_ref, out_ref, *total_refs):
    blocks, _, _, width = out_ref.shape
    heads = width // HEAD_DIM
    for head, total_ref in enumerate(total_refs):
        total_ref[: blocks - 1] = terms_ref[1:, :, 0, :, head_columns(head)].astype(jnp.float32)
        total_ref[blocks - 1] = jnp.zeros_like(total_ref[blocks - 1])
    for block in range(blocks):
        for slot in range(1, TOPK):
            for head, total_ref in enumerate(total_refs):
                target = selection_ref[(block * heads + head) * TOPK + slot]
                total_ref[target] += terms_ref[block, :, slot, :, head_columns(head)].astype(
                    jnp.float32
                )
    for head, total_ref in enumerate(total_refs):
        out_ref[:, :, :, head_columns(head)] = total_ref[...].astype(out_ref.dtype)


def fold(array):
    return jnp.sum(array.reshape(-1, SUBLANES, array.shape[1]), axis=0)


def causal(scores, first):
    key_at = lax.broadcasted_iota(jnp.int32, scores.shape, 0)
    query_at = lax.broadcasted_iota(jnp.int32, scores.shape, 1) + first
    return jnp.where(key_at <= query_at, scores, MASKED)


def own_forward_kernel(
    selection_ref,
    query_ref,
    key_ref,
    value_ref,
    grad_ref,
    listed_ref,
    turned_ref,
    stats_ref,
    held_ref,
    sem,
):
    heads, _, rows = stats_ref.shape
    copies = [
        pltpu.make_async_copy(source, held_ref.at[index], sem.at[index])
        for index, source in enumerate((query_ref, grad_ref, key_ref, value_ref))
    ]
    for copy in copies:
        copy.start()

    def hand_on(index, carry):
        listed_ref[index] = selection_ref[index]
        return carry

    lax.fori_loop(0, selection_ref.shape[0], hand_on, 0)
    for copy in copies:
        copy.wait()

    def one_head(head, carry):
        columns = head_columns(head)
        key, value = held_ref[2, :, columns], held_ref[3, :, columns]
        for index in range(2):
            turned_ref[index, head] = held_ref[index, :, columns].T
        for first in range(0, rows, TILE):
            tile = pl.ds(first, TILE)
            scores = causal(dot(key, turned_ref[0, head, :, tile], 1, 0), first)
            top = jnp.max(scores, axis=0, keepdims=True)
            raised = jnp.exp2((scores - top) * EXPONENT)
            product = raised * dot(value, turned_ref[1, head, :, tile], 1, 0)
            stats_ref[head, 0:1, tile] = top
            stats_ref[head, 1:2, tile] = jnp.sum(raised, axis=0, keepdims=True)
            stats_ref[head, 2:3, tile] = jnp.sum(product, axis=0, keepdims=True)
        return carry

    lax.fori_loop(0, heads, one_head, 0)


def far_kernel(
    selection_ref,
    position_ref,
    turned_ref,
    query_ref,
    grad_ref,
    listed_ref,
    own_stats_ref,
    terms_ref,
    stats_ref,
    rows_ref,
    sem,
    *scratch,
):
    heads, _, rows = own_stats_ref.shape
    chunks, _, _, chunk, _ = listed_ref.shape
    block = position_ref[0]
    copies = [
        pltpu.make_async_copy(source, rows_ref.at[index], sem.at[index])
        for index, source in enumerate((query_ref, grad_ref))
    ]
    for copy in copies:
        copy.start()

    def listed(which, head):
        return listed_ref[:, which, :, :, head_columns(head)].reshape(TOPK * rows, HEAD_DIM)

    def softmax(head):
        score_ref, grad_prob_ref, prob_ref, grad_score_ref = scratch[4 * head : 4 * head + 4]
        live = [
            selection_ref[(block * heads + head) * TOPK + slot] < block for slot in range(TOPK)
        ]
        shape = (chunks, TOPK, chunk, TILE)
        for first in range(0, rows, TILE):
            tile = pl.ds(first, TILE)
            scores = dot(listed(0, head), turned_ref[0, head, :, tile], 1, 0)
            score_ref[:, :, :, tile] = scores.reshape(shape)
            grad_probs = dot(listed(1, head), turned_ref[1, head, :, tile], 1, 0)
            grad_prob_ref[:, :, :, tile] = grad_probs.reshape(shape)
            top = jnp.full((1, TILE), MASKED, jnp.float32)
            for slot in range(TOPK):
                highest = jnp.max(
                    score_ref[:, slot, :, tile].reshape(rows, TILE), axis=0, keepdims=True
                )
                top = jnp.maximum(top, jnp.where(live[slot], highest, MASKED))
            total = jnp.zeros((SUBLANES, TILE), jnp.float32)
            product = jnp.zeros_like(total)
            for slot in range(TOPK):
                shift = jnp.where(live[slot], top, -MASKED)
                for part in range(chunks):
                    raised = jnp.exp2((score_ref[part, slot, :, tile] - shift) * EXPONENT)
                    score_ref[part, slot, :, tile] = raised
                    total += fold(raised)
                    product += fold(raised * grad_prob_ref[part, slot, :, tile])
            total = jnp.sum(total, axis=0, keepdims=True)
            product = jnp.sum(product, axis=0, keepdims=True)
            own_top = own_stats_ref[head, 0:1, tile]
            highest = jnp.maximum(own_top, top)
            own_factor = jnp.exp2((own_top - highest) * EXPONENT)
            factor = jnp.exp2((top - highest) * EXPONENT)
            inverse = 1.0 / (own_factor * own_stats_ref[head, 1:2, tile] + factor * total)
            weight = factor * inverse
            delta = own_factor * inverse * own_stats_ref[head, 2:3, tile] + weight * product
            stats_ref[head, 0:1, tile] = highest
            stats_ref[head, 1:2, tile] = inverse
            stats_ref[head, 2:3, tile] = delta
            for slot in range(TOPK):
                for part in range(chunks):
                    probability = score_ref[part, slot, :, tile] * weight
                    prob_ref[part, slot, :, tile] = probability.astype(jnp.bfloat16)
                    grad_score_ref[part, slot, :, tile] = (
                        probability * (grad_prob_ref[part, slot, :, tile] - delta)
                    ).astype(jnp.bfloat16)

    def gradients(head):
        _, _, prob_ref, grad_score_ref = scratch[4 * head : 4 * head + 4]
        columns = head_columns(head)
        query, grad = rows_ref[0, :, columns], rows_ref[1, :, columns]
        shape = (chunks, TOPK, chunk, HEAD_DIM)
        prob = prob_ref[...].reshape(TOPK * rows, rows)
        grad_scores = grad_score_ref[...].reshape(TOPK * rows, rows)
        grad_key = dot(grad_scores, query, 1, 0) * SCALING
        terms_ref[:, 0, :, :, columns] = grad_key.astype(jnp.bfloat16).reshape(shape)
        grad_value = dot(prob, grad, 1, 0)
        terms_ref[:, 1, :, :, columns] = grad_value.astype(jnp.bfloat16).reshape(shape)

    for head in range(heads):
        softmax(head)
        if head == 0:
            for copy in copies:
                copy.wait()
        gradients(head)


def own_backward_kernel(
    selection_ref,
    position_ref,
    query_ref,
    key_ref,
    value_ref,
    grad_ref,
    listed_ref,
    stats_ref,
    own_ref,
):
    heads, _, rows = stats_ref.shape
    chunks, _, chunk, _ = own_ref.shape
    block = position_ref[0]

    def one_head(head, carry):
        columns = head_columns(head)
        query, grad = query_ref[:, columns], grad_ref[:, columns]
        highest, inverse = stats_ref[head, 0:1, :], stats_ref[head, 1:2, :]
        delta = stats_ref[head, 2:3, :]

        def scores_and_grads(scores, shift, value):
            probability = jnp.exp2((scores - shift) * EXPONENT) * inverse
            grad_probs = dot(value, grad, 1, 1)
            return probability, (probability * (grad_probs - delta)).astype(jnp.bfloat16)

        key = key_ref[:, columns]
        probability, grad_scores = scores_and_grads(
            causal(dot(key, query, 1, 1), 0), highest, value_ref[:, columns]
        )
        total = dot(key.T, grad_scores, 1, 0)
        grad_key = dot(grad_scores, query, 1, 0) * SCALING
        grad_value = dot(probability.astype(jnp.bfloat16), grad, 1, 0)
        for slot in range(TOPK):
            live = selection_ref[(block * heads + head) * TOPK + slot] < block
            shift = jnp.where(live, highest, -MASKED)
            key, value = (
                listed_ref[:, which, slot, :, columns].reshape(rows, HEAD_DIM)
                for which in range(2)
            )
            _, grad_scores = scores_and_grads(dot(key, query, 1, 1), shift, value)
            total += dot(key.T, grad_scores, 1, 0)
        for index, result in enumerate(((total * SCALING).T, grad_key, grad_value)):
            own_ref[:, index, :, columns] = result.astype(jnp.bfloat16).reshape(
                chunks, chunk, HEAD_DIM
            )
        return carry

    lax.fori_loop(0, heads, one_head, 0)


def finish_kernel(own_ref, others_ref, out_ref):
    out_ref[:, 0] = own_ref[:, 0]
    out_ref[:, 1:] = (
        others_ref[...].astype(jnp.float32) + own_ref[:, 1:].astype(jnp.float32)
    ).astype(jnp.bfloat16)


def lay_kernel(parts_ref, *refs):
    outs, sem = refs[:-1], refs[-1]
    senders, _, _, width = parts_ref.shape
    copies = [
        pltpu.make_async_copy(
            parts_ref.at[sender, index],
            out.at[:, pl.ds(sender * width, width)],
            sem.at[index, sender],
        )
        for index, out in enumerate(outs)
        for sender in range(senders)
    ]
    for copy in copies:
        copy.start()
    for copy in copies:
        copy.wait()


def on_device(query_input, key_input, value_input, grad_output, selection):
    rows, width = query_input.shape
    heads = width // HEAD_DIM
    chain, spread = lax.axis_size("chain"), lax.axis_size("heads")
    chunk = rows // chain
    share = rows // spread
    listed = selection.reshape(-1)
    position = lax.axis_index("chain").astype(jnp.int32).reshape(1)
    smem = pl.BlockSpec(memory_space=pltpu.SMEM)
    vmem = pl.BlockSpec(memory_space=pltpu.VMEM)
    anywhere = pl.BlockSpec(memory_space=pl.ANY)
    low, full = jnp.bfloat16, jnp.float32

    def swap(array, axis):
        return lax.all_to_all(array, axis, split_axis=0, concat_axis=0, tiled=True)

    def call(kernel, name, in_specs, out_specs, out_shape, scratch=(), limit=4, slots=0):
        flops = 2 * heads * slots * rows * rows * HEAD_DIM
        return pl.pallas_call(
            kernel,
            out_shape=out_shape,
            in_specs=in_specs,
            out_specs=out_specs,
            scratch_shapes=list(scratch),
            cost_estimate=pl.CostEstimate(
                flops=flops, bytes_accessed=4 * MIB, transcendentals=heads * rows * rows
            ),
            compiler_params=pltpu.CompilerParams(vmem_limit_bytes=limit * MIB),
            name=name,
        )

    pair = call(
        stack_kernel,
        "stack",
        [anywhere] * 2,
        anywhere,
        jax.ShapeDtypeStruct((chain, 2, chunk, width), low),
        [
            pltpu.VMEM((2, chain, chunk, width), low),
            pltpu.SemaphoreType.DMA((2, 2)),
            pltpu.SemaphoreType.DMA((2, 2)),
        ],
        limit=59,
    )(key_input.reshape(chain, chunk, width), value_input.reshape(chain, chunk, width))
    held = swap(pair, "chain")
    listed, turned, own_stats = call(
        own_forward_kernel,
        "own_forward",
        [smem] + [anywhere] * 4,
        (smem, vmem, vmem),
        (
            jax.ShapeDtypeStruct(listed.shape, jnp.int32),
            jax.ShapeDtypeStruct((2, heads, HEAD_DIM, rows), low),
            jax.ShapeDtypeStruct((heads, STATS, rows), full),
        ),
        [pltpu.VMEM((4, rows, width), low), pltpu.SemaphoreType.DMA((4,))],
        limit=16,
        slots=2,
    )(listed, query_input, key_input, value_input, grad_output)
    picked = call(
        pick_kernel,
        "pick",
        [smem, vmem],
        anywhere,
        jax.ShapeDtypeStruct((chain, 2, TOPK, chunk, width), low),
        [
            pltpu.VMEM((chain, 2, TOPK, chunk, width), low),
            pltpu.SemaphoreType.DMA((chain,)),
        ],
    )(listed, held)
    slots = swap(picked, "chain")
    terms, stats = call(
        far_kernel,
        "far",
        [smem, smem, vmem, anywhere, anywhere, vmem, vmem],
        (vmem, vmem),
        (
            jax.ShapeDtypeStruct((chain, 2, TOPK, chunk, width), low),
            jax.ShapeDtypeStruct((heads, STATS, rows), full),
        ),
        [pltpu.VMEM((2, rows, width), low), pltpu.SemaphoreType.DMA((2,))]
        + [
            pltpu.VMEM((chain, TOPK, chunk, rows), full),
            pltpu.VMEM((chain, TOPK, chunk, rows), full),
            pltpu.VMEM((chain, TOPK, chunk, rows), low),
            pltpu.VMEM((chain, TOPK, chunk, rows), low),
        ]
        * heads,
        limit=32,
        slots=4 * TOPK,
    )(listed, position, turned, query_input, grad_output, slots, own_stats)
    returned = swap(terms, "chain")
    own = call(
        own_backward_kernel,
        "own_backward",
        [smem] * 2 + [vmem] * 6,
        vmem,
        jax.ShapeDtypeStruct((chain, 3, chunk, width), low),
        limit=12,
        slots=5 + 3 * TOPK,
    )(listed, position, query_input, key_input, value_input, grad_output, slots, stats)
    summed = call(
        reduce_kernel,
        "reduce",
        [smem, vmem],
        vmem,
        jax.ShapeDtypeStruct((chain, 2, chunk, width), low),
        [pltpu.VMEM((chain, 2, chunk, HEAD_DIM), full)] * heads,
    )(listed, returned)
    others = swap(summed, "chain")

    def by_share(array):
        lead = array.shape[1:-2]
        array = array.reshape((spread, chain // spread) + lead + (chunk, width))
        return jnp.moveaxis(array, 1, -3).reshape((spread,) + lead + (share, width))

    whole = call(
        finish_kernel,
        "finish",
        [vmem] * 2,
        vmem,
        jax.ShapeDtypeStruct((spread, 3, share, width), low),
    )(by_share(own), by_share(others))
    whole = swap(whole, "heads")
    return call(
        lay_kernel,
        "lay",
        [vmem],
        (anywhere,) * 3,
        (jax.ShapeDtypeStruct((share, spread * width), low),) * 3,
        [pltpu.SemaphoreType.DMA((3, spread))],
    )(whole)


def solution(mesh):
    in_specs = (
        P("chain", "heads"),
        P("chain", "heads"),
        P("chain", "heads"),
        P("chain", "heads"),
        P(None, "heads", None),
    )
    out_specs = (
        P(("chain", "heads"), None),
        P(("chain", "heads"), None),
        P(("chain", "heads"), None),
    )
    return jax.shard_map(
        on_device, mesh=mesh, in_specs=in_specs, out_specs=out_specs, check_vma=False
    )
```

```python
import math

import jax
import jax.numpy as jnp
from jax import lax
from jax.experimental import pallas as pl
from jax.experimental.pallas import tpu as pltpu
from jax.sharding import PartitionSpec as P

HEAD_DIM = 128
TOPK = 3
MASKED = -1e30
SCALING = HEAD_DIM ** (-0.5)
EXPONENT = SCALING * math.log2(math.e)
TILE = 256
STATS = 8
SUBLANES = 8
MIB = 1 << 20


def head_columns(head, offset=0):
    start = head * HEAD_DIM + offset
    if isinstance(head, int):
        return pl.ds(start, HEAD_DIM)
    return pl.ds(pl.multiple_of(start, HEAD_DIM), HEAD_DIM)


def dot(left, right, left_dim, right_dim):
    return lax.dot_general(
        left, right, (((left_dim,), (right_dim,)), ((), ())), preferred_element_type=jnp.float32
    )


def stack_kernel(key_ref, value_ref, out_ref, held_ref, in_sem, out_sem):
    pieces = in_sem.shape[1]
    length = key_ref.shape[0] // pieces
    arrive, leave = [], []
    for index, part in enumerate((key_ref, value_ref)):
        for piece in range(pieces):
            span = pl.ds(piece * length, length)
            held = held_ref.at[index, span]
            arrive.append(pltpu.make_async_copy(part.at[span], held, in_sem.at[index, piece]))
            leave.append(
                pltpu.make_async_copy(held, out_ref.at[span, index], out_sem.at[index, piece])
            )
    for copy in arrive:
        copy.start()
    for first, second in zip(arrive, leave):
        first.wait()
        second.start()
    for copy in leave:
        copy.wait()


def pick_kernel(selection_ref, held_ref, out_ref, filled_ref, sem):
    blocks, _, _, width = held_ref.shape
    heads = width // HEAD_DIM
    copies = []
    for block in range(blocks):
        filled_ref[block, :, 0] = held_ref[max(block - 1, 0)]
        for head in range(heads):
            columns = head_columns(head)
            for slot in range(1, TOPK):
                source = selection_ref[(block * heads + head) * TOPK + slot]
                filled_ref[block, :, slot, :, columns] = held_ref[source, :, :, columns]
        copies.append(
            pltpu.make_async_copy(filled_ref.at[block], out_ref.at[block], sem.at[block])
        )
        copies[-1].start()
    for copy in copies:
        copy.wait()


def reduce_kernel(selection_ref, terms_ref, out_ref, *total_refs):
    blocks, _, _, width = out_ref.shape
    heads = width // HEAD_DIM
    for head, total_ref in enumerate(total_refs):
        total_ref[: blocks - 1] = terms_ref[1:, :, 0, :, head_columns(head)].astype(jnp.float32)
        total_ref[blocks - 1] = jnp.zeros_like(total_ref[blocks - 1])
    for block in range(blocks):
        for slot in range(1, TOPK):
            for head, total_ref in enumerate(total_refs):
                target = selection_ref[(block * heads + head) * TOPK + slot]
                total_ref[target] += terms_ref[block, :, slot, :, head_columns(head)].astype(
                    jnp.float32
                )
    for head, total_ref in enumerate(total_refs):
        out_ref[:, :, :, head_columns(head)] = total_ref[...].astype(out_ref.dtype)


def fold(array):
    return jnp.sum(array.reshape(-1, SUBLANES, array.shape[1]), axis=0)


def causal(scores, first):
    key_at = lax.broadcasted_iota(jnp.int32, scores.shape, 0)
    query_at = lax.broadcasted_iota(jnp.int32, scores.shape, 1) + first
    return jnp.where(key_at <= query_at, scores, MASKED)


def own_forward_kernel(
    selection_ref,
    query_ref,
    key_ref,
    value_ref,
    grad_ref,
    listed_ref,
    turned_ref,
    stats_ref,
    held_ref,
    sem,
):
    heads, _, rows = stats_ref.shape
    copies = [
        pltpu.make_async_copy(source, held_ref.at[index], sem.at[index])
        for index, source in enumerate((query_ref, grad_ref, key_ref, value_ref))
    ]
    for copy in copies:
        copy.start()

    def hand_on(index, carry):
        listed_ref[index] = selection_ref[index]
        return carry

    lax.fori_loop(0, selection_ref.shape[0], hand_on, 0)
    for copy in copies:
        copy.wait()

    def one_head(head, carry):
        columns = head_columns(head)
        key, value = held_ref[2, :, columns], held_ref[3, :, columns]
        for index in range(2):
            turned_ref[index, head] = held_ref[index, :, columns].T
        for first in range(0, rows, TILE):
            tile = pl.ds(first, TILE)
            scores = causal(dot(key, turned_ref[0, head, :, tile], 1, 0), first)
            top = jnp.max(scores, axis=0, keepdims=True)
            raised = jnp.exp2((scores - top) * EXPONENT)
            product = raised * dot(value, turned_ref[1, head, :, tile], 1, 0)
            stats_ref[head, 0:1, tile] = top
            stats_ref[head, 1:2, tile] = jnp.sum(raised, axis=0, keepdims=True)
            stats_ref[head, 2:3, tile] = jnp.sum(product, axis=0, keepdims=True)
        return carry

    lax.fori_loop(0, heads, one_head, 0)


def far_kernel(
    selection_ref,
    position_ref,
    turned_ref,
    query_ref,
    grad_ref,
    listed_ref,
    own_stats_ref,
    terms_ref,
    part_ref,
    stats_ref,
    rows_ref,
    sem,
    *scratch,
):
    heads, _, rows = own_stats_ref.shape
    chunks, _, _, chunk, _ = listed_ref.shape
    block = position_ref[0]
    copies = [
        pltpu.make_async_copy(source, rows_ref.at[index], sem.at[index])
        for index, source in enumerate((query_ref, grad_ref))
    ]
    for copy in copies:
        copy.start()

    def listed(which, head):
        return listed_ref[:, which, :, :, head_columns(head)].reshape(TOPK * rows, HEAD_DIM)

    def one_slot(which, slot, head):
        return listed_ref[:, which, slot, :, head_columns(head)].reshape(rows, HEAD_DIM)

    def softmax(head):
        raised_ref, prob_ref, grad_score_ref = scratch[3 * head : 3 * head + 3]
        live = [
            selection_ref[(block * heads + head) * TOPK + slot] < block for slot in range(TOPK)
        ]
        for first in range(0, rows, TILE):
            tile = pl.ds(first, TILE)
            query, grad = turned_ref[0, head, :, tile], turned_ref[1, head, :, tile]
            scores = dot(listed(0, head), query, 1, 0).reshape(chunks, TOPK, chunk, TILE)
            top = jnp.full((1, TILE), MASKED, jnp.float32)
            for slot in range(TOPK):
                highest = jnp.max(scores[:, slot].reshape(rows, TILE), axis=0, keepdims=True)
                top = jnp.maximum(top, jnp.where(live[slot], highest, MASKED))
            total = jnp.zeros((SUBLANES, TILE), jnp.float32)
            product = jnp.zeros_like(total)
            for slot in range(TOPK):
                shift = jnp.where(live[slot], top, -MASKED)
                scores = dot(one_slot(0, slot, head), query, 1, 0)
                raised = jnp.exp2((scores - shift) * EXPONENT)
                raised_ref[slot, :, tile] = raised
                total += fold(raised)
                product += fold(raised * dot(one_slot(1, slot, head), grad, 1, 0))
            total = jnp.sum(total, axis=0, keepdims=True)
            product = jnp.sum(product, axis=0, keepdims=True)
            own_top = own_stats_ref[head, 0:1, tile]
            highest = jnp.maximum(own_top, top)
            own_factor = jnp.exp2((own_top - highest) * EXPONENT)
            factor = jnp.exp2((top - highest) * EXPONENT)
            inverse = 1.0 / (own_factor * own_stats_ref[head, 1:2, tile] + factor * total)
            own_weight, weight = own_factor * inverse, factor * inverse
            delta = own_weight * own_stats_ref[head, 2:3, tile] + weight * product
            stats_ref[head, 0:1, tile] = own_weight
            stats_ref[head, 1:2, tile] = delta
            for slot in range(TOPK):
                probability = raised_ref[slot, :, tile] * weight
                prob_ref[slot, :, tile] = probability.astype(jnp.bfloat16)
                grad_probs = dot(one_slot(1, slot, head), grad, 1, 0)
                grad_score_ref[slot, :, tile] = (probability * (grad_probs - delta)).astype(
                    jnp.bfloat16
                )

    def gradients(head):
        _, prob_ref, grad_score_ref = scratch[3 * head : 3 * head + 3]
        columns = head_columns(head)
        query, grad = rows_ref[0, :, columns], rows_ref[1, :, columns]
        shape = (chunks, chunk, HEAD_DIM)
        part = None
        for slot in range(TOPK):
            grad_scores = grad_score_ref[slot]
            grad_key = dot(grad_scores, query, 1, 0) * SCALING
            terms_ref[:, 0, slot, :, columns] = grad_key.astype(jnp.bfloat16).reshape(shape)
            grad_value = dot(prob_ref[slot], grad, 1, 0)
            terms_ref[:, 1, slot, :, columns] = grad_value.astype(jnp.bfloat16).reshape(shape)
            product = dot(one_slot(0, slot, head).T, grad_scores, 1, 0)
            part = product if part is None else part + product
        part_ref[head] = part

    for head in range(heads):
        softmax(head)
        if head == 0:
            for copy in copies:
                copy.wait()
        gradients(head)


def own_backward_kernel(
    query_ref,
    key_ref,
    value_ref,
    grad_ref,
    part_ref,
    own_stats_ref,
    stats_ref,
    own_ref,
):
    heads, _, rows = stats_ref.shape
    chunks, _, chunk, _ = own_ref.shape

    def one_head(head, carry):
        columns = head_columns(head)
        query, key = query_ref[:, columns], key_ref[:, columns]
        value, grad = value_ref[:, columns], grad_ref[:, columns]
        scores = causal(dot(key, query, 1, 1), 0)
        raised = jnp.exp2((scores - own_stats_ref[head, 0:1, :]) * EXPONENT)
        probability = raised * stats_ref[head, 0:1, :]
        grad_probs = dot(value, grad, 1, 1)
        grad_scores = (probability * (grad_probs - stats_ref[head, 1:2, :])).astype(jnp.bfloat16)
        results = (
            ((part_ref[head] + dot(key.T, grad_scores, 1, 0)) * SCALING).T,
            dot(grad_scores, query, 1, 0) * SCALING,
            dot(probability.astype(jnp.bfloat16), grad, 1, 0),
        )
        for index, result in enumerate(results):
            own_ref[:, index, :, columns] = result.astype(jnp.bfloat16).reshape(
                chunks, chunk, HEAD_DIM
            )
        return carry

    lax.fori_loop(0, heads, one_head, 0)


def finish_kernel(own_ref, others_ref, out_ref):
    out_ref[:, 0] = own_ref[:, 0]
    out_ref[:, 1:] = (
        others_ref[...].astype(jnp.float32) + own_ref[:, 1:].astype(jnp.float32)
    ).astype(jnp.bfloat16)


def lay_kernel(parts_ref, *refs):
    outs, sem = refs[:-1], refs[-1]
    senders, _, _, width = parts_ref.shape
    copies = [
        pltpu.make_async_copy(
            parts_ref.at[sender, index],
            out.at[:, pl.ds(sender * width, width)],
            sem.at[index, sender],
        )
        for index, out in enumerate(outs)
        for sender in range(senders)
    ]
    for copy in copies:
        copy.start()
    for copy in copies:
        copy.wait()


def on_device(query_input, key_input, value_input, grad_output, selection):
    rows, width = query_input.shape
    heads = width // HEAD_DIM
    chain, spread = lax.axis_size("chain"), lax.axis_size("heads")
    chunk = rows // chain
    share = rows // spread
    listed = selection.reshape(-1)
    position = lax.axis_index("chain").astype(jnp.int32).reshape(1)
    smem = pl.BlockSpec(memory_space=pltpu.SMEM)
    vmem = pl.BlockSpec(memory_space=pltpu.VMEM)
    anywhere = pl.BlockSpec(memory_space=pl.ANY)
    low, full = jnp.bfloat16, jnp.float32

    def swap(array, axis):
        return lax.all_to_all(array, axis, split_axis=0, concat_axis=0, tiled=True)

    def call(kernel, name, in_specs, out_specs, out_shape, scratch=(), limit=4, slots=0):
        flops = 2 * heads * slots * rows * rows * HEAD_DIM
        return pl.pallas_call(
            kernel,
            out_shape=out_shape,
            in_specs=in_specs,
            out_specs=out_specs,
            scratch_shapes=list(scratch),
            cost_estimate=pl.CostEstimate(
                flops=flops, bytes_accessed=4 * MIB, transcendentals=heads * rows * rows
            ),
            compiler_params=pltpu.CompilerParams(vmem_limit_bytes=limit * MIB),
            name=name,
        )

    pair = call(
        stack_kernel,
        "stack",
        [anywhere] * 2,
        anywhere,
        jax.ShapeDtypeStruct((chain, 2, chunk, width), low),
        [
            pltpu.VMEM((2, chain, chunk, width), low),
            pltpu.SemaphoreType.DMA((2, 2)),
            pltpu.SemaphoreType.DMA((2, 2)),
        ],
        limit=59,
    )(key_input.reshape(chain, chunk, width), value_input.reshape(chain, chunk, width))
    held = swap(pair, "chain")
    listed, turned, own_stats = call(
        own_forward_kernel,
        "own_forward",
        [smem] + [anywhere] * 4,
        (smem, vmem, vmem),
        (
            jax.ShapeDtypeStruct(listed.shape, jnp.int32),
            jax.ShapeDtypeStruct((2, heads, HEAD_DIM, rows), low),
            jax.ShapeDtypeStruct((heads, STATS, rows), full),
        ),
        [pltpu.VMEM((4, rows, width), low), pltpu.SemaphoreType.DMA((4,))],
        limit=16,
        slots=2,
    )(listed, query_input, key_input, value_input, grad_output)
    picked = call(
        pick_kernel,
        "pick",
        [smem, vmem],
        anywhere,
        jax.ShapeDtypeStruct((chain, 2, TOPK, chunk, width), low),
        [
            pltpu.VMEM((chain, 2, TOPK, chunk, width), low),
            pltpu.SemaphoreType.DMA((chain,)),
        ],
    )(listed, held)
    slots = swap(picked, "chain")
    terms, part, stats = call(
        far_kernel,
        "far",
        [smem, smem, vmem, anywhere, anywhere, vmem, vmem],
        (vmem, vmem, vmem),
        (
            jax.ShapeDtypeStruct((chain, 2, TOPK, chunk, width), low),
            jax.ShapeDtypeStruct((heads, HEAD_DIM, rows), full),
            jax.ShapeDtypeStruct((heads, STATS, rows), full),
        ),
        [pltpu.VMEM((2, rows, width), low), pltpu.SemaphoreType.DMA((2,))]
        + [
            pltpu.VMEM((TOPK, rows, rows), full),
            pltpu.VMEM((TOPK, rows, rows), low),
            pltpu.VMEM((TOPK, rows, rows), low),
        ]
        * heads,
        limit=32,
        slots=5 * TOPK,
    )(listed, position, turned, query_input, grad_output, slots, own_stats)
    returned = swap(terms, "chain")
    own = call(
        own_backward_kernel,
        "own_backward",
        [vmem] * 7,
        vmem,
        jax.ShapeDtypeStruct((chain, 3, chunk, width), low),
        limit=12,
        slots=5,
    )(query_input, key_input, value_input, grad_output, part, own_stats, stats)
    summed = call(
        reduce_kernel,
        "reduce",
        [smem, vmem],
        vmem,
        jax.ShapeDtypeStruct((chain, 2, chunk, width), low),
        [pltpu.VMEM((chain, 2, chunk, HEAD_DIM), full)] * heads,
    )(listed, returned)
    others = swap(summed, "chain")

    def by_share(array):
        lead = array.shape[1:-2]
        array = array.reshape((spread, chain // spread) + lead + (chunk, width))
        return jnp.moveaxis(array, 1, -3).reshape((spread,) + lead + (share, width))

    whole = call(
        finish_kernel,
        "finish",
        [vmem] * 2,
        vmem,
        jax.ShapeDtypeStruct((spread, 3, share, width), low),
    )(by_share(own), by_share(others))
    whole = swap(whole, "heads")
    return call(
        lay_kernel,
        "lay",
        [vmem],
        (anywhere,) * 3,
        (jax.ShapeDtypeStruct((share, spread * width), low),) * 3,
        [pltpu.SemaphoreType.DMA((3, spread))],
    )(whole)


def solution(mesh):
    in_specs = (
        P("chain", "heads"),
        P("chain", "heads"),
        P("chain", "heads"),
        P("chain", "heads"),
        P(None, "heads", None),
    )
    out_specs = (
        P(("chain", "heads"), None),
        P(("chain", "heads"), None),
        P(("chain", "heads"), None),
    )
    return jax.shard_map(
        on_device, mesh=mesh, in_specs=in_specs, out_specs=out_specs, check_vma=False
    )
```

```python
import math

import jax
import jax.numpy as jnp
from jax import lax
from jax.experimental import pallas as pl
from jax.experimental.pallas import tpu as pltpu
from jax.sharding import PartitionSpec as P

HEAD_DIM = 128
TOPK = 3
MASKED = -1e30
SCALING = HEAD_DIM ** (-0.5)
EXPONENT = SCALING * math.log2(math.e)
TILE = 256
STATS = 8
SUBLANES = 8
MIB = 1 << 20


def head_columns(head, offset=0):
    start = head * HEAD_DIM + offset
    if isinstance(head, int):
        return pl.ds(start, HEAD_DIM)
    return pl.ds(pl.multiple_of(start, HEAD_DIM), HEAD_DIM)


def dot(left, right, left_dim, right_dim):
    return lax.dot_general(
        left, right, (((left_dim,), (right_dim,)), ((), ())), preferred_element_type=jnp.float32
    )


def stack_kernel(key_ref, value_ref, out_ref, held_ref, in_sem, out_sem):
    pieces = in_sem.shape[1]
    length = key_ref.shape[0] // pieces
    arrive, leave = [], []
    for index, part in enumerate((key_ref, value_ref)):
        for piece in range(pieces):
            span = pl.ds(piece * length, length)
            held = held_ref.at[index, span]
            arrive.append(pltpu.make_async_copy(part.at[span], held, in_sem.at[index, piece]))
            leave.append(
                pltpu.make_async_copy(held, out_ref.at[span, index], out_sem.at[index, piece])
            )
    for copy in arrive:
        copy.start()
    for first, second in zip(arrive, leave):
        first.wait()
        second.start()
    for copy in leave:
        copy.wait()


def pick_kernel(selection_ref, held_ref, out_ref, filled_ref, sem):
    blocks, _, _, width = held_ref.shape
    heads = width // HEAD_DIM
    copies = []
    for block in range(blocks):
        filled_ref[block, :, 0] = held_ref[max(block - 1, 0)]
        for head in range(heads):
            columns = head_columns(head)
            for slot in range(1, TOPK):
                source = selection_ref[(block * heads + head) * TOPK + slot]
                filled_ref[block, :, slot, :, columns] = held_ref[source, :, :, columns]
        copies.append(
            pltpu.make_async_copy(filled_ref.at[block], out_ref.at[block], sem.at[block])
        )
        copies[-1].start()
    for copy in copies:
        copy.wait()


def reduce_kernel(selection_ref, terms_ref, out_ref, *total_refs):
    blocks, _, _, width = out_ref.shape
    heads = width // HEAD_DIM
    for head, total_ref in enumerate(total_refs):
        total_ref[: blocks - 1] = terms_ref[1:, :, 0, :, head_columns(head)].astype(jnp.float32)
        total_ref[blocks - 1] = jnp.zeros_like(total_ref[blocks - 1])
    for block in range(blocks):
        for slot in range(1, TOPK):
            for head, total_ref in enumerate(total_refs):
                target = selection_ref[(block * heads + head) * TOPK + slot]
                total_ref[target] += terms_ref[block, :, slot, :, head_columns(head)].astype(
                    jnp.float32
                )
    for head, total_ref in enumerate(total_refs):
        out_ref[:, :, :, head_columns(head)] = total_ref[...].astype(out_ref.dtype)


def fold(array):
    return jnp.sum(array.reshape(-1, SUBLANES, array.shape[1]), axis=0)


def causal(scores, first):
    key_at = lax.broadcasted_iota(jnp.int32, scores.shape, 0)
    query_at = lax.broadcasted_iota(jnp.int32, scores.shape, 1) + first
    return jnp.where(key_at <= query_at, scores, MASKED)


def own_forward_kernel(
    selection_ref,
    query_ref,
    key_ref,
    value_ref,
    grad_ref,
    listed_ref,
    turned_ref,
    stats_ref,
    held_ref,
    sem,
):
    heads, _, rows = stats_ref.shape
    copies = [
        pltpu.make_async_copy(source, held_ref.at[index], sem.at[index])
        for index, source in enumerate((query_ref, grad_ref, key_ref, value_ref))
    ]
    for copy in copies:
        copy.start()

    def hand_on(index, carry):
        listed_ref[index] = selection_ref[index]
        return carry

    lax.fori_loop(0, selection_ref.shape[0], hand_on, 0)
    for copy in copies:
        copy.wait()

    def one_head(head, carry):
        columns = head_columns(head)
        key, value = held_ref[2, :, columns], held_ref[3, :, columns]
        for index in range(2):
            turned_ref[index, head] = held_ref[index, :, columns].T
        for first in range(0, rows, TILE):
            tile = pl.ds(first, TILE)
            scores = causal(dot(key, turned_ref[0, head, :, tile], 1, 0), first)
            top = jnp.max(scores, axis=0, keepdims=True)
            raised = jnp.exp2((scores - top) * EXPONENT)
            product = raised * dot(value, turned_ref[1, head, :, tile], 1, 0)
            stats_ref[head, 0:1, tile] = top
            stats_ref[head, 1:2, tile] = jnp.sum(raised, axis=0, keepdims=True)
            stats_ref[head, 2:3, tile] = jnp.sum(product, axis=0, keepdims=True)
        return carry

    lax.fori_loop(0, heads, one_head, 0)


def far_kernel(
    selection_ref,
    position_ref,
    turned_ref,
    query_ref,
    grad_ref,
    listed_ref,
    own_stats_ref,
    terms_ref,
    part_ref,
    stats_ref,
    rows_ref,
    sem,
    score_ref,
    grad_prob_ref,
    prob_ref,
    grad_score_ref,
):
    heads, _, rows = own_stats_ref.shape
    chunks, _, _, chunk, _ = listed_ref.shape
    block = position_ref[0]
    tiles = rows // TILE
    copies = [
        pltpu.make_async_copy(source, rows_ref.at[index], sem.at[index])
        for index, source in enumerate((query_ref, grad_ref))
    ]
    for copy in copies:
        copy.start()

    def listed(which, slot, columns):
        return listed_ref[:, which, slot, :, columns].reshape(rows, HEAD_DIM)

    def softmax(index, carry):
        head, at = index // tiles, index % tiles
        columns = head_columns(head)
        tile = pl.ds(pl.multiple_of(at * TILE, TILE), TILE)
        live = [
            selection_ref[(block * heads + head) * TOPK + slot] < block for slot in range(TOPK)
        ]
        query, grad = turned_ref[0, head, :, tile], turned_ref[1, head, :, tile]
        top = jnp.full((1, TILE), MASKED, jnp.float32)
        for slot in range(TOPK):
            scores = dot(listed(0, slot, columns), query, 1, 0)
            score_ref[slot] = scores
            highest = jnp.max(scores, axis=0, keepdims=True)
            top = jnp.maximum(top, jnp.where(live[slot], highest, MASKED))
        total = jnp.zeros((SUBLANES, TILE), jnp.float32)
        product = jnp.zeros_like(total)
        for slot in range(TOPK):
            shift = jnp.where(live[slot], top, -MASKED)
            raised = jnp.exp2((score_ref[slot] - shift) * EXPONENT)
            score_ref[slot] = raised
            grad_probs = dot(listed(1, slot, columns), grad, 1, 0)
            grad_prob_ref[slot] = grad_probs
            total += fold(raised)
            product += fold(raised * grad_probs)
        total = jnp.sum(total, axis=0, keepdims=True)
        product = jnp.sum(product, axis=0, keepdims=True)
        own_top = own_stats_ref[head, 0:1, tile]
        highest = jnp.maximum(own_top, top)
        own_factor = jnp.exp2((own_top - highest) * EXPONENT)
        factor = jnp.exp2((top - highest) * EXPONENT)
        inverse = 1.0 / (own_factor * own_stats_ref[head, 1:2, tile] + factor * total)
        own_weight, weight = own_factor * inverse, factor * inverse
        delta = own_weight * own_stats_ref[head, 2:3, tile] + weight * product
        stats_ref[head, 0:1, tile] = own_weight
        stats_ref[head, 1:2, tile] = delta
        for slot in range(TOPK):
            probability = score_ref[slot] * weight
            prob_ref[head, slot, :, tile] = probability.astype(jnp.bfloat16)
            grad_score_ref[head, slot, :, tile] = (
                probability * (grad_prob_ref[slot] - delta)
            ).astype(jnp.bfloat16)
        return carry

    def gradients(index, carry):
        head, slot = index // TOPK, index % TOPK
        columns = head_columns(head)
        shape = (chunks, chunk, HEAD_DIM)
        grad_scores = grad_score_ref[head, slot]
        grad_key = dot(grad_scores, rows_ref[0, :, columns], 1, 0) * SCALING
        terms_ref[:, 0, slot, :, columns] = grad_key.astype(jnp.bfloat16).reshape(shape)
        grad_value = dot(prob_ref[head, slot], rows_ref[1, :, columns], 1, 0)
        terms_ref[:, 1, slot, :, columns] = grad_value.astype(jnp.bfloat16).reshape(shape)
        part_ref[head] += dot(listed(0, slot, columns).T, grad_scores, 1, 0)
        return carry

    part_ref[...] = jnp.zeros_like(part_ref)
    lax.fori_loop(0, heads * tiles, softmax, 0)
    for copy in copies:
        copy.wait()
    lax.fori_loop(0, heads * TOPK, gradients, 0)


def own_backward_kernel(
    query_ref,
    key_ref,
    value_ref,
    grad_ref,
    part_ref,
    own_stats_ref,
    stats_ref,
    own_ref,
):
    heads, _, rows = stats_ref.shape
    chunks, _, chunk, _ = own_ref.shape

    def one_head(head, carry):
        columns = head_columns(head)
        query, key = query_ref[:, columns], key_ref[:, columns]
        value, grad = value_ref[:, columns], grad_ref[:, columns]
        scores = causal(dot(key, query, 1, 1), 0)
        raised = jnp.exp2((scores - own_stats_ref[head, 0:1, :]) * EXPONENT)
        probability = raised * stats_ref[head, 0:1, :]
        grad_probs = dot(value, grad, 1, 1)
        grad_scores = (probability * (grad_probs - stats_ref[head, 1:2, :])).astype(jnp.bfloat16)
        results = (
            ((part_ref[head] + dot(key.T, grad_scores, 1, 0)) * SCALING).T,
            dot(grad_scores, query, 1, 0) * SCALING,
            dot(probability.astype(jnp.bfloat16), grad, 1, 0),
        )
        for index, result in enumerate(results):
            own_ref[:, index, :, columns] = result.astype(jnp.bfloat16).reshape(
                chunks, chunk, HEAD_DIM
            )
        return carry

    lax.fori_loop(0, heads, one_head, 0)


def finish_kernel(own_ref, others_ref, out_ref):
    out_ref[:, 0] = own_ref[:, 0]
    out_ref[:, 1:] = (
        others_ref[...].astype(jnp.float32) + own_ref[:, 1:].astype(jnp.float32)
    ).astype(jnp.bfloat16)


def lay_kernel(parts_ref, *refs):
    outs, sem = refs[:-1], refs[-1]
    senders, _, _, width = parts_ref.shape
    copies = [
        pltpu.make_async_copy(
            parts_ref.at[sender, index],
            out.at[:, pl.ds(sender * width, width)],
            sem.at[index, sender],
        )
        for index, out in enumerate(outs)
        for sender in range(senders)
    ]
    for copy in copies:
        copy.start()
    for copy in copies:
        copy.wait()


def on_device(query_input, key_input, value_input, grad_output, selection):
    rows, width = query_input.shape
    heads = width // HEAD_DIM
    chain, spread = lax.axis_size("chain"), lax.axis_size("heads")
    chunk = rows // chain
    share = rows // spread
    listed = selection.reshape(-1)
    position = lax.axis_index("chain").astype(jnp.int32).reshape(1)
    smem = pl.BlockSpec(memory_space=pltpu.SMEM)
    vmem = pl.BlockSpec(memory_space=pltpu.VMEM)
    anywhere = pl.BlockSpec(memory_space=pl.ANY)
    low, full = jnp.bfloat16, jnp.float32

    def swap(array, axis):
        return lax.all_to_all(array, axis, split_axis=0, concat_axis=0, tiled=True)

    def call(kernel, name, in_specs, out_specs, out_shape, scratch=(), limit=4, slots=0):
        flops = 2 * heads * slots * rows * rows * HEAD_DIM
        return pl.pallas_call(
            kernel,
            out_shape=out_shape,
            in_specs=in_specs,
            out_specs=out_specs,
            scratch_shapes=list(scratch),
            cost_estimate=pl.CostEstimate(
                flops=flops, bytes_accessed=4 * MIB, transcendentals=heads * rows * rows
            ),
            compiler_params=pltpu.CompilerParams(vmem_limit_bytes=limit * MIB),
            name=name,
        )

    pair = call(
        stack_kernel,
        "stack",
        [anywhere] * 2,
        anywhere,
        jax.ShapeDtypeStruct((chain, 2, chunk, width), low),
        [
            pltpu.VMEM((2, chain, chunk, width), low),
            pltpu.SemaphoreType.DMA((2, 2)),
            pltpu.SemaphoreType.DMA((2, 2)),
        ],
        limit=59,
    )(key_input.reshape(chain, chunk, width), value_input.reshape(chain, chunk, width))
    held = swap(pair, "chain")
    listed, turned, own_stats = call(
        own_forward_kernel,
        "own_forward",
        [smem] + [anywhere] * 4,
        (smem, vmem, vmem),
        (
            jax.ShapeDtypeStruct(listed.shape, jnp.int32),
            jax.ShapeDtypeStruct((2, heads, HEAD_DIM, rows), low),
            jax.ShapeDtypeStruct((heads, STATS, rows), full),
        ),
        [pltpu.VMEM((4, rows, width), low), pltpu.SemaphoreType.DMA((4,))],
        limit=16,
        slots=2,
    )(listed, query_input, key_input, value_input, grad_output)
    picked = call(
        pick_kernel,
        "pick",
        [smem, vmem],
        anywhere,
        jax.ShapeDtypeStruct((chain, 2, TOPK, chunk, width), low),
        [
            pltpu.VMEM((chain, 2, TOPK, chunk, width), low),
            pltpu.SemaphoreType.DMA((chain,)),
        ],
    )(listed, held)
    slots = swap(picked, "chain")
    terms, part, stats = call(
        far_kernel,
        "far",
        [smem, smem, vmem, anywhere, anywhere, vmem, vmem],
        (vmem, vmem, vmem),
        (
            jax.ShapeDtypeStruct((chain, 2, TOPK, chunk, width), low),
            jax.ShapeDtypeStruct((heads, HEAD_DIM, rows), full),
            jax.ShapeDtypeStruct((heads, STATS, rows), full),
        ),
        [
            pltpu.VMEM((2, rows, width), low),
            pltpu.SemaphoreType.DMA((2,)),
            pltpu.VMEM((TOPK, rows, TILE), full),
            pltpu.VMEM((TOPK, rows, TILE), full),
            pltpu.VMEM((heads, TOPK, rows, rows), low),
            pltpu.VMEM((heads, TOPK, rows, rows), low),
        ],
        limit=32,
        slots=5 * TOPK,
    )(listed, position, turned, query_input, grad_output, slots, own_stats)
    returned = swap(terms, "chain")
    own = call(
        own_backward_kernel,
        "own_backward",
        [vmem] * 7,
        vmem,
        jax.ShapeDtypeStruct((chain, 3, chunk, width), low),
        limit=12,
        slots=5,
    )(query_input, key_input, value_input, grad_output, part, own_stats, stats)
    summed = call(
        reduce_kernel,
        "reduce",
        [smem, vmem],
        vmem,
        jax.ShapeDtypeStruct((chain, 2, chunk, width), low),
        [pltpu.VMEM((chain, 2, chunk, HEAD_DIM), full)] * heads,
    )(listed, returned)
    others = swap(summed, "chain")

    def by_share(array):
        lead = array.shape[1:-2]
        array = array.reshape((spread, chain // spread) + lead + (chunk, width))
        return jnp.moveaxis(array, 1, -3).reshape((spread,) + lead + (share, width))

    whole = call(
        finish_kernel,
        "finish",
        [vmem] * 2,
        vmem,
        jax.ShapeDtypeStruct((spread, 3, share, width), low),
    )(by_share(own), by_share(others))
    whole = swap(whole, "heads")
    return call(
        lay_kernel,
        "lay",
        [vmem],
        (anywhere,) * 3,
        (jax.ShapeDtypeStruct((share, spread * width), low),) * 3,
        [pltpu.SemaphoreType.DMA((3, spread))],
    )(whole)


def solution(mesh):
    in_specs = (
        P("chain", "heads"),
        P("chain", "heads"),
        P("chain", "heads"),
        P("chain", "heads"),
        P(None, "heads", None),
    )
    out_specs = (
        P(("chain", "heads"), None),
        P(("chain", "heads"), None),
        P(("chain", "heads"), None),
    )
    return jax.shard_map(
        on_device, mesh=mesh, in_specs=in_specs, out_specs=out_specs, check_vma=False
    )
```

```python
import math

import jax
import jax.numpy as jnp
from jax import lax
from jax.experimental import pallas as pl
from jax.experimental.pallas import tpu as pltpu
from jax.sharding import PartitionSpec as P

HEAD_DIM = 128
TOPK = 3
MASKED = -1e30
SCALING = HEAD_DIM ** (-0.5)
EXPONENT = SCALING * math.log2(math.e)
TILE = 256
STATS = 8
SUBLANES = 8
MIB = 1 << 20


def head_columns(head, offset=0):
    start = head * HEAD_DIM + offset
    if isinstance(head, int):
        return pl.ds(start, HEAD_DIM)
    return pl.ds(pl.multiple_of(start, HEAD_DIM), HEAD_DIM)


def dot(left, right, left_dim, right_dim):
    return lax.dot_general(
        left, right, (((left_dim,), (right_dim,)), ((), ())), preferred_element_type=jnp.float32
    )


def stack_kernel(key_ref, value_ref, out_ref, held_ref, in_sem, out_sem):
    pieces = in_sem.shape[1]
    length = key_ref.shape[0] // pieces
    arrive, leave = [], []
    for index, part in enumerate((key_ref, value_ref)):
        for piece in range(pieces):
            span = pl.ds(piece * length, length)
            held = held_ref.at[index, span]
            arrive.append(pltpu.make_async_copy(part.at[span], held, in_sem.at[index, piece]))
            leave.append(
                pltpu.make_async_copy(held, out_ref.at[span, index], out_sem.at[index, piece])
            )
    for copy in arrive:
        copy.start()
    for first, second in zip(arrive, leave):
        first.wait()
        second.start()
    for copy in leave:
        copy.wait()


def pick_kernel(selection_ref, held_ref, out_ref, filled_ref, sem):
    blocks, _, _, width = held_ref.shape
    heads = width // HEAD_DIM
    copies = []
    for block in range(blocks):
        filled_ref[block, :, 0] = held_ref[max(block - 1, 0)]
        for head in range(heads):
            columns = head_columns(head)
            for slot in range(1, TOPK):
                source = selection_ref[(block * heads + head) * TOPK + slot]
                filled_ref[block, :, slot, :, columns] = held_ref[source, :, :, columns]
        copies.append(
            pltpu.make_async_copy(filled_ref.at[block], out_ref.at[block], sem.at[block])
        )
        copies[-1].start()
    for copy in copies:
        copy.wait()


def reduce_kernel(selection_ref, terms_ref, after_ref, out_ref, *total_refs):
    blocks, _, _, width = out_ref.shape
    heads = width // HEAD_DIM
    for head, total_ref in enumerate(total_refs):
        total_ref[: blocks - 1] = terms_ref[1:, :, 0, :, head_columns(head)].astype(jnp.float32)
        total_ref[blocks - 1] = jnp.zeros_like(total_ref[blocks - 1])
    for block in range(blocks):
        for slot in range(1, TOPK):
            for head, total_ref in enumerate(total_refs):
                target = selection_ref[(block * heads + head) * TOPK + slot]
                total_ref[target] += terms_ref[block, :, slot, :, head_columns(head)].astype(
                    jnp.float32
                )
    for head, total_ref in enumerate(total_refs):
        out_ref[:, :, :, head_columns(head)] = total_ref[...].astype(out_ref.dtype)


def fold(array):
    return jnp.sum(array.reshape(-1, SUBLANES, array.shape[1]), axis=0)


def causal(scores, first):
    key_at = lax.broadcasted_iota(jnp.int32, scores.shape, 0)
    query_at = lax.broadcasted_iota(jnp.int32, scores.shape, 1) + first
    return jnp.where(key_at <= query_at, scores, MASKED)


def own_forward_kernel(
    selection_ref,
    query_ref,
    key_ref,
    value_ref,
    grad_ref,
    listed_ref,
    turned_ref,
    stats_ref,
    held_ref,
    sem,
):
    heads, _, rows = stats_ref.shape
    copies = [
        pltpu.make_async_copy(source, held_ref.at[index], sem.at[index])
        for index, source in enumerate((query_ref, grad_ref, key_ref, value_ref))
    ]
    for copy in copies:
        copy.start()

    def hand_on(index, carry):
        listed_ref[index] = selection_ref[index]
        return carry

    lax.fori_loop(0, selection_ref.shape[0], hand_on, 0)
    for copy in copies:
        copy.wait()

    def one_head(head, carry):
        columns = head_columns(head)
        key, value = held_ref[2, :, columns], held_ref[3, :, columns]
        for index in range(2):
            turned_ref[index, head] = held_ref[index, :, columns].T
        for first in range(0, rows, TILE):
            tile = pl.ds(first, TILE)
            scores = causal(dot(key, turned_ref[0, head, :, tile], 1, 0), first)
            top = jnp.max(scores, axis=0, keepdims=True)
            raised = jnp.exp2((scores - top) * EXPONENT)
            product = raised * dot(value, turned_ref[1, head, :, tile], 1, 0)
            stats_ref[head, 0:1, tile] = top
            stats_ref[head, 1:2, tile] = jnp.sum(raised, axis=0, keepdims=True)
            stats_ref[head, 2:3, tile] = jnp.sum(product, axis=0, keepdims=True)
        return carry

    lax.fori_loop(0, heads, one_head, 0)


def far_kernel(
    selection_ref,
    position_ref,
    turned_ref,
    query_ref,
    grad_ref,
    listed_ref,
    own_stats_ref,
    terms_ref,
    part_ref,
    stats_ref,
    rows_ref,
    sem,
    held_terms_ref,
    terms_sem,
    *scratch,
):
    heads, _, rows = own_stats_ref.shape
    chunks, _, _, chunk, _ = listed_ref.shape
    block = position_ref[0]
    copies = [
        pltpu.make_async_copy(source, rows_ref.at[index], sem.at[index])
        for index, source in enumerate((query_ref, grad_ref))
    ]
    for copy in copies:
        copy.start()

    def listed(which, head):
        return listed_ref[:, which, :, :, head_columns(head)].reshape(TOPK * rows, HEAD_DIM)

    def softmax(head):
        score_ref, grad_prob_ref, prob_ref, grad_score_ref = scratch[4 * head : 4 * head + 4]
        live = [
            selection_ref[(block * heads + head) * TOPK + slot] < block for slot in range(TOPK)
        ]
        shape = (chunks, TOPK, chunk, TILE)
        for first in range(0, rows, TILE):
            tile = pl.ds(first, TILE)
            scores = dot(listed(0, head), turned_ref[0, head, :, tile], 1, 0)
            score_ref[:, :, :, tile] = scores.reshape(shape)
            grad_probs = dot(listed(1, head), turned_ref[1, head, :, tile], 1, 0)
            grad_prob_ref[:, :, :, tile] = grad_probs.reshape(shape)
            top = jnp.full((1, TILE), MASKED, jnp.float32)
            for slot in range(TOPK):
                highest = jnp.max(
                    score_ref[:, slot, :, tile].reshape(rows, TILE), axis=0, keepdims=True
                )
                top = jnp.maximum(top, jnp.where(live[slot], highest, MASKED))
            total = jnp.zeros((SUBLANES, TILE), jnp.float32)
            product = jnp.zeros_like(total)
            for slot in range(TOPK):
                shift = jnp.where(live[slot], top, -MASKED)
                for part in range(chunks):
                    raised = jnp.exp2((score_ref[part, slot, :, tile] - shift) * EXPONENT)
                    score_ref[part, slot, :, tile] = raised
                    total += fold(raised)
                    product += fold(raised * grad_prob_ref[part, slot, :, tile])
            total = jnp.sum(total, axis=0, keepdims=True)
            product = jnp.sum(product, axis=0, keepdims=True)
            own_top = own_stats_ref[head, 0:1, tile]
            highest = jnp.maximum(own_top, top)
            own_factor = jnp.exp2((own_top - highest) * EXPONENT)
            factor = jnp.exp2((top - highest) * EXPONENT)
            inverse = 1.0 / (own_factor * own_stats_ref[head, 1:2, tile] + factor * total)
            own_weight, weight = own_factor * inverse, factor * inverse
            delta = own_weight * own_stats_ref[head, 2:3, tile] + weight * product
            stats_ref[head, 0:1, tile] = own_weight
            stats_ref[head, 1:2, tile] = delta
            for slot in range(TOPK):
                for part in range(chunks):
                    probability = score_ref[part, slot, :, tile] * weight
                    prob_ref[part, slot, :, tile] = probability.astype(jnp.bfloat16)
                    grad_score_ref[part, slot, :, tile] = (
                        probability * (grad_prob_ref[part, slot, :, tile] - delta)
                    ).astype(jnp.bfloat16)

    def gradients(head):
        _, _, prob_ref, grad_score_ref = scratch[4 * head : 4 * head + 4]
        columns = head_columns(head)
        query, grad = rows_ref[0, :, columns], rows_ref[1, :, columns]
        shape = (chunks, TOPK, chunk, HEAD_DIM)
        prob = prob_ref[...].reshape(TOPK * rows, rows)
        grad_scores = grad_score_ref[...].reshape(TOPK * rows, rows)
        for which in range(2):
            if which == 0:
                term = dot(grad_scores, query, 1, 0) * SCALING
            else:
                term = dot(prob, grad, 1, 0)
            held_terms_ref[:, which, :, :, columns] = term.astype(jnp.bfloat16).reshape(shape)
            copy = pltpu.make_async_copy(
                held_terms_ref.at[:, which, :, :, columns],
                terms_ref.at[:, which, :, :, columns],
                terms_sem.at[head, which],
            )
            copy.start()
            sent.append(copy)
        part_ref[head] = dot(listed(0, head).T, grad_scores, 1, 0)

    sent = []
    for head in range(heads):
        softmax(head)
        if head == 0:
            for copy in copies:
                copy.wait()
        gradients(head)
    for copy in sent:
        copy.wait()


def own_backward_kernel(
    place_ref,
    query_ref,
    key_ref,
    value_ref,
    grad_ref,
    part_ref,
    own_stats_ref,
    stats_ref,
    own_ref,
    *refs,
):
    piece_refs, grad_query_ref = refs[:-1], refs[-1]
    heads, _, rows = stats_ref.shape
    chunks, _, chunk, _ = own_ref.shape

    def one_head(head, carry):
        columns = head_columns(head)
        query, key = query_ref[:, columns], key_ref[:, columns]
        value, grad = value_ref[:, columns], grad_ref[:, columns]
        scores = causal(dot(key, query, 1, 1), 0)
        raised = jnp.exp2((scores - own_stats_ref[head, 0:1, :]) * EXPONENT)
        probability = raised * stats_ref[head, 0:1, :]
        grad_probs = dot(value, grad, 1, 1)
        grad_scores = (probability * (grad_probs - stats_ref[head, 1:2, :])).astype(jnp.bfloat16)
        grad_query = (part_ref[head] + dot(key.T, grad_scores, 1, 0)) * SCALING
        grad_query_ref[:, columns] = grad_query.T.astype(jnp.bfloat16)
        results = (
            dot(grad_scores, query, 1, 0) * SCALING,
            dot(probability.astype(jnp.bfloat16), grad, 1, 0),
        )
        for index, result in enumerate(results):
            own_ref[:, index, :, columns] = result.astype(jnp.bfloat16).reshape(
                chunks, chunk, HEAD_DIM
            )
        return carry

    lax.fori_loop(0, heads, one_head, 0)
    planes = len(piece_refs)
    plane = place_ref[1]
    length = rows // planes
    for step, piece_ref in enumerate(piece_refs):
        first = pl.multiple_of(((plane + step) % planes) * length, length)
        piece_ref[...] = grad_query_ref[pl.ds(first, length), :]


def join_kernel(place_ref, *refs):
    piece_refs, out_ref = refs[:-1], refs[-1]
    share = out_ref.shape[1]
    first = pl.multiple_of((1 - place_ref[2]) * share, share)
    for step, piece_ref in enumerate(piece_refs):
        out_ref[step] = piece_ref[pl.ds(first, share), :]


def finish_kernel(own_ref, others_ref, after_ref, out_ref):
    out_ref[...] = (
        others_ref[...].astype(jnp.float32) + own_ref[...].astype(jnp.float32)
    ).astype(jnp.bfloat16)


def lay_kernel(place_ref, parts_ref, other_ref, *refs):
    piece_refs, (query_ref, key_ref, value_ref, sem) = refs[:-4], refs[-4:]
    senders, _, share, width = parts_ref.shape
    planes = len(piece_refs)
    cores = senders // planes
    plane, core = place_ref[1], place_ref[2]
    copies = []

    def put(source, out, sender):
        first = sender * width
        if not isinstance(sender, int):
            first = pl.multiple_of(first, width)
        target = out.at[:, pl.ds(first, width)]
        copies.append(pltpu.make_async_copy(source, target, sem.at[len(copies)]))
        copies[-1].start()

    for step, piece_ref in enumerate(piece_refs):
        origin = (plane - step + planes) % planes
        rows = pl.ds(pl.multiple_of(core * share, share), share)
        put(piece_ref.at[rows], query_ref, origin * cores + core)
        if cores > 1:
            put(other_ref.at[step], query_ref, origin * cores + 1 - core)
    for sender in range(senders):
        put(parts_ref.at[sender, 0], key_ref, sender)
        put(parts_ref.at[sender, 1], value_ref, sender)
    for copy in copies:
        copy.wait()


def on_device(query_input, key_input, value_input, grad_output, selection):
    rows, width = query_input.shape
    heads = width // HEAD_DIM
    chain, spread = lax.axis_size("chain"), lax.axis_size("heads")
    chunk = rows // chain
    share = rows // spread
    listed = selection.reshape(-1)
    cores = 2 if spread % 2 == 0 else 1
    planes = spread // cores
    at = lax.axis_index("heads")
    position = jnp.stack([lax.axis_index("chain"), at // cores, at % cores]).astype(jnp.int32)
    smem = pl.BlockSpec(memory_space=pltpu.SMEM)
    vmem = pl.BlockSpec(memory_space=pltpu.VMEM)
    anywhere = pl.BlockSpec(memory_space=pl.ANY)
    low, full = jnp.bfloat16, jnp.float32

    def swap(array, axis):
        return lax.all_to_all(array, axis, split_axis=0, concat_axis=0, tiled=True)

    def call(kernel, name, in_specs, out_specs, out_shape, scratch=(), limit=4, slots=0):
        flops = 2 * heads * slots * rows * rows * HEAD_DIM
        return pl.pallas_call(
            kernel,
            out_shape=out_shape,
            in_specs=in_specs,
            out_specs=out_specs,
            scratch_shapes=list(scratch),
            cost_estimate=pl.CostEstimate(
                flops=flops, bytes_accessed=4 * MIB, transcendentals=heads * rows * rows
            ),
            compiler_params=pltpu.CompilerParams(vmem_limit_bytes=limit * MIB),
            name=name,
        )

    pair = call(
        stack_kernel,
        "stack",
        [anywhere] * 2,
        anywhere,
        jax.ShapeDtypeStruct((chain, 2, chunk, width), low),
        [
            pltpu.VMEM((2, chain, chunk, width), low),
            pltpu.SemaphoreType.DMA((2, 2)),
            pltpu.SemaphoreType.DMA((2, 2)),
        ],
        limit=59,
    )(key_input.reshape(chain, chunk, width), value_input.reshape(chain, chunk, width))
    held = swap(pair, "chain")
    listed, turned, own_stats = call(
        own_forward_kernel,
        "own_forward",
        [smem] + [anywhere] * 4,
        (smem, vmem, vmem),
        (
            jax.ShapeDtypeStruct(listed.shape, jnp.int32),
            jax.ShapeDtypeStruct((2, heads, HEAD_DIM, rows), low),
            jax.ShapeDtypeStruct((heads, STATS, rows), full),
        ),
        [pltpu.VMEM((4, rows, width), low), pltpu.SemaphoreType.DMA((4,))],
        limit=16,
        slots=2,
    )(listed, query_input, key_input, value_input, grad_output)
    picked = call(
        pick_kernel,
        "pick",
        [smem, vmem],
        anywhere,
        jax.ShapeDtypeStruct((chain, 2, TOPK, chunk, width), low),
        [
            pltpu.VMEM((chain, 2, TOPK, chunk, width), low),
            pltpu.SemaphoreType.DMA((chain,)),
        ],
    )(listed, held)
    slots = swap(picked, "chain")
    terms, part, stats = call(
        far_kernel,
        "far",
        [smem, smem, vmem, anywhere, anywhere, vmem, vmem],
        (anywhere, vmem, vmem),
        (
            jax.ShapeDtypeStruct((chain, 2, TOPK, chunk, width), low),
            jax.ShapeDtypeStruct((heads, HEAD_DIM, rows), full),
            jax.ShapeDtypeStruct((heads, STATS, rows), full),
        ),
        [
            pltpu.VMEM((2, rows, width), low),
            pltpu.SemaphoreType.DMA((2,)),
            pltpu.VMEM((chain, 2, TOPK, chunk, width), low),
            pltpu.SemaphoreType.DMA((heads, 2)),
        ]
        + [
            pltpu.VMEM((chain, TOPK, chunk, rows), full),
            pltpu.VMEM((chain, TOPK, chunk, rows), full),
            pltpu.VMEM((chain, TOPK, chunk, rows), low),
            pltpu.VMEM((chain, TOPK, chunk, rows), low),
        ]
        * heads,
        limit=32,
        slots=5 * TOPK,
    )(listed, position, turned, query_input, grad_output, slots, own_stats)
    returned = swap(terms, "chain")
    own, *pieces = call(
        own_backward_kernel,
        "own_backward",
        [smem] + [vmem] * 7,
        (vmem,) * (1 + planes),
        (jax.ShapeDtypeStruct((chain, 2, chunk, width), low),)
        + (jax.ShapeDtypeStruct((rows // planes, width), low),) * planes,
        [pltpu.VMEM((rows, width), low)],
        limit=12,
        slots=5,
    )(position, query_input, key_input, value_input, grad_output, part, own_stats, stats)

    def to_plane(piece, step):
        if step == 0:
            return piece
        pairs = [(one, (one + step * cores) % spread) for one in range(spread)]
        return lax.ppermute(piece, "heads", pairs)

    for step in sorted(range(planes), key=lambda step: -min(step, planes - step)):
        pieces[step] = to_plane(pieces[step], step)
    joined = other = pieces[0]
    if cores > 1:
        joined = call(
            join_kernel,
            "join",
            [smem] + [vmem] * planes,
            vmem,
            jax.ShapeDtypeStruct((planes, share, width), low),
        )(position, *pieces)
        other = lax.ppermute(joined, "heads", [(one, one ^ 1) for one in range(spread)])
    summed = call(
        reduce_kernel,
        "reduce",
        [smem, vmem, anywhere],
        vmem,
        jax.ShapeDtypeStruct((chain, 2, chunk, width), low),
        [pltpu.VMEM((chain, 2, chunk, HEAD_DIM), full)] * heads,
    )(listed, returned, joined)
    others = swap(summed, "chain")

    def by_share(array):
        lead = array.shape[1:-2]
        array = array.reshape((spread, chain // spread) + lead + (chunk, width))
        return jnp.moveaxis(array, 1, -3).reshape((spread,) + lead + (share, width))

    whole = call(
        finish_kernel,
        "finish",
        [vmem] * 2 + [anywhere],
        vmem,
        jax.ShapeDtypeStruct((spread, 2, share, width), low),
    )(by_share(own), by_share(others), other)
    whole = swap(whole, "heads")
    return call(
        lay_kernel,
        "lay",
        [smem] + [vmem] * (2 + planes),
        (anywhere,) * 3,
        (jax.ShapeDtypeStruct((share, spread * width), low),) * 3,
        [pltpu.SemaphoreType.DMA((3 * spread,))],
    )(position, whole, other, *pieces)


def solution(mesh):
    in_specs = (
        P("chain", "heads"),
        P("chain", "heads"),
        P("chain", "heads"),
        P("chain", "heads"),
        P(None, "heads", None),
    )
    out_specs = (
        P(("chain", "heads"), None),
        P(("chain", "heads"), None),
        P(("chain", "heads"), None),
    )
    return jax.shard_map(
        on_device, mesh=mesh, in_specs=in_specs, out_specs=out_specs, check_vma=False
    )
```

```python
import functools
import math

import jax
import jax.numpy as jnp
from jax import lax
from jax.experimental import pallas as pl
from jax.experimental.pallas import tpu as pltpu
from jax.sharding import PartitionSpec as P

HEAD_DIM = 128
TOPK = 3
MASKED = -1e30
SCALING = HEAD_DIM ** (-0.5)
EXPONENT = SCALING * math.log2(math.e)
TILE = 256
STATS = 8
SUBLANES = 8
EARLY = 5
MIB = 1 << 20


def head_columns(head, offset=0):
    start = head * HEAD_DIM + offset
    if isinstance(head, int):
        return pl.ds(start, HEAD_DIM)
    return pl.ds(pl.multiple_of(start, HEAD_DIM), HEAD_DIM)


def dot(left, right, left_dim, right_dim):
    return lax.dot_general(
        left, right, (((left_dim,), (right_dim,)), ((), ())), preferred_element_type=jnp.float32
    )


def stack_kernel(key_ref, value_ref, out_ref, held_ref, in_sem, out_sem):
    pieces = in_sem.shape[1]
    length = key_ref.shape[0] // pieces
    arrive, leave = [], []
    for index, part in enumerate((key_ref, value_ref)):
        for piece in range(pieces):
            span = pl.ds(piece * length, length)
            held = held_ref.at[index, span]
            arrive.append(pltpu.make_async_copy(part.at[span], held, in_sem.at[index, piece]))
            leave.append(
                pltpu.make_async_copy(held, out_ref.at[span, index], out_sem.at[index, piece])
            )
    for copy in arrive:
        copy.start()
    for first, second in zip(arrive, leave):
        first.wait()
        second.start()
    for copy in leave:
        copy.wait()


def pick_kernel(selection_ref, held_ref, out_ref, filled_ref, sem):
    blocks, _, _, width = held_ref.shape
    heads = width // HEAD_DIM
    copies = []
    for block in range(blocks):
        filled_ref[block, :, 0] = held_ref[max(block - 1, 0)]
        for head in range(heads):
            columns = head_columns(head)
            for slot in range(1, TOPK):
                source = selection_ref[(block * heads + head) * TOPK + slot]
                filled_ref[block, :, slot, :, columns] = held_ref[source, :, :, columns]
        copies.append(
            pltpu.make_async_copy(filled_ref.at[block], out_ref.at[block], sem.at[block])
        )
        copies[-1].start()
    for copy in copies:
        copy.wait()


def reduce_kernel(after, selection_ref, terms_ref, *refs):
    out_ref, total_refs = refs[after], refs[after + 1 :]
    blocks, _, _, width = out_ref.shape
    heads = width // HEAD_DIM
    for head, total_ref in enumerate(total_refs):
        total_ref[: blocks - 1] = terms_ref[1:, head, :, 0].astype(jnp.float32)
        total_ref[blocks - 1] = jnp.zeros_like(total_ref[blocks - 1])
    for block in range(blocks):
        for slot in range(1, TOPK):
            for head, total_ref in enumerate(total_refs):
                target = selection_ref[(block * heads + head) * TOPK + slot]
                total_ref[target] += terms_ref[block, head, :, slot].astype(jnp.float32)
    for head, total_ref in enumerate(total_refs):
        out_ref[:, :, :, head_columns(head)] = total_ref[...].astype(out_ref.dtype)


def fold(array):
    return jnp.sum(array.reshape(-1, SUBLANES, array.shape[1]), axis=0)


def causal(scores, first):
    key_at = lax.broadcasted_iota(jnp.int32, scores.shape, 0)
    query_at = lax.broadcasted_iota(jnp.int32, scores.shape, 1) + first
    return jnp.where(key_at <= query_at, scores, MASKED)


def own_forward_kernel(
    selection_ref,
    query_ref,
    key_ref,
    value_ref,
    grad_ref,
    listed_ref,
    stats_ref,
    held_ref,
    sem,
):
    heads, _, rows = stats_ref.shape
    copies = [
        pltpu.make_async_copy(source, held_ref.at[index], sem.at[index])
        for index, source in enumerate((query_ref, grad_ref, key_ref, value_ref))
    ]
    for copy in copies:
        copy.start()

    def hand_on(index, carry):
        listed_ref[index] = selection_ref[index]
        return carry

    lax.fori_loop(0, selection_ref.shape[0], hand_on, 0)
    for copy in copies:
        copy.wait()

    def one_head(head, carry):
        columns = head_columns(head)
        key, value = held_ref[2, :, columns], held_ref[3, :, columns]
        for first in range(0, rows, TILE):
            tile = pl.ds(first, TILE)
            scores = causal(dot(key, held_ref[0, tile, columns], 1, 1), first)
            top = jnp.max(scores, axis=0, keepdims=True)
            raised = jnp.exp2((scores - top) * EXPONENT)
            product = raised * dot(value, held_ref[1, tile, columns], 1, 1)
            stats_ref[head, 0:1, tile] = top
            stats_ref[head, 1:2, tile] = jnp.sum(raised, axis=0, keepdims=True)
            stats_ref[head, 2:3, tile] = jnp.sum(product, axis=0, keepdims=True)
        return carry

    lax.fori_loop(0, heads, one_head, 0)


def far_kernel(
    selection_ref,
    position_ref,
    query_ref,
    grad_ref,
    listed_ref,
    own_stats_ref,
    terms_ref,
    part_ref,
    stats_ref,
    held_terms_ref,
    held_part_ref,
    sem,
    *scratch,
):
    heads, _, rows = own_stats_ref.shape
    chunks, _, _, chunk, _ = listed_ref.shape
    block = position_ref[0]
    sent = []

    def send(source, target, index):
        sent.append(pltpu.make_async_copy(source, target, sem.at[index]))
        sent[-1].start()

    def listed(which, head):
        return listed_ref[:, which, :, :, head_columns(head)].reshape(TOPK * rows, HEAD_DIM)

    def softmax(head):
        score_ref, grad_prob_ref, prob_ref, grad_score_ref = scratch[4 * head : 4 * head + 4]
        live = [
            selection_ref[(block * heads + head) * TOPK + slot] < block for slot in range(TOPK)
        ]
        shape = (chunks, TOPK, chunk, TILE)
        for first in range(0, rows, TILE):
            tile = pl.ds(first, TILE)
            scores = dot(listed(0, head), query_ref[tile, head_columns(head)], 1, 1)
            score_ref[:, :, :, tile] = scores.reshape(shape)
            grad_probs = dot(listed(1, head), grad_ref[tile, head_columns(head)], 1, 1)
            grad_prob_ref[:, :, :, tile] = grad_probs.reshape(shape)
            top = jnp.full((1, TILE), MASKED, jnp.float32)
            for slot in range(TOPK):
                highest = jnp.max(
                    score_ref[:, slot, :, tile].reshape(rows, TILE), axis=0, keepdims=True
                )
                top = jnp.maximum(top, jnp.where(live[slot], highest, MASKED))
            total = jnp.zeros((SUBLANES, TILE), jnp.float32)
            product = jnp.zeros_like(total)
            for slot in range(TOPK):
                shift = jnp.where(live[slot], top, -MASKED)
                for part in range(chunks):
                    raised = jnp.exp2((score_ref[part, slot, :, tile] - shift) * EXPONENT)
                    score_ref[part, slot, :, tile] = raised
                    total += fold(raised)
                    product += fold(raised * grad_prob_ref[part, slot, :, tile])
            total = jnp.sum(total, axis=0, keepdims=True)
            product = jnp.sum(product, axis=0, keepdims=True)
            own_top = own_stats_ref[head, 0:1, tile]
            highest = jnp.maximum(own_top, top)
            own_factor = jnp.exp2((own_top - highest) * EXPONENT)
            factor = jnp.exp2((top - highest) * EXPONENT)
            inverse = 1.0 / (own_factor * own_stats_ref[head, 1:2, tile] + factor * total)
            own_weight, weight = own_factor * inverse, factor * inverse
            delta = own_weight * own_stats_ref[head, 2:3, tile] + weight * product
            stats_ref[head, 0:1, tile] = own_weight
            stats_ref[head, 1:2, tile] = delta
            for slot in range(TOPK):
                for part in range(chunks):
                    probability = score_ref[part, slot, :, tile] * weight
                    prob_ref[part, slot, :, tile] = probability.astype(jnp.bfloat16)
                    grad_score_ref[part, slot, :, tile] = (
                        probability * (grad_prob_ref[part, slot, :, tile] - delta)
                    ).astype(jnp.bfloat16)

    def gradients(head):
        _, _, prob_ref, grad_score_ref = scratch[4 * head : 4 * head + 4]
        columns = head_columns(head)
        query, grad = query_ref[:, columns], grad_ref[:, columns]
        shape = (chunks, TOPK, chunk, HEAD_DIM)
        prob = prob_ref[...].reshape(TOPK * rows, rows)
        grad_scores = grad_score_ref[...].reshape(TOPK * rows, rows)
        held_part_ref[head] = dot(listed(0, head).T, grad_scores, 1, 0)
        send(held_part_ref.at[head], part_ref.at[head], 2 * head)
        grad_key = dot(grad_scores, query, 1, 0) * SCALING
        held_terms_ref[:, head, 0] = grad_key.astype(jnp.bfloat16).reshape(shape)
        grad_value = dot(prob, grad, 1, 0)
        held_terms_ref[:, head, 1] = grad_value.astype(jnp.bfloat16).reshape(shape)
        send(held_terms_ref.at[:, head], terms_ref.at[:, head], 2 * head + 1)

    for head in range(heads):
        softmax(head)
        gradients(head)
    for copy in sent:
        copy.wait()


def own_backward_kernel(
    place_ref,
    query_ref,
    key_ref,
    value_ref,
    grad_ref,
    part_ref,
    own_stats_ref,
    stats_ref,
    own_ref,
    *refs,
):
    piece_refs, (grad_query_ref, held_part_ref, sem) = refs[:-3], refs[-3:]
    heads, _, rows = stats_ref.shape
    fetch = pltpu.make_async_copy(part_ref, held_part_ref, sem)
    fetch.start()
    chunks, _, chunk, _ = own_ref.shape

    def one_head(head, carry):
        columns = head_columns(head)
        query, key = query_ref[:, columns], key_ref[:, columns]
        value, grad = value_ref[:, columns], grad_ref[:, columns]
        scores = causal(dot(key, query, 1, 1), 0)
        raised = jnp.exp2((scores - own_stats_ref[head, 0:1, :]) * EXPONENT)
        probability = raised * stats_ref[head, 0:1, :]
        grad_probs = dot(value, grad, 1, 1)
        grad_scores = (probability * (grad_probs - stats_ref[head, 1:2, :])).astype(jnp.bfloat16)
        pl.when(head == 0)(fetch.wait)
        grad_query = (held_part_ref[head] + dot(key.T, grad_scores, 1, 0)) * SCALING
        grad_query_ref[:, columns] = grad_query.T.astype(jnp.bfloat16)
        results = (
            dot(grad_scores, query, 1, 0) * SCALING,
            dot(probability.astype(jnp.bfloat16), grad, 1, 0),
        )
        for index, result in enumerate(results):
            own_ref[:, index, :, columns] = result.astype(jnp.bfloat16).reshape(
                chunks, chunk, HEAD_DIM
            )
        return carry

    lax.fori_loop(0, heads, one_head, 0)
    planes = len(piece_refs)
    plane = place_ref[1]
    length = rows // planes
    for step, piece_ref in enumerate(piece_refs):
        first = pl.multiple_of(((plane + step) % planes) * length, length)
        piece_ref[...] = grad_query_ref[pl.ds(first, length), :]


def join_kernel(place_ref, *refs):
    piece_refs, out_ref = refs[:-1], refs[-1]
    share = out_ref.shape[1]
    first = pl.multiple_of((1 - place_ref[2]) * share, share)
    for step, piece_ref in enumerate(piece_refs):
        out_ref[step] = piece_ref[pl.ds(first, share), :]


def finish_kernel(own_ref, others_ref, after_ref, out_ref):
    out_ref[...] = (
        others_ref[...].astype(jnp.float32) + own_ref[...].astype(jnp.float32)
    ).astype(jnp.bfloat16)


def lay_kernel(place_ref, parts_ref, other_ref, *refs):
    piece_refs, (query_ref, key_ref, value_ref, sem) = refs[:-4], refs[-4:]
    senders, _, share, width = parts_ref.shape
    planes = len(piece_refs)
    cores = senders // planes
    plane, core = place_ref[1], place_ref[2]
    copies = []

    def put(source, out, sender):
        first = sender * width
        if not isinstance(sender, int):
            first = pl.multiple_of(first, width)
        target = out.at[:, pl.ds(first, width)]
        copies.append(pltpu.make_async_copy(source, target, sem.at[len(copies)]))
        copies[-1].start()

    for step, piece_ref in enumerate(piece_refs):
        origin = (plane - step + planes) % planes
        rows = pl.ds(pl.multiple_of(core * share, share), share)
        put(piece_ref.at[rows], query_ref, origin * cores + core)
        if cores > 1:
            put(other_ref.at[step], query_ref, origin * cores + 1 - core)
    for sender in range(senders):
        put(parts_ref.at[sender, 0], key_ref, sender)
        put(parts_ref.at[sender, 1], value_ref, sender)
    for copy in copies:
        copy.wait()


def on_device(query_input, key_input, value_input, grad_output, selection):
    rows, width = query_input.shape
    heads = width // HEAD_DIM
    chain, spread = lax.axis_size("chain"), lax.axis_size("heads")
    chunk = rows // chain
    share = rows // spread
    listed = selection.reshape(-1)
    cores = 2 if spread % 2 == 0 else 1
    planes = spread // cores
    at = lax.axis_index("heads")
    position = jnp.stack([lax.axis_index("chain"), at // cores, at % cores]).astype(jnp.int32)
    smem = pl.BlockSpec(memory_space=pltpu.SMEM)
    vmem = pl.BlockSpec(memory_space=pltpu.VMEM)
    anywhere = pl.BlockSpec(memory_space=pl.ANY)
    low, full = jnp.bfloat16, jnp.float32

    def swap(array, axis):
        return lax.all_to_all(array, axis, split_axis=0, concat_axis=0, tiled=True)

    def call(kernel, name, in_specs, out_specs, out_shape, scratch=(), limit=4, slots=0):
        flops = 2 * heads * slots * rows * rows * HEAD_DIM
        return pl.pallas_call(
            kernel,
            out_shape=out_shape,
            in_specs=in_specs,
            out_specs=out_specs,
            scratch_shapes=list(scratch),
            cost_estimate=pl.CostEstimate(
                flops=flops, bytes_accessed=4 * MIB, transcendentals=heads * rows * rows
            ),
            compiler_params=pltpu.CompilerParams(vmem_limit_bytes=limit * MIB),
            name=name,
        )

    pair = call(
        stack_kernel,
        "stack",
        [anywhere] * 2,
        anywhere,
        jax.ShapeDtypeStruct((chain, 2, chunk, width), low),
        [
            pltpu.VMEM((2, chain, chunk, width), low),
            pltpu.SemaphoreType.DMA((2, 2)),
            pltpu.SemaphoreType.DMA((2, 2)),
        ],
        limit=59,
    )(key_input.reshape(chain, chunk, width), value_input.reshape(chain, chunk, width))
    held = swap(pair, "chain")
    listed, own_stats = call(
        own_forward_kernel,
        "own_forward",
        [smem] + [anywhere] * 4,
        (smem, vmem),
        (
            jax.ShapeDtypeStruct(listed.shape, jnp.int32),
            jax.ShapeDtypeStruct((heads, STATS, rows), full),
        ),
        [pltpu.VMEM((4, rows, width), low), pltpu.SemaphoreType.DMA((4,))],
        limit=16,
        slots=2,
    )(listed, query_input, key_input, value_input, grad_output)
    picked = call(
        pick_kernel,
        "pick",
        [smem, vmem],
        anywhere,
        jax.ShapeDtypeStruct((chain, 2, TOPK, chunk, width), low),
        [
            pltpu.VMEM((chain, 2, TOPK, chunk, width), low),
            pltpu.SemaphoreType.DMA((chain,)),
        ],
    )(listed, held)
    slots = swap(picked, "chain")
    terms, part, stats = call(
        far_kernel,
        "far",
        [smem, smem] + [vmem] * 4,
        (anywhere, anywhere, vmem),
        (
            jax.ShapeDtypeStruct((chain, heads, 2, TOPK, chunk, HEAD_DIM), low),
            jax.ShapeDtypeStruct((heads, HEAD_DIM, rows), full),
            jax.ShapeDtypeStruct((heads, STATS, rows), full),
        ),
        [
            pltpu.VMEM((chain, heads, 2, TOPK, chunk, HEAD_DIM), low),
            pltpu.VMEM((heads, HEAD_DIM, rows), full),
            pltpu.SemaphoreType.DMA((2 * heads,)),
        ]
        + [
            pltpu.VMEM((chain, TOPK, chunk, rows), full),
            pltpu.VMEM((chain, TOPK, chunk, rows), full),
            pltpu.VMEM((chain, TOPK, chunk, rows), low),
            pltpu.VMEM((chain, TOPK, chunk, rows), low),
        ]
        * heads,
        limit=32,
        slots=5 * TOPK,
    )(listed, position, query_input, grad_output, slots, own_stats)
    returned = swap(terms, "chain")
    own, *pieces = call(
        own_backward_kernel,
        "own_backward",
        [smem] + [vmem] * 4 + [anywhere] + [vmem] * 2,
        (vmem,) * (1 + planes),
        (jax.ShapeDtypeStruct((chain, 2, chunk, width), low),)
        + (jax.ShapeDtypeStruct((rows // planes, width), low),) * planes,
        [
            pltpu.VMEM((rows, width), low),
            pltpu.VMEM((heads, HEAD_DIM, rows), full),
            pltpu.SemaphoreType.DMA(()),
        ],
        limit=12,
        slots=5,
    )(position, query_input, key_input, value_input, grad_output, part, own_stats, stats)

    def to_plane(piece, step):
        if step == 0:
            return piece
        pairs = [(one, (one + step * cores) % spread) for one in range(spread)]
        return lax.ppermute(piece, "heads", pairs)

    order = sorted(range(planes), key=lambda step: -min(step, planes - step))
    for step in order:
        pieces[step] = to_plane(pieces[step], step)
    early = [pieces[step] for step in order[:EARLY]]
    summed = call(
        functools.partial(reduce_kernel, len(early)),
        "reduce",
        [smem, vmem] + [anywhere] * len(early),
        vmem,
        jax.ShapeDtypeStruct((chain, 2, chunk, width), low),
        [pltpu.VMEM((chain, 2, chunk, HEAD_DIM), full)] * heads,
    )(listed, returned, *early)
    joined = other = pieces[0]
    if cores > 1:
        joined = call(
            join_kernel,
            "join",
            [smem] + [vmem] * planes,
            vmem,
            jax.ShapeDtypeStruct((planes, share, width), low),
        )(position, *pieces)
        other = lax.ppermute(joined, "heads", [(one, one ^ 1) for one in range(spread)])
    others = swap(summed, "chain")

    def by_share(array):
        lead = array.shape[1:-2]
        array = array.reshape((spread, chain // spread) + lead + (chunk, width))
        return jnp.moveaxis(array, 1, -3).reshape((spread,) + lead + (share, width))

    whole = call(
        finish_kernel,
        "finish",
        [vmem] * 2 + [anywhere],
        vmem,
        jax.ShapeDtypeStruct((spread, 2, share, width), low),
    )(by_share(own), by_share(others), other)
    whole = swap(whole, "heads")
    return call(
        lay_kernel,
        "lay",
        [smem] + [vmem] * (2 + planes),
        (anywhere,) * 3,
        (jax.ShapeDtypeStruct((share, spread * width), low),) * 3,
        [pltpu.SemaphoreType.DMA((3 * spread,))],
    )(position, whole, other, *pieces)


def solution(mesh):
    in_specs = (
        P("chain", "heads"),
        P("chain", "heads"),
        P("chain", "heads"),
        P("chain", "heads"),
        P(None, "heads", None),
    )
    out_specs = (
        P(("chain", "heads"), None),
        P(("chain", "heads"), None),
        P(("chain", "heads"), None),
    )
    return jax.shard_map(
        on_device, mesh=mesh, in_specs=in_specs, out_specs=out_specs, check_vma=False
    )
```

```python
import functools
import math

import jax
import jax.numpy as jnp
from jax import lax
from jax.experimental import pallas as pl
from jax.experimental.pallas import tpu as pltpu
from jax.sharding import PartitionSpec as P

HEAD_DIM = 128
TOPK = 3
MASKED = -1e30
SCALING = HEAD_DIM ** (-0.5)
EXPONENT = SCALING * math.log2(math.e)
TILE = 256
STATS = 8
SUBLANES = 8
EARLY = 5
MIB = 1 << 20


def head_columns(head, offset=0):
    start = head * HEAD_DIM + offset
    if isinstance(head, int):
        return pl.ds(start, HEAD_DIM)
    return pl.ds(pl.multiple_of(start, HEAD_DIM), HEAD_DIM)


def dot(left, right, left_dim, right_dim):
    return lax.dot_general(
        left, right, (((left_dim,), (right_dim,)), ((), ())), preferred_element_type=jnp.float32
    )


def stack_kernel(key_ref, value_ref, out_ref, held_ref, in_sem, out_sem):
    pieces = in_sem.shape[1]
    length = key_ref.shape[0] // pieces
    arrive, leave = [], []
    for index, part in enumerate((key_ref, value_ref)):
        for piece in range(pieces):
            span = pl.ds(piece * length, length)
            held = held_ref.at[index, span]
            arrive.append(pltpu.make_async_copy(part.at[span], held, in_sem.at[index, piece]))
            leave.append(
                pltpu.make_async_copy(held, out_ref.at[span, index], out_sem.at[index, piece])
            )
    for copy in arrive:
        copy.start()
    for first, second in zip(arrive, leave):
        first.wait()
        second.start()
    for copy in leave:
        copy.wait()


def pick_kernel(selection_ref, held_ref, out_ref, filled_ref, sem):
    blocks, _, _, width = held_ref.shape
    heads = width // HEAD_DIM
    copies = []
    for block in range(blocks):
        filled_ref[block, :, 0] = held_ref[max(block - 1, 0)]
        for head in range(heads):
            columns = head_columns(head)
            for slot in range(1, TOPK):
                source = selection_ref[(block * heads + head) * TOPK + slot]
                filled_ref[block, :, slot, :, columns] = held_ref[source, :, :, columns]
        copies.append(
            pltpu.make_async_copy(filled_ref.at[block], out_ref.at[block], sem.at[block])
        )
        copies[-1].start()
    for copy in copies:
        copy.wait()


def reduce_kernel(after, selection_ref, terms_ref, *refs):
    out_ref, total_refs = refs[after], refs[after + 1 :]
    blocks, _, _, width = out_ref.shape
    heads = width // HEAD_DIM
    for head, total_ref in enumerate(total_refs):
        total_ref[: blocks - 1] = terms_ref[1:, head, :, 0].astype(jnp.float32)
        total_ref[blocks - 1] = jnp.zeros_like(total_ref[blocks - 1])
    for block in range(blocks):
        for slot in range(1, TOPK):
            for head, total_ref in enumerate(total_refs):
                target = selection_ref[(block * heads + head) * TOPK + slot]
                total_ref[target] += terms_ref[block, head, :, slot].astype(jnp.float32)
    for head, total_ref in enumerate(total_refs):
        out_ref[:, :, :, head_columns(head)] = total_ref[...].astype(out_ref.dtype)


def fold(array):
    return jnp.sum(array.reshape(-1, SUBLANES, array.shape[1]), axis=0)


def causal(scores, first):
    key_at = lax.broadcasted_iota(jnp.int32, scores.shape, 0)
    query_at = lax.broadcasted_iota(jnp.int32, scores.shape, 1) + first
    return jnp.where(key_at <= query_at, scores, MASKED)


def own_forward_kernel(
    selection_ref,
    query_ref,
    key_ref,
    value_ref,
    grad_ref,
    listed_ref,
    stats_ref,
    held_ref,
    sem,
):
    heads, _, rows = stats_ref.shape
    copies = [
        pltpu.make_async_copy(source, held_ref.at[index], sem.at[index])
        for index, source in enumerate((query_ref, grad_ref, key_ref, value_ref))
    ]
    for copy in copies:
        copy.start()

    def hand_on(index, carry):
        listed_ref[index] = selection_ref[index]
        return carry

    lax.fori_loop(0, selection_ref.shape[0], hand_on, 0)
    for copy in copies:
        copy.wait()

    def one_head(head, carry):
        columns = head_columns(head)
        key, value = held_ref[2, :, columns], held_ref[3, :, columns]
        for first in range(0, rows, TILE):
            tile = pl.ds(first, TILE)
            scores = causal(dot(key, held_ref[0, tile, columns], 1, 1), first)
            top = jnp.max(scores, axis=0, keepdims=True)
            raised = jnp.exp2((scores - top) * EXPONENT)
            product = raised * dot(value, held_ref[1, tile, columns], 1, 1)
            stats_ref[head, 0:1, tile] = top
            stats_ref[head, 1:2, tile] = jnp.sum(raised, axis=0, keepdims=True)
            stats_ref[head, 2:3, tile] = jnp.sum(product, axis=0, keepdims=True)
        return carry

    lax.fori_loop(0, heads, one_head, 0)


def far_kernel(
    selection_ref,
    position_ref,
    query_ref,
    grad_ref,
    listed_ref,
    own_stats_ref,
    terms_ref,
    part_ref,
    stats_ref,
    *scratch,
):
    heads, _, rows = own_stats_ref.shape
    chunks, _, _, chunk, _ = listed_ref.shape
    block = position_ref[0]
    def listed(which, head):
        return listed_ref[:, which, :, :, head_columns(head)].reshape(TOPK * rows, HEAD_DIM)

    def softmax(head):
        score_ref, grad_prob_ref, prob_ref, grad_score_ref = scratch[4 * head : 4 * head + 4]
        live = [
            selection_ref[(block * heads + head) * TOPK + slot] < block for slot in range(TOPK)
        ]
        shape = (chunks, TOPK, chunk, TILE)
        for first in range(0, rows, TILE):
            tile = pl.ds(first, TILE)
            scores = dot(listed(0, head), query_ref[tile, head_columns(head)], 1, 1)
            score_ref[:, :, :, tile] = scores.reshape(shape)
            grad_probs = dot(listed(1, head), grad_ref[tile, head_columns(head)], 1, 1)
            grad_prob_ref[:, :, :, tile] = grad_probs.reshape(shape)
            top = jnp.full((1, TILE), MASKED, jnp.float32)
            for slot in range(TOPK):
                highest = jnp.max(
                    score_ref[:, slot, :, tile].reshape(rows, TILE), axis=0, keepdims=True
                )
                top = jnp.maximum(top, jnp.where(live[slot], highest, MASKED))
            total = jnp.zeros((SUBLANES, TILE), jnp.float32)
            product = jnp.zeros_like(total)
            for slot in range(TOPK):
                shift = jnp.where(live[slot], top, -MASKED)
                for part in range(chunks):
                    raised = jnp.exp2((score_ref[part, slot, :, tile] - shift) * EXPONENT)
                    score_ref[part, slot, :, tile] = raised
                    total += fold(raised)
                    product += fold(raised * grad_prob_ref[part, slot, :, tile])
            total = jnp.sum(total, axis=0, keepdims=True)
            product = jnp.sum(product, axis=0, keepdims=True)
            own_top = own_stats_ref[head, 0:1, tile]
            highest = jnp.maximum(own_top, top)
            own_factor = jnp.exp2((own_top - highest) * EXPONENT)
            factor = jnp.exp2((top - highest) * EXPONENT)
            inverse = 1.0 / (own_factor * own_stats_ref[head, 1:2, tile] + factor * total)
            own_weight, weight = own_factor * inverse, factor * inverse
            delta = own_weight * own_stats_ref[head, 2:3, tile] + weight * product
            stats_ref[head, 0:1, tile] = own_weight
            stats_ref[head, 1:2, tile] = delta
            for slot in range(TOPK):
                for part in range(chunks):
                    probability = score_ref[part, slot, :, tile] * weight
                    prob_ref[part, slot, :, tile] = probability.astype(jnp.bfloat16)
                    grad_score_ref[part, slot, :, tile] = (
                        probability * (grad_prob_ref[part, slot, :, tile] - delta)
                    ).astype(jnp.bfloat16)

    def gradients(head):
        _, _, prob_ref, grad_score_ref = scratch[4 * head : 4 * head + 4]
        columns = head_columns(head)
        query, grad = query_ref[:, columns], grad_ref[:, columns]
        shape = (chunks, TOPK, chunk, HEAD_DIM)
        prob = prob_ref[...].reshape(TOPK * rows, rows)
        grad_scores = grad_score_ref[...].reshape(TOPK * rows, rows)
        grad_key = dot(grad_scores, query, 1, 0) * SCALING
        terms_ref[:, head, 0] = grad_key.astype(jnp.bfloat16).reshape(shape)
        grad_value = dot(prob, grad, 1, 0)
        terms_ref[:, head, 1] = grad_value.astype(jnp.bfloat16).reshape(shape)
        part_ref[head] = dot(listed(0, head).T, grad_scores, 1, 0).astype(jnp.bfloat16)

    for head in range(heads):
        softmax(head)
        gradients(head)


def own_backward_kernel(
    place_ref,
    query_ref,
    key_ref,
    value_ref,
    grad_ref,
    part_ref,
    own_stats_ref,
    stats_ref,
    own_ref,
    *refs,
):
    piece_refs, grad_query_ref = refs[:-1], refs[-1]
    heads, _, rows = stats_ref.shape
    chunks, _, chunk, _ = own_ref.shape

    def one_head(head, carry):
        columns = head_columns(head)
        query, key = query_ref[:, columns], key_ref[:, columns]
        value, grad = value_ref[:, columns], grad_ref[:, columns]
        scores = causal(dot(key, query, 1, 1), 0)
        raised = jnp.exp2((scores - own_stats_ref[head, 0:1, :]) * EXPONENT)
        probability = raised * stats_ref[head, 0:1, :]
        grad_probs = dot(value, grad, 1, 1)
        grad_scores = (probability * (grad_probs - stats_ref[head, 1:2, :])).astype(jnp.bfloat16)
        grad_query = dot(key.T, grad_scores, 1, 0) + part_ref[head].astype(jnp.float32)
        grad_query = grad_query * SCALING
        grad_query_ref[:, columns] = grad_query.T.astype(jnp.bfloat16)
        results = (
            dot(grad_scores, query, 1, 0) * SCALING,
            dot(probability.astype(jnp.bfloat16), grad, 1, 0),
        )
        for index, result in enumerate(results):
            own_ref[:, index, :, columns] = result.astype(jnp.bfloat16).reshape(
                chunks, chunk, HEAD_DIM
            )
        return carry

    lax.fori_loop(0, heads, one_head, 0)
    planes = len(piece_refs)
    plane = place_ref[1]
    length = rows // planes
    for step, piece_ref in enumerate(piece_refs):
        first = pl.multiple_of(((plane + step) % planes) * length, length)
        piece_ref[...] = grad_query_ref[pl.ds(first, length), :]


def join_kernel(place_ref, *refs):
    piece_refs, out_ref = refs[:-1], refs[-1]
    share = out_ref.shape[1]
    first = pl.multiple_of((1 - place_ref[2]) * share, share)
    for step, piece_ref in enumerate(piece_refs):
        out_ref[step] = piece_ref[pl.ds(first, share), :]


def finish_kernel(own_ref, others_ref, after_ref, out_ref):
    out_ref[...] = (
        others_ref[...].astype(jnp.float32) + own_ref[...].astype(jnp.float32)
    ).astype(jnp.bfloat16)


def lay_kernel(place_ref, parts_ref, other_ref, *refs):
    piece_refs, (query_ref, key_ref, value_ref, sem) = refs[:-4], refs[-4:]
    senders, _, share, width = parts_ref.shape
    planes = len(piece_refs)
    cores = senders // planes
    plane, core = place_ref[1], place_ref[2]
    copies = []

    def put(source, out, sender):
        first = sender * width
        if not isinstance(sender, int):
            first = pl.multiple_of(first, width)
        target = out.at[:, pl.ds(first, width)]
        copies.append(pltpu.make_async_copy(source, target, sem.at[len(copies)]))
        copies[-1].start()

    for step, piece_ref in enumerate(piece_refs):
        origin = (plane - step + planes) % planes
        rows = pl.ds(pl.multiple_of(core * share, share), share)
        put(piece_ref.at[rows], query_ref, origin * cores + core)
        if cores > 1:
            put(other_ref.at[step], query_ref, origin * cores + 1 - core)
    for sender in range(senders):
        put(parts_ref.at[sender, 0], key_ref, sender)
        put(parts_ref.at[sender, 1], value_ref, sender)
    for copy in copies:
        copy.wait()


def on_device(query_input, key_input, value_input, grad_output, selection):
    rows, width = query_input.shape
    heads = width // HEAD_DIM
    chain, spread = lax.axis_size("chain"), lax.axis_size("heads")
    chunk = rows // chain
    share = rows // spread
    listed = selection.reshape(-1)
    cores = 2 if spread % 2 == 0 else 1
    planes = spread // cores
    at = lax.axis_index("heads")
    position = jnp.stack([lax.axis_index("chain"), at // cores, at % cores]).astype(jnp.int32)
    smem = pl.BlockSpec(memory_space=pltpu.SMEM)
    vmem = pl.BlockSpec(memory_space=pltpu.VMEM)
    anywhere = pl.BlockSpec(memory_space=pl.ANY)
    low, full = jnp.bfloat16, jnp.float32

    def swap(array, axis):
        return lax.all_to_all(array, axis, split_axis=0, concat_axis=0, tiled=True)

    def call(kernel, name, in_specs, out_specs, out_shape, scratch=(), limit=4, slots=0):
        flops = 2 * heads * slots * rows * rows * HEAD_DIM
        return pl.pallas_call(
            kernel,
            out_shape=out_shape,
            in_specs=in_specs,
            out_specs=out_specs,
            scratch_shapes=list(scratch),
            cost_estimate=pl.CostEstimate(
                flops=flops, bytes_accessed=4 * MIB, transcendentals=heads * rows * rows
            ),
            compiler_params=pltpu.CompilerParams(vmem_limit_bytes=limit * MIB),
            name=name,
        )

    pair = call(
        stack_kernel,
        "stack",
        [anywhere] * 2,
        anywhere,
        jax.ShapeDtypeStruct((chain, 2, chunk, width), low),
        [
            pltpu.VMEM((2, chain, chunk, width), low),
            pltpu.SemaphoreType.DMA((2, 2)),
            pltpu.SemaphoreType.DMA((2, 2)),
        ],
        limit=59,
    )(key_input.reshape(chain, chunk, width), value_input.reshape(chain, chunk, width))
    held = swap(pair, "chain")
    listed, own_stats = call(
        own_forward_kernel,
        "own_forward",
        [smem] + [anywhere] * 4,
        (smem, vmem),
        (
            jax.ShapeDtypeStruct(listed.shape, jnp.int32),
            jax.ShapeDtypeStruct((heads, STATS, rows), full),
        ),
        [pltpu.VMEM((4, rows, width), low), pltpu.SemaphoreType.DMA((4,))],
        limit=16,
        slots=2,
    )(listed, query_input, key_input, value_input, grad_output)
    picked = call(
        pick_kernel,
        "pick",
        [smem, vmem],
        anywhere,
        jax.ShapeDtypeStruct((chain, 2, TOPK, chunk, width), low),
        [
            pltpu.VMEM((chain, 2, TOPK, chunk, width), low),
            pltpu.SemaphoreType.DMA((chain,)),
        ],
    )(listed, held)
    slots = swap(picked, "chain")
    terms, part, stats = call(
        far_kernel,
        "far",
        [smem, smem] + [vmem] * 4,
        (vmem, vmem, vmem),
        (
            jax.ShapeDtypeStruct((chain, heads, 2, TOPK, chunk, HEAD_DIM), low),
            jax.ShapeDtypeStruct((heads, HEAD_DIM, rows), low),
            jax.ShapeDtypeStruct((heads, STATS, rows), full),
        ),
        [
            pltpu.VMEM((chain, TOPK, chunk, rows), full),
            pltpu.VMEM((chain, TOPK, chunk, rows), full),
            pltpu.VMEM((chain, TOPK, chunk, rows), low),
            pltpu.VMEM((chain, TOPK, chunk, rows), low),
        ]
        * heads,
        limit=32,
        slots=5 * TOPK,
    )(listed, position, query_input, grad_output, slots, own_stats)
    returned = swap(terms, "chain")
    own, *pieces = call(
        own_backward_kernel,
        "own_backward",
        [smem] + [vmem] * 7,
        (vmem,) * (1 + planes),
        (jax.ShapeDtypeStruct((chain, 2, chunk, width), low),)
        + (jax.ShapeDtypeStruct((rows // planes, width), low),) * planes,
        [pltpu.VMEM((rows, width), low)],
        limit=12,
        slots=5,
    )(position, query_input, key_input, value_input, grad_output, part, own_stats, stats)

    def to_plane(piece, step):
        if step == 0:
            return piece
        pairs = [(one, (one + step * cores) % spread) for one in range(spread)]
        return lax.ppermute(piece, "heads", pairs)

    order = sorted(range(planes), key=lambda step: -min(step, planes - step))
    for step in order:
        pieces[step] = to_plane(pieces[step], step)
    early = [pieces[step] for step in order[:EARLY]]
    summed = call(
        functools.partial(reduce_kernel, len(early)),
        "reduce",
        [smem, vmem] + [anywhere] * len(early),
        vmem,
        jax.ShapeDtypeStruct((chain, 2, chunk, width), low),
        [pltpu.VMEM((chain, 2, chunk, HEAD_DIM), full)] * heads,
    )(listed, returned, *early)
    joined = other = pieces[0]
    if cores > 1:
        joined = call(
            join_kernel,
            "join",
            [smem] + [vmem] * planes,
            vmem,
            jax.ShapeDtypeStruct((planes, share, width), low),
        )(position, *pieces)
        other = lax.ppermute(joined, "heads", [(one, one ^ 1) for one in range(spread)])
    others = swap(summed, "chain")

    def by_share(array):
        lead = array.shape[1:-2]
        array = array.reshape((spread, chain // spread) + lead + (chunk, width))
        return jnp.moveaxis(array, 1, -3).reshape((spread,) + lead + (share, width))

    whole = call(
        finish_kernel,
        "finish",
        [vmem] * 2 + [anywhere],
        vmem,
        jax.ShapeDtypeStruct((spread, 2, share, width), low),
    )(by_share(own), by_share(others), other)
    whole = swap(whole, "heads")
    return call(
        lay_kernel,
        "lay",
        [smem] + [vmem] * (2 + planes),
        (anywhere,) * 3,
        (jax.ShapeDtypeStruct((share, spread * width), low),) * 3,
        [pltpu.SemaphoreType.DMA((3 * spread,))],
    )(position, whole, other, *pieces)


def solution(mesh):
    in_specs = (
        P("chain", "heads"),
        P("chain", "heads"),
        P("chain", "heads"),
        P("chain", "heads"),
        P(None, "heads", None),
    )
    out_specs = (
        P(("chain", "heads"), None),
        P(("chain", "heads"), None),
        P(("chain", "heads"), None),
    )
    return jax.shard_map(
        on_device, mesh=mesh, in_specs=in_specs, out_specs=out_specs, check_vma=False
    )
```

```python
import functools
import math

import jax
import jax.numpy as jnp
from jax import lax
from jax.experimental import pallas as pl
from jax.experimental.pallas import tpu as pltpu
from jax.sharding import PartitionSpec as P

HEAD_DIM = 128
TOPK = 3
MASKED = -1e30
SCALING = HEAD_DIM ** (-0.5)
EXPONENT = SCALING * math.log2(math.e)
TILE = 256
STATS = 8
SUBLANES = 8
EARLY = 6
MIB = 1 << 20


def head_columns(head, offset=0):
    start = head * HEAD_DIM + offset
    if isinstance(head, int):
        return pl.ds(start, HEAD_DIM)
    return pl.ds(pl.multiple_of(start, HEAD_DIM), HEAD_DIM)


def dot(left, right, left_dim, right_dim):
    return lax.dot_general(
        left, right, (((left_dim,), (right_dim,)), ((), ())), preferred_element_type=jnp.float32
    )


def stack_kernel(key_ref, value_ref, out_ref, held_ref, in_sem, out_sem):
    pieces = in_sem.shape[1]
    length = key_ref.shape[0] // pieces
    arrive, leave = [], []
    for index, part in enumerate((key_ref, value_ref)):
        for piece in range(pieces):
            span = pl.ds(piece * length, length)
            held = held_ref.at[index, span]
            arrive.append(pltpu.make_async_copy(part.at[span], held, in_sem.at[index, piece]))
            leave.append(
                pltpu.make_async_copy(held, out_ref.at[span, index], out_sem.at[index, piece])
            )
    for copy in arrive:
        copy.start()
    for first, second in zip(arrive, leave):
        first.wait()
        second.start()
    for copy in leave:
        copy.wait()


def pick_kernel(selection_ref, held_ref, out_ref, filled_ref, sem):
    blocks, _, _, width = held_ref.shape
    heads = width // HEAD_DIM
    copies = []
    for block in range(blocks):
        filled_ref[block, :, 0] = held_ref[max(block - 1, 0)]
        for head in range(heads):
            columns = head_columns(head)
            for slot in range(1, TOPK):
                source = selection_ref[(block * heads + head) * TOPK + slot]
                filled_ref[block, :, slot, :, columns] = held_ref[source, :, :, columns]
        copies.append(
            pltpu.make_async_copy(filled_ref.at[block], out_ref.at[block], sem.at[block])
        )
        copies[-1].start()
    for copy in copies:
        copy.wait()


def reduce_kernel(after, selection_ref, terms_ref, *refs):
    out_ref, total_refs = refs[after], refs[after + 1 :]
    blocks, _, _, width = out_ref.shape
    heads = width // HEAD_DIM
    for head, total_ref in enumerate(total_refs):
        total_ref[: blocks - 1] = terms_ref[1:, head, :, 0].astype(jnp.float32)
        total_ref[blocks - 1] = jnp.zeros_like(total_ref[blocks - 1])
    for block in range(blocks):
        for slot in range(1, TOPK):
            for head, total_ref in enumerate(total_refs):
                target = selection_ref[(block * heads + head) * TOPK + slot]
                total_ref[target] += terms_ref[block, head, :, slot].astype(jnp.float32)
    for head, total_ref in enumerate(total_refs):
        out_ref[:, :, :, head_columns(head)] = total_ref[...].astype(out_ref.dtype)


def fold(array):
    return jnp.sum(array.reshape(-1, SUBLANES, array.shape[1]), axis=0)


def causal(scores, first):
    key_at = lax.broadcasted_iota(jnp.int32, scores.shape, 0)
    query_at = lax.broadcasted_iota(jnp.int32, scores.shape, 1) + first
    return jnp.where(key_at <= query_at, scores, MASKED)


def own_forward_kernel(
    selection_ref,
    query_ref,
    key_ref,
    value_ref,
    grad_ref,
    listed_ref,
    stats_ref,
    held_ref,
    sem,
):
    heads, _, rows = stats_ref.shape
    copies = [
        pltpu.make_async_copy(source, held_ref.at[index], sem.at[index])
        for index, source in enumerate((query_ref, grad_ref, key_ref, value_ref))
    ]
    for copy in copies:
        copy.start()

    def hand_on(index, carry):
        listed_ref[index] = selection_ref[index]
        return carry

    lax.fori_loop(0, selection_ref.shape[0], hand_on, 0)
    for copy in copies:
        copy.wait()

    def one_head(head, carry):
        columns = head_columns(head)
        key, value = held_ref[2, :, columns], held_ref[3, :, columns]
        for first in range(0, rows, TILE):
            tile = pl.ds(first, TILE)
            scores = causal(dot(key, held_ref[0, tile, columns], 1, 1), first)
            top = jnp.max(scores, axis=0, keepdims=True)
            raised = jnp.exp2((scores - top) * EXPONENT)
            product = raised * dot(value, held_ref[1, tile, columns], 1, 1)
            stats_ref[head, 0:1, tile] = top
            stats_ref[head, 1:2, tile] = jnp.sum(raised, axis=0, keepdims=True)
            stats_ref[head, 2:3, tile] = jnp.sum(product, axis=0, keepdims=True)
        return carry

    lax.fori_loop(0, heads, one_head, 0)


def far_kernel(
    selection_ref,
    position_ref,
    query_ref,
    grad_ref,
    listed_ref,
    own_stats_ref,
    terms_ref,
    part_ref,
    stats_ref,
    *scratch,
):
    heads, _, rows = own_stats_ref.shape
    chunks, _, _, chunk, _ = listed_ref.shape
    block = position_ref[0]
    def listed(which, head):
        return listed_ref[:, which, :, :, head_columns(head)].reshape(TOPK * rows, HEAD_DIM)

    def softmax(head):
        score_ref, grad_prob_ref, prob_ref, grad_score_ref = scratch[4 * head : 4 * head + 4]
        live = [
            selection_ref[(block * heads + head) * TOPK + slot] < block for slot in range(TOPK)
        ]
        shape = (chunks, TOPK, chunk, TILE)
        for first in range(0, rows, TILE):
            tile = pl.ds(first, TILE)
            scores = dot(listed(0, head), query_ref[tile, head_columns(head)], 1, 1)
            score_ref[:, :, :, tile] = scores.reshape(shape)
            grad_probs = dot(listed(1, head), grad_ref[tile, head_columns(head)], 1, 1)
            grad_prob_ref[:, :, :, tile] = grad_probs.reshape(shape)
            top = jnp.full((1, TILE), MASKED, jnp.float32)
            for slot in range(TOPK):
                highest = jnp.max(
                    score_ref[:, slot, :, tile].reshape(rows, TILE), axis=0, keepdims=True
                )
                top = jnp.maximum(top, jnp.where(live[slot], highest, MASKED))
            total = jnp.zeros((SUBLANES, TILE), jnp.float32)
            product = jnp.zeros_like(total)
            for slot in range(TOPK):
                shift = jnp.where(live[slot], top, -MASKED)
                for part in range(chunks):
                    raised = jnp.exp2((score_ref[part, slot, :, tile] - shift) * EXPONENT)
                    score_ref[part, slot, :, tile] = raised
                    total += fold(raised)
                    product += fold(raised * grad_prob_ref[part, slot, :, tile])
            total = jnp.sum(total, axis=0, keepdims=True)
            product = jnp.sum(product, axis=0, keepdims=True)
            own_top = own_stats_ref[head, 0:1, tile]
            highest = jnp.maximum(own_top, top)
            own_factor = jnp.exp2((own_top - highest) * EXPONENT)
            factor = jnp.exp2((top - highest) * EXPONENT)
            inverse = 1.0 / (own_factor * own_stats_ref[head, 1:2, tile] + factor * total)
            own_weight, weight = own_factor * inverse, factor * inverse
            delta = own_weight * own_stats_ref[head, 2:3, tile] + weight * product
            stats_ref[head, 0:1, tile] = own_weight
            stats_ref[head, 1:2, tile] = delta
            for slot in range(TOPK):
                for part in range(chunks):
                    probability = score_ref[part, slot, :, tile] * weight
                    prob_ref[part, slot, :, tile] = probability.astype(jnp.bfloat16)
                    grad_score_ref[part, slot, :, tile] = (
                        probability * (grad_prob_ref[part, slot, :, tile] - delta)
                    ).astype(jnp.bfloat16)

    def gradients(head):
        _, _, prob_ref, grad_score_ref = scratch[4 * head : 4 * head + 4]
        columns = head_columns(head)
        query, grad = query_ref[:, columns], grad_ref[:, columns]
        shape = (chunks, TOPK, chunk, HEAD_DIM)
        prob = prob_ref[...].reshape(TOPK * rows, rows)
        grad_scores = grad_score_ref[...].reshape(TOPK * rows, rows)
        grad_key = dot(grad_scores, query, 1, 0) * SCALING
        terms_ref[:, head, 0] = grad_key.astype(jnp.bfloat16).reshape(shape)
        grad_value = dot(prob, grad, 1, 0)
        terms_ref[:, head, 1] = grad_value.astype(jnp.bfloat16).reshape(shape)
        part_ref[head] = dot(listed(0, head).T, grad_scores, 1, 0).astype(jnp.bfloat16)

    for head in range(heads):
        softmax(head)
        gradients(head)


def own_backward_kernel(
    place_ref,
    query_ref,
    key_ref,
    value_ref,
    grad_ref,
    part_ref,
    own_stats_ref,
    stats_ref,
    own_ref,
    *refs,
):
    piece_refs, grad_query_ref = refs[:-1], refs[-1]
    heads, _, rows = stats_ref.shape
    chunks, _, chunk, _ = own_ref.shape

    def one_head(head, carry):
        columns = head_columns(head)
        query, key = query_ref[:, columns], key_ref[:, columns]
        value, grad = value_ref[:, columns], grad_ref[:, columns]
        scores = causal(dot(key, query, 1, 1), 0)
        raised = jnp.exp2((scores - own_stats_ref[head, 0:1, :]) * EXPONENT)
        probability = raised * stats_ref[head, 0:1, :]
        grad_probs = dot(value, grad, 1, 1)
        grad_scores = (probability * (grad_probs - stats_ref[head, 1:2, :])).astype(jnp.bfloat16)
        grad_query = dot(key.T, grad_scores, 1, 0) + part_ref[head].astype(jnp.float32)
        grad_query = grad_query * SCALING
        grad_query_ref[:, columns] = grad_query.T.astype(jnp.bfloat16)
        results = (
            dot(grad_scores, query, 1, 0) * SCALING,
            dot(probability.astype(jnp.bfloat16), grad, 1, 0),
        )
        for index, result in enumerate(results):
            own_ref[:, index, :, columns] = result.astype(jnp.bfloat16).reshape(
                chunks, chunk, HEAD_DIM
            )
        return carry

    lax.fori_loop(0, heads, one_head, 0)
    planes = len(piece_refs)
    plane = place_ref[1]
    length = rows // planes
    for step, piece_ref in enumerate(piece_refs):
        first = pl.multiple_of(((plane + step) % planes) * length, length)
        piece_ref[...] = grad_query_ref[pl.ds(first, length), :]


def join_kernel(place_ref, *refs):
    piece_refs, out_ref = refs[:-1], refs[-1]
    share = out_ref.shape[1]
    first = pl.multiple_of((1 - place_ref[2]) * share, share)
    for step, piece_ref in enumerate(piece_refs):
        out_ref[step] = piece_ref[pl.ds(first, share), :]


def finish_kernel(own_ref, others_ref, after_ref, out_ref):
    out_ref[...] = (
        others_ref[...].astype(jnp.float32) + own_ref[...].astype(jnp.float32)
    ).astype(jnp.bfloat16)


def lay_kernel(place_ref, parts_ref, other_ref, *refs):
    piece_refs, (query_ref, key_ref, value_ref, sem) = refs[:-4], refs[-4:]
    senders, _, share, width = parts_ref.shape
    planes = len(piece_refs)
    cores = senders // planes
    plane, core = place_ref[1], place_ref[2]
    copies = []

    def put(source, out, sender):
        first = sender * width
        if not isinstance(sender, int):
            first = pl.multiple_of(first, width)
        target = out.at[:, pl.ds(first, width)]
        copies.append(pltpu.make_async_copy(source, target, sem.at[len(copies)]))
        copies[-1].start()

    for step, piece_ref in enumerate(piece_refs):
        origin = (plane - step + planes) % planes
        rows = pl.ds(pl.multiple_of(core * share, share), share)
        put(piece_ref.at[rows], query_ref, origin * cores + core)
        if cores > 1:
            put(other_ref.at[step], query_ref, origin * cores + 1 - core)
    for sender in range(senders):
        put(parts_ref.at[sender, 0], key_ref, sender)
        put(parts_ref.at[sender, 1], value_ref, sender)
    for copy in copies:
        copy.wait()


def on_device(query_input, key_input, value_input, grad_output, selection):
    rows, width = query_input.shape
    heads = width // HEAD_DIM
    chain, spread = lax.axis_size("chain"), lax.axis_size("heads")
    chunk = rows // chain
    share = rows // spread
    listed = selection.reshape(-1)
    cores = 2 if spread % 2 == 0 else 1
    planes = spread // cores
    at = lax.axis_index("heads")
    position = jnp.stack([lax.axis_index("chain"), at // cores, at % cores]).astype(jnp.int32)
    smem = pl.BlockSpec(memory_space=pltpu.SMEM)
    vmem = pl.BlockSpec(memory_space=pltpu.VMEM)
    anywhere = pl.BlockSpec(memory_space=pl.ANY)
    low, full = jnp.bfloat16, jnp.float32

    def swap(array, axis):
        return lax.all_to_all(array, axis, split_axis=0, concat_axis=0, tiled=True)

    def call(kernel, name, in_specs, out_specs, out_shape, scratch=(), limit=4, slots=0):
        flops = 2 * heads * slots * rows * rows * HEAD_DIM
        return pl.pallas_call(
            kernel,
            out_shape=out_shape,
            in_specs=in_specs,
            out_specs=out_specs,
            scratch_shapes=list(scratch),
            cost_estimate=pl.CostEstimate(
                flops=flops, bytes_accessed=4 * MIB, transcendentals=heads * rows * rows
            ),
            compiler_params=pltpu.CompilerParams(vmem_limit_bytes=limit * MIB),
            name=name,
        )

    pair = call(
        stack_kernel,
        "stack",
        [anywhere] * 2,
        anywhere,
        jax.ShapeDtypeStruct((chain, 2, chunk, width), low),
        [
            pltpu.VMEM((2, chain, chunk, width), low),
            pltpu.SemaphoreType.DMA((2, 2)),
            pltpu.SemaphoreType.DMA((2, 2)),
        ],
        limit=59,
    )(key_input.reshape(chain, chunk, width), value_input.reshape(chain, chunk, width))
    held = swap(pair, "chain")
    listed, own_stats = call(
        own_forward_kernel,
        "own_forward",
        [smem] + [anywhere] * 4,
        (smem, vmem),
        (
            jax.ShapeDtypeStruct(listed.shape, jnp.int32),
            jax.ShapeDtypeStruct((heads, STATS, rows), full),
        ),
        [pltpu.VMEM((4, rows, width), low), pltpu.SemaphoreType.DMA((4,))],
        limit=16,
        slots=2,
    )(listed, query_input, key_input, value_input, grad_output)
    picked = call(
        pick_kernel,
        "pick",
        [smem, vmem],
        anywhere,
        jax.ShapeDtypeStruct((chain, 2, TOPK, chunk, width), low),
        [
            pltpu.VMEM((chain, 2, TOPK, chunk, width), low),
            pltpu.SemaphoreType.DMA((chain,)),
        ],
    )(listed, held)
    slots = swap(picked, "chain")
    terms, part, stats = call(
        far_kernel,
        "far",
        [smem, smem] + [vmem] * 4,
        (vmem, vmem, vmem),
        (
            jax.ShapeDtypeStruct((chain, heads, 2, TOPK, chunk, HEAD_DIM), low),
            jax.ShapeDtypeStruct((heads, HEAD_DIM, rows), low),
            jax.ShapeDtypeStruct((heads, STATS, rows), full),
        ),
        [
            pltpu.VMEM((chain, TOPK, chunk, rows), full),
            pltpu.VMEM((chain, TOPK, chunk, rows), full),
            pltpu.VMEM((chain, TOPK, chunk, rows), low),
            pltpu.VMEM((chain, TOPK, chunk, rows), low),
        ]
        * heads,
        limit=32,
        slots=5 * TOPK,
    )(listed, position, query_input, grad_output, slots, own_stats)
    returned = swap(terms, "chain")
    own, *pieces = call(
        own_backward_kernel,
        "own_backward",
        [smem] + [vmem] * 7,
        (vmem,) * (1 + planes),
        (jax.ShapeDtypeStruct((chain, 2, chunk, width), low),)
        + (jax.ShapeDtypeStruct((rows // planes, width), low),) * planes,
        [pltpu.VMEM((rows, width), low)],
        limit=12,
        slots=5,
    )(position, query_input, key_input, value_input, grad_output, part, own_stats, stats)

    def to_plane(piece, step):
        if step == 0:
            return piece
        pairs = [(one, (one + step * cores) % spread) for one in range(spread)]
        return lax.ppermute(piece, "heads", pairs)

    order = sorted(range(planes), key=lambda step: -min(step, planes - step))
    for step in order:
        pieces[step] = to_plane(pieces[step], step)
    early = [pieces[step] for step in order[:EARLY]]
    summed = call(
        functools.partial(reduce_kernel, len(early)),
        "reduce",
        [smem, vmem] + [anywhere] * len(early),
        vmem,
        jax.ShapeDtypeStruct((chain, 2, chunk, width), low),
        [pltpu.VMEM((chain, 2, chunk, HEAD_DIM), full)] * heads,
    )(listed, returned, *early)
    joined = other = pieces[0]
    if cores > 1:
        joined = call(
            join_kernel,
            "join",
            [smem] + [vmem] * planes,
            vmem,
            jax.ShapeDtypeStruct((planes, share, width), low),
        )(position, *pieces)
        other = lax.ppermute(joined, "heads", [(one, one ^ 1) for one in range(spread)])
    others = swap(summed, "chain")

    def by_share(array):
        lead = array.shape[1:-2]
        array = array.reshape((spread, chain // spread) + lead + (chunk, width))
        return jnp.moveaxis(array, 1, -3).reshape((spread,) + lead + (share, width))

    whole = call(
        finish_kernel,
        "finish",
        [vmem] * 2 + [anywhere],
        vmem,
        jax.ShapeDtypeStruct((spread, 2, share, width), low),
    )(by_share(own), by_share(others), other)
    whole = swap(whole, "heads")
    return call(
        lay_kernel,
        "lay",
        [smem] + [vmem] * (2 + planes),
        (anywhere,) * 3,
        (jax.ShapeDtypeStruct((share, spread * width), low),) * 3,
        [pltpu.SemaphoreType.DMA((3 * spread,))],
    )(position, whole, other, *pieces)


def solution(mesh):
    in_specs = (
        P("chain", "heads"),
        P("chain", "heads"),
        P("chain", "heads"),
        P("chain", "heads"),
        P(None, "heads", None),
    )
    out_specs = (
        P(("chain", "heads"), None),
        P(("chain", "heads"), None),
        P(("chain", "heads"), None),
    )
    return jax.shard_map(
        on_device, mesh=mesh, in_specs=in_specs, out_specs=out_specs, check_vma=False
    )
```

```python
import functools
import math

import jax
import jax.numpy as jnp
from jax import lax
from jax.experimental import pallas as pl
from jax.experimental.pallas import tpu as pltpu
from jax.sharding import PartitionSpec as P

HEAD_DIM = 128
TOPK = 3
MASKED = -1e30
SCALING = HEAD_DIM ** (-0.5)
EXPONENT = SCALING * math.log2(math.e)
TILE = 256
STATS = 8
SUBLANES = 8
EARLY = 7
MIB = 1 << 20


def head_columns(head, offset=0):
    start = head * HEAD_DIM + offset
    if isinstance(head, int):
        return pl.ds(start, HEAD_DIM)
    return pl.ds(pl.multiple_of(start, HEAD_DIM), HEAD_DIM)


def dot(left, right, left_dim, right_dim):
    return lax.dot_general(
        left, right, (((left_dim,), (right_dim,)), ((), ())), preferred_element_type=jnp.float32
    )


def stack_kernel(key_ref, value_ref, out_ref, held_ref, in_sem, out_sem):
    pieces = in_sem.shape[1]
    length = key_ref.shape[0] // pieces
    arrive, leave = [], []
    for index, part in enumerate((key_ref, value_ref)):
        for piece in range(pieces):
            span = pl.ds(piece * length, length)
            held = held_ref.at[index, span]
            arrive.append(pltpu.make_async_copy(part.at[span], held, in_sem.at[index, piece]))
            leave.append(
                pltpu.make_async_copy(held, out_ref.at[span, index], out_sem.at[index, piece])
            )
    for copy in arrive:
        copy.start()
    for first, second in zip(arrive, leave):
        first.wait()
        second.start()
    for copy in leave:
        copy.wait()


def pick_kernel(selection_ref, held_ref, out_ref, filled_ref, sem):
    blocks, _, _, width = held_ref.shape
    heads = width // HEAD_DIM
    copies = []
    for block in range(blocks):
        filled_ref[block, :, 0] = held_ref[max(block - 1, 0)]
        for head in range(heads):
            columns = head_columns(head)
            for slot in range(1, TOPK):
                source = selection_ref[(block * heads + head) * TOPK + slot]
                filled_ref[block, :, slot, :, columns] = held_ref[source, :, :, columns]
        copies.append(
            pltpu.make_async_copy(filled_ref.at[block], out_ref.at[block], sem.at[block])
        )
        copies[-1].start()
    for copy in copies:
        copy.wait()


def reduce_kernel(after, selection_ref, terms_ref, *refs):
    out_ref, total_refs = refs[after], refs[after + 1 :]
    blocks, _, _, width = out_ref.shape
    heads = width // HEAD_DIM
    for head, total_ref in enumerate(total_refs):
        total_ref[: blocks - 1] = terms_ref[1:, head, :, 0].astype(jnp.float32)
        total_ref[blocks - 1] = jnp.zeros_like(total_ref[blocks - 1])
    for block in range(blocks):
        for slot in range(1, TOPK):
            for head, total_ref in enumerate(total_refs):
                target = selection_ref[(block * heads + head) * TOPK + slot]
                total_ref[target] += terms_ref[block, head, :, slot].astype(jnp.float32)
    for head, total_ref in enumerate(total_refs):
        out_ref[:, :, :, head_columns(head)] = total_ref[...].astype(out_ref.dtype)


def fold(array):
    return jnp.sum(array.reshape(-1, SUBLANES, array.shape[1]), axis=0)


def causal(scores, first):
    key_at = lax.broadcasted_iota(jnp.int32, scores.shape, 0)
    query_at = lax.broadcasted_iota(jnp.int32, scores.shape, 1) + first
    return jnp.where(key_at <= query_at, scores, MASKED)


def own_forward_kernel(
    selection_ref,
    query_ref,
    key_ref,
    value_ref,
    grad_ref,
    listed_ref,
    stats_ref,
    held_ref,
    sem,
):
    heads, _, rows = stats_ref.shape
    copies = [
        pltpu.make_async_copy(source, held_ref.at[index], sem.at[index])
        for index, source in enumerate((query_ref, grad_ref, key_ref, value_ref))
    ]
    for copy in copies:
        copy.start()

    def hand_on(index, carry):
        listed_ref[index] = selection_ref[index]
        return carry

    lax.fori_loop(0, selection_ref.shape[0], hand_on, 0)
    for copy in copies:
        copy.wait()

    def one_head(head, carry):
        columns = head_columns(head)
        key, value = held_ref[2, :, columns], held_ref[3, :, columns]
        for first in range(0, rows, TILE):
            tile = pl.ds(first, TILE)
            scores = causal(dot(key, held_ref[0, tile, columns], 1, 1), first)
            top = jnp.max(scores, axis=0, keepdims=True)
            raised = jnp.exp2((scores - top) * EXPONENT)
            product = raised * dot(value, held_ref[1, tile, columns], 1, 1)
            stats_ref[head, 0:1, tile] = top
            stats_ref[head, 1:2, tile] = jnp.sum(raised, axis=0, keepdims=True)
            stats_ref[head, 2:3, tile] = jnp.sum(product, axis=0, keepdims=True)
        return carry

    lax.fori_loop(0, heads, one_head, 0)


def far_kernel(
    selection_ref,
    position_ref,
    query_ref,
    grad_ref,
    listed_ref,
    own_stats_ref,
    terms_ref,
    part_ref,
    stats_ref,
    *scratch,
):
    heads, _, rows = own_stats_ref.shape
    chunks, _, _, chunk, _ = listed_ref.shape
    block = position_ref[0]
    def listed(which, head):
        return listed_ref[:, which, :, :, head_columns(head)].reshape(TOPK * rows, HEAD_DIM)

    def softmax(head):
        score_ref, grad_prob_ref, prob_ref, grad_score_ref = scratch[4 * head : 4 * head + 4]
        live = [
            selection_ref[(block * heads + head) * TOPK + slot] < block for slot in range(TOPK)
        ]
        shape = (chunks, TOPK, chunk, TILE)
        for first in range(0, rows, TILE):
            tile = pl.ds(first, TILE)
            scores = dot(listed(0, head), query_ref[tile, head_columns(head)], 1, 1)
            score_ref[:, :, :, tile] = scores.reshape(shape)
            grad_probs = dot(listed(1, head), grad_ref[tile, head_columns(head)], 1, 1)
            grad_prob_ref[:, :, :, tile] = grad_probs.reshape(shape)
            top = jnp.full((1, TILE), MASKED, jnp.float32)
            for slot in range(TOPK):
                highest = jnp.max(
                    score_ref[:, slot, :, tile].reshape(rows, TILE), axis=0, keepdims=True
                )
                top = jnp.maximum(top, jnp.where(live[slot], highest, MASKED))
            total = jnp.zeros((SUBLANES, TILE), jnp.float32)
            product = jnp.zeros_like(total)
            for slot in range(TOPK):
                shift = jnp.where(live[slot], top, -MASKED)
                for part in range(chunks):
                    raised = jnp.exp2((score_ref[part, slot, :, tile] - shift) * EXPONENT)
                    score_ref[part, slot, :, tile] = raised
                    total += fold(raised)
                    product += fold(raised * grad_prob_ref[part, slot, :, tile])
            total = jnp.sum(total, axis=0, keepdims=True)
            product = jnp.sum(product, axis=0, keepdims=True)
            own_top = own_stats_ref[head, 0:1, tile]
            highest = jnp.maximum(own_top, top)
            own_factor = jnp.exp2((own_top - highest) * EXPONENT)
            factor = jnp.exp2((top - highest) * EXPONENT)
            inverse = 1.0 / (own_factor * own_stats_ref[head, 1:2, tile] + factor * total)
            own_weight, weight = own_factor * inverse, factor * inverse
            delta = own_weight * own_stats_ref[head, 2:3, tile] + weight * product
            stats_ref[head, 0:1, tile] = own_weight
            stats_ref[head, 1:2, tile] = delta
            for slot in range(TOPK):
                for part in range(chunks):
                    probability = score_ref[part, slot, :, tile] * weight
                    prob_ref[part, slot, :, tile] = probability.astype(jnp.bfloat16)
                    grad_score_ref[part, slot, :, tile] = (
                        probability * (grad_prob_ref[part, slot, :, tile] - delta)
                    ).astype(jnp.bfloat16)

    def gradients(head):
        _, _, prob_ref, grad_score_ref = scratch[4 * head : 4 * head + 4]
        columns = head_columns(head)
        query, grad = query_ref[:, columns], grad_ref[:, columns]
        shape = (chunks, TOPK, chunk, HEAD_DIM)
        prob = prob_ref[...].reshape(TOPK * rows, rows)
        grad_scores = grad_score_ref[...].reshape(TOPK * rows, rows)
        grad_key = dot(grad_scores, query, 1, 0) * SCALING
        terms_ref[:, head, 0] = grad_key.astype(jnp.bfloat16).reshape(shape)
        grad_value = dot(prob, grad, 1, 0)
        terms_ref[:, head, 1] = grad_value.astype(jnp.bfloat16).reshape(shape)
        part_ref[head] = dot(listed(0, head).T, grad_scores, 1, 0).astype(jnp.bfloat16)

    for head in range(heads):
        softmax(head)
        gradients(head)


def own_backward_kernel(
    place_ref,
    query_ref,
    key_ref,
    value_ref,
    grad_ref,
    part_ref,
    own_stats_ref,
    stats_ref,
    own_ref,
    *refs,
):
    piece_refs, grad_query_ref = refs[:-1], refs[-1]
    heads, _, rows = stats_ref.shape
    chunks, _, chunk, _ = own_ref.shape

    def one_head(head, carry):
        columns = head_columns(head)
        query, key = query_ref[:, columns], key_ref[:, columns]
        value, grad = value_ref[:, columns], grad_ref[:, columns]
        scores = causal(dot(key, query, 1, 1), 0)
        raised = jnp.exp2((scores - own_stats_ref[head, 0:1, :]) * EXPONENT)
        probability = raised * stats_ref[head, 0:1, :]
        grad_probs = dot(value, grad, 1, 1)
        grad_scores = (probability * (grad_probs - stats_ref[head, 1:2, :])).astype(jnp.bfloat16)
        grad_query = dot(key.T, grad_scores, 1, 0) + part_ref[head].astype(jnp.float32)
        grad_query = grad_query * SCALING
        grad_query_ref[:, columns] = grad_query.T.astype(jnp.bfloat16)
        results = (
            dot(grad_scores, query, 1, 0) * SCALING,
            dot(probability.astype(jnp.bfloat16), grad, 1, 0),
        )
        for index, result in enumerate(results):
            own_ref[:, index, :, columns] = result.astype(jnp.bfloat16).reshape(
                chunks, chunk, HEAD_DIM
            )
        return carry

    lax.fori_loop(0, heads, one_head, 0)
    planes = len(piece_refs)
    plane = place_ref[1]
    length = rows // planes
    for step, piece_ref in enumerate(piece_refs):
        first = pl.multiple_of(((plane + step) % planes) * length, length)
        piece_ref[...] = grad_query_ref[pl.ds(first, length), :]


def join_kernel(place_ref, *refs):
    piece_refs, out_ref = refs[:-1], refs[-1]
    share = out_ref.shape[1]
    first = pl.multiple_of((1 - place_ref[2]) * share, share)
    for step, piece_ref in enumerate(piece_refs):
        out_ref[step] = piece_ref[pl.ds(first, share), :]


def finish_kernel(own_ref, others_ref, after_ref, out_ref):
    out_ref[...] = (
        others_ref[...].astype(jnp.float32) + own_ref[...].astype(jnp.float32)
    ).astype(jnp.bfloat16)


def lay_kernel(place_ref, parts_ref, other_ref, *refs):
    piece_refs, (query_ref, key_ref, value_ref, sem) = refs[:-4], refs[-4:]
    senders, _, share, width = parts_ref.shape
    planes = len(piece_refs)
    cores = senders // planes
    plane, core = place_ref[1], place_ref[2]
    copies = []

    def put(source, out, sender):
        first = sender * width
        if not isinstance(sender, int):
            first = pl.multiple_of(first, width)
        target = out.at[:, pl.ds(first, width)]
        copies.append(pltpu.make_async_copy(source, target, sem.at[len(copies)]))
        copies[-1].start()

    for step, piece_ref in enumerate(piece_refs):
        origin = (plane - step + planes) % planes
        rows = pl.ds(pl.multiple_of(core * share, share), share)
        put(piece_ref.at[rows], query_ref, origin * cores + core)
        if cores > 1:
            put(other_ref.at[step], query_ref, origin * cores + 1 - core)
    for sender in range(senders):
        put(parts_ref.at[sender, 0], key_ref, sender)
        put(parts_ref.at[sender, 1], value_ref, sender)
    for copy in copies:
        copy.wait()


def on_device(query_input, key_input, value_input, grad_output, selection):
    rows, width = query_input.shape
    heads = width // HEAD_DIM
    chain, spread = lax.axis_size("chain"), lax.axis_size("heads")
    chunk = rows // chain
    share = rows // spread
    listed = selection.reshape(-1)
    cores = 2 if spread % 2 == 0 else 1
    planes = spread // cores
    at = lax.axis_index("heads")
    position = jnp.stack([lax.axis_index("chain"), at // cores, at % cores]).astype(jnp.int32)
    smem = pl.BlockSpec(memory_space=pltpu.SMEM)
    vmem = pl.BlockSpec(memory_space=pltpu.VMEM)
    anywhere = pl.BlockSpec(memory_space=pl.ANY)
    low, full = jnp.bfloat16, jnp.float32

    def swap(array, axis):
        return lax.all_to_all(array, axis, split_axis=0, concat_axis=0, tiled=True)

    def call(kernel, name, in_specs, out_specs, out_shape, scratch=(), limit=4, slots=0):
        flops = 2 * heads * slots * rows * rows * HEAD_DIM
        return pl.pallas_call(
            kernel,
            out_shape=out_shape,
            in_specs=in_specs,
            out_specs=out_specs,
            scratch_shapes=list(scratch),
            cost_estimate=pl.CostEstimate(
                flops=flops, bytes_accessed=4 * MIB, transcendentals=heads * rows * rows
            ),
            compiler_params=pltpu.CompilerParams(vmem_limit_bytes=limit * MIB),
            name=name,
        )

    pair = call(
        stack_kernel,
        "stack",
        [anywhere] * 2,
        anywhere,
        jax.ShapeDtypeStruct((chain, 2, chunk, width), low),
        [
            pltpu.VMEM((2, chain, chunk, width), low),
            pltpu.SemaphoreType.DMA((2, 2)),
            pltpu.SemaphoreType.DMA((2, 2)),
        ],
        limit=59,
    )(key_input.reshape(chain, chunk, width), value_input.reshape(chain, chunk, width))
    held = swap(pair, "chain")
    listed, own_stats = call(
        own_forward_kernel,
        "own_forward",
        [smem] + [anywhere] * 4,
        (smem, vmem),
        (
            jax.ShapeDtypeStruct(listed.shape, jnp.int32),
            jax.ShapeDtypeStruct((heads, STATS, rows), full),
        ),
        [pltpu.VMEM((4, rows, width), low), pltpu.SemaphoreType.DMA((4,))],
        limit=16,
        slots=2,
    )(listed, query_input, key_input, value_input, grad_output)
    picked = call(
        pick_kernel,
        "pick",
        [smem, vmem],
        anywhere,
        jax.ShapeDtypeStruct((chain, 2, TOPK, chunk, width), low),
        [
            pltpu.VMEM((chain, 2, TOPK, chunk, width), low),
            pltpu.SemaphoreType.DMA((chain,)),
        ],
    )(listed, held)
    slots = swap(picked, "chain")
    terms, part, stats = call(
        far_kernel,
        "far",
        [smem, smem] + [vmem] * 4,
        (vmem, vmem, vmem),
        (
            jax.ShapeDtypeStruct((chain, heads, 2, TOPK, chunk, HEAD_DIM), low),
            jax.ShapeDtypeStruct((heads, HEAD_DIM, rows), low),
            jax.ShapeDtypeStruct((heads, STATS, rows), full),
        ),
        [
            pltpu.VMEM((chain, TOPK, chunk, rows), full),
            pltpu.VMEM((chain, TOPK, chunk, rows), full),
            pltpu.VMEM((chain, TOPK, chunk, rows), low),
            pltpu.VMEM((chain, TOPK, chunk, rows), low),
        ]
        * heads,
        limit=32,
        slots=5 * TOPK,
    )(listed, position, query_input, grad_output, slots, own_stats)
    returned = swap(terms, "chain")
    own, *pieces = call(
        own_backward_kernel,
        "own_backward",
        [smem] + [vmem] * 7,
        (vmem,) * (1 + planes),
        (jax.ShapeDtypeStruct((chain, 2, chunk, width), low),)
        + (jax.ShapeDtypeStruct((rows // planes, width), low),) * planes,
        [pltpu.VMEM((rows, width), low)],
        limit=12,
        slots=5,
    )(position, query_input, key_input, value_input, grad_output, part, own_stats, stats)

    def to_plane(piece, step):
        if step == 0:
            return piece
        pairs = [(one, (one + step * cores) % spread) for one in range(spread)]
        return lax.ppermute(piece, "heads", pairs)

    order = sorted(range(planes), key=lambda step: -min(step, planes - step))
    for step in order:
        pieces[step] = to_plane(pieces[step], step)
    early = [pieces[step] for step in order[:EARLY]]
    summed = call(
        functools.partial(reduce_kernel, len(early)),
        "reduce",
        [smem, vmem] + [anywhere] * len(early),
        vmem,
        jax.ShapeDtypeStruct((chain, 2, chunk, width), low),
        [pltpu.VMEM((chain, 2, chunk, HEAD_DIM), full)] * heads,
    )(listed, returned, *early)
    joined = other = pieces[0]
    if cores > 1:
        joined = call(
            join_kernel,
            "join",
            [smem] + [vmem] * planes,
            vmem,
            jax.ShapeDtypeStruct((planes, share, width), low),
        )(position, *pieces)
        other = lax.ppermute(joined, "heads", [(one, one ^ 1) for one in range(spread)])
    others = swap(summed, "chain")

    def by_share(array):
        lead = array.shape[1:-2]
        array = array.reshape((spread, chain // spread) + lead + (chunk, width))
        return jnp.moveaxis(array, 1, -3).reshape((spread,) + lead + (share, width))

    whole = call(
        finish_kernel,
        "finish",
        [vmem] * 2 + [anywhere],
        vmem,
        jax.ShapeDtypeStruct((spread, 2, share, width), low),
    )(by_share(own), by_share(others), other)
    whole = swap(whole, "heads")
    return call(
        lay_kernel,
        "lay",
        [smem] + [vmem] * (2 + planes),
        (anywhere,) * 3,
        (jax.ShapeDtypeStruct((share, spread * width), low),) * 3,
        [pltpu.SemaphoreType.DMA((3 * spread,))],
    )(position, whole, other, *pieces)


def solution(mesh):
    in_specs = (
        P("chain", "heads"),
        P("chain", "heads"),
        P("chain", "heads"),
        P("chain", "heads"),
        P(None, "heads", None),
    )
    out_specs = (
        P(("chain", "heads"), None),
        P(("chain", "heads"), None),
        P(("chain", "heads"), None),
    )
    return jax.shard_map(
        on_device, mesh=mesh, in_specs=in_specs, out_specs=out_specs, check_vma=False
    )
```
